32 devices in a mesh: batch: 8 (over z, x), ch: 4 (over y, core).
Axes of the slice: x: 2, y: 2, z: 4, core: 2. Of those that a mesh axis runs over, the one named last changes fastest.
Arguments:
- clip_features: bfloat16 [528, 36864], P('ch', 'batch'), may hold values from -6 to 6
- visible: int32 [64, 4, 12, 12], P('batch'), may hold values from 0 to 1, as said below
- direct_early: bfloat16 [528, 256], P(None, 'ch'), may hold values from -0.25 to 0.25
- narrow_early: bfloat16 [528, 160], P(None, 'ch'), may hold values from -0.25 to 0.25
- squeeze_early: bfloat16 [528, 32], P(None, 'ch'), may hold values from -0.25 to 0.25
- project_early: bfloat16 [528, 128], P(None, 'ch'), may hold values from -0.25 to 0.25
- direct_late: bfloat16 [832, 256], P(None, 'ch'), may hold values from -0.21875 to 0.21875
- narrow_late: bfloat16 [832, 160], P(None, 'ch'), may hold values from -0.21875 to 0.21875
- squeeze_late: bfloat16 [832, 32], P(None, 'ch'), may hold values from -0.21875 to 0.21875
- project_late: bfloat16 [832, 128], P(None, 'ch'), may hold values from -0.21875 to 0.21875
- wide_kernels: bfloat16 [2, 1382400], P(None, 'ch'), may hold values from -0.09375 to 0.09375
- spread_kernels: bfloat16 [2, 27, 32, 128], P(None, None, None, 'ch'), may hold values from -0.21875 to 0.21875
- direct_norm: bfloat16 [2, 2, 256], P(None, None, 'ch'), may hold values from -1 to 2, as said below
- narrow_norm: bfloat16 [2, 2, 160], P(None, None, 'ch'), may hold values from -1 to 2, as said below
- wide_norm: bfloat16 [2, 2, 320], P(None, None, 'ch'), may hold values from -1 to 2, as said below
- squeeze_norm: bfloat16 [2, 2, 32], P(None, None, 'ch'), may hold values from -1 to 2, as said below
- spread_norm: bfloat16 [2, 2, 128], P(None, None, 'ch'), may hold values from -1 to 2, as said below
- project_norm: bfloat16 [2, 2, 128], P(None, None, 'ch'), may hold values from -1 to 2, as said below
- upstream_direct: bfloat16 [64, 2, 6, 6, 256], P('batch', None, None, None, 'ch'), may hold values from -6 to 6
- upstream_wide: bfloat16 [64, 2, 6, 6, 320], P('batch', None, None, None, 'ch'), may hold values from -6 to 6
- upstream_spread: bfloat16 [64, 2, 6, 6, 128], P('batch', None, None, None, 'ch'), may hold values from -6 to 6
- upstream_project: bfloat16 [64, 2, 6, 6, 128], P('batch', None, None, None, 'ch'), may hold values from -6 to 6
Outputs:
- output_direct: bfloat16 [64, 2, 6, 6, 256], P('batch', None, None, None, 'ch')
- output_wide: bfloat16 [64, 2, 6, 6, 320], P('batch', None, None, None, 'ch')
- output_spread: bfloat16 [64, 2, 6, 6, 128], P('batch', None, None, None, 'ch')
- output_project: bfloat16 [64, 2, 6, 6, 128], P('batch', None, None, None, 'ch')
- feature_grad: float32 [528, 36864], P('ch', 'batch')
- direct_early_grad: float32 [528, 256], P(None, 'ch')
- narrow_early_grad: float32 [528, 160], P(None, 'ch')
- squeeze_early_grad: float32 [528, 32], P(None, 'ch')
- project_early_grad: float32 [528, 128], P(None, 'ch')
- direct_late_grad: float32 [832, 256], P(None, 'ch')
- narrow_late_grad: float32 [832, 160], P(None, 'ch')
- squeeze_late_grad: float32 [832, 32], P(None, 'ch')
- project_late_grad: float32 [832, 128], P(None, 'ch')
- wide_kernels_grad: float32 [2, 1382400], P(None, 'ch')
- spread_kernels_grad: float32 [2, 27, 32, 128], P(None, None, None, 'ch')
- direct_norm_grad: float32 [2, 2, 256], P(None, None, 'ch')
- narrow_norm_grad: float32 [2, 2, 160], P(None, None, 'ch')
- wide_norm_grad: float32 [2, 2, 320], P(None, None, 'ch')
- squeeze_norm_grad: float32 [2, 2, 32], P(None, None, 'ch')
- spread_norm_grad: float32 [2, 2, 128], P(None, None, 'ch')
- project_norm_grad: float32 [2, 2, 128], P(None, None, 'ch')
The draws below stay inside these ranges and needn't reach their ends.
Inputs may be any that keep to these rules, and one draw needn't show every extreme that they name: `visible`: each clip has one or two occluded tubes, boxes in frames, rows and columns with each side at most half of the clip's; every clip keeps at least three quarters of its voxels. `direct_norm`: row 0 of each block holds positive scales, row 1 shifts. `narrow_norm`: row 0 of each block holds positive scales, row 1 shifts. `wide_norm`: row 0 of each block holds positive scales, row 1 shifts. `squeeze_norm`: row 0 of each block holds positive scales, row 1 shifts. `spread_norm`: row 0 of each block holds positive scales, row 1 shifts. `project_norm`: row 0 of each block holds positive scales, row 1 shifts.
All inputs are finite; a program needn't handle non-finite values.
Results may differ from the reference program's by a relative error of at most 0.025.
Values may be sent and summed in bfloat16 or wider, within the bound.
No kernel may reach another device: no remote copies, remote signals or barrier semaphores. Data moves between devices by JAX's collectives and lax.ppermute only.
A program may use at most 640 MiB of HBM per device.

```python
import jax
import jax.numpy as jnp
from jax import lax

FRAMES = 4
HEIGHT = 12
WIDTH = 12
FEATURES = 528
DIRECT = 256
NARROW = 160
WIDE = 320
SQUEEZE = 32
SPREAD = 128
PROJECT = 128
CONCAT = 832
CLIPS = 64
HALF_FRAMES = 2
HALF_HEIGHT = 6
HALF_WIDTH = 6
VOXELS = 576


def tube_span(size_key, start_key, extent):
    span_size = jax.random.randint(size_key, (CLIPS, 2), 1, extent // 2 + 1)
    span_start = jax.random.randint(start_key, (CLIPS, 2), 0, extent - span_size + 1)
    position = jnp.arange(extent)[None, None, :]
    return (position >= span_start[:, :, None]) & (position < (span_start + span_size)[:, :, None])


def draw_visible(key, part):
    key = jax.random.fold_in(key, 7)
    subkeys = jax.random.split(key, 6)
    in_frames = tube_span(subkeys[0], subkeys[1], FRAMES)
    in_rows = tube_span(subkeys[2], subkeys[3], HEIGHT)
    in_columns = tube_span(subkeys[4], subkeys[5], WIDTH)
    covered = in_frames[:, :, :, None, None] & in_rows[:, :, None, :, None] & in_columns[:, :, None, None, :]
    return 1 - jnp.any(covered, axis=1).astype(jnp.int32)


def affine_draw(key, channel_count):
    scale_key, shift_key = jax.random.split(key)
    scales = jnp.exp(jax.random.uniform(scale_key, (2, 1, channel_count), jnp.float32, -0.69, 0.69))
    shifts = jax.random.uniform(shift_key, (2, 1, channel_count), jnp.float32, -1.0, 1.0)
    return jnp.concatenate([scales, shifts], axis=1).astype(jnp.bfloat16)


def draw_direct_norm(key, part):
    key = jax.random.fold_in(key, 21)
    return affine_draw(key, DIRECT)


def draw_narrow_norm(key, part):
    key = jax.random.fold_in(key, 22)
    return affine_draw(key, NARROW)


def draw_wide_norm(key, part):
    key = jax.random.fold_in(key, 23)
    return affine_draw(key, WIDE)


def draw_squeeze_norm(key, part):
    key = jax.random.fold_in(key, 24)
    return affine_draw(key, SQUEEZE)


def draw_spread_norm(key, part):
    key = jax.random.fold_in(key, 25)
    return affine_draw(key, SPREAD)


def draw_project_norm(key, part):
    key = jax.random.fold_in(key, 26)
    return affine_draw(key, PROJECT)


def steps_of(stream_key, shape, cuts, least, high):
    level, own = 1.0, jax.random.fold_in(stream_key, 6)
    for axis_at, blocks in cuts:
        draws = jnp.exp(jax.random.uniform(jax.random.fold_in(own, axis_at), (blocks,), jnp.float32, least / len(cuts), high / len(cuts)))
        level = level * jnp.repeat(draws, shape[axis_at] // blocks).reshape([-1 if axis == axis_at else 1 for axis in range(len(shape))])
    return level


def normal_values(own_key, shape, spread, bound, cuts=(), held_as=jnp.bfloat16):
    loudness = steps_of(own_key, shape, cuts, -0.22, 0.18) if cuts else 1.0
    values = jax.random.normal(own_key, shape, jnp.float32) * spread * loudness
    return jnp.minimum(jnp.maximum(values, -bound), bound).astype(held_as)


def setup_inputs(seed: int = 0) -> dict:
    splits = jax.random.split(jax.random.key(seed), 23)
    clip_features = normal_values(splits[0], (FEATURES, CLIPS * VOXELS), 1.0, 6.0, ((0, 4), (1, 8)))
    visible = draw_visible(jax.random.fold_in(splits[22], 71), 0)
    direct_early = normal_values(splits[2], (FEATURES, DIRECT), FEATURES ** -0.5, 0.25, ((1, 4),))
    narrow_early = normal_values(splits[3], (FEATURES, NARROW), FEATURES ** -0.5, 0.25, ((1, 4),))
    squeeze_early = normal_values(splits[4], (FEATURES, SQUEEZE), FEATURES ** -0.5, 0.25, ((1, 4),))
    project_early = normal_values(splits[5], (FEATURES, PROJECT), FEATURES ** -0.5, 0.25, ((1, 4),))
    direct_late = normal_values(splits[6], (CONCAT, DIRECT), CONCAT ** -0.5, 0.21875, ((1, 4),))
    narrow_late = normal_values(splits[7], (CONCAT, NARROW), CONCAT ** -0.5, 0.21875, ((1, 4),))
    squeeze_late = normal_values(splits[8], (CONCAT, SQUEEZE), CONCAT ** -0.5, 0.21875, ((1, 4),))
    project_late = normal_values(splits[9], (CONCAT, PROJECT), CONCAT ** -0.5, 0.21875, ((1, 4),))
    wide_kernels = normal_values(splits[10], (2, WIDE * 27 * NARROW), (27 * NARROW) ** -0.5, 0.09375, ((1, 4),))
    spread_kernels = normal_values(splits[11], (2, 27, SQUEEZE, SPREAD), (27 * SQUEEZE) ** -0.5, 0.21875, ((3, 4),))
    direct_norm = draw_direct_norm(jax.random.fold_in(splits[22], 71), 0)
    narrow_norm = draw_narrow_norm(jax.random.fold_in(splits[22], 71), 0)
    wide_norm = draw_wide_norm(jax.random.fold_in(splits[22], 71), 0)
    squeeze_norm = draw_squeeze_norm(jax.random.fold_in(splits[22], 71), 0)
    spread_norm = draw_spread_norm(jax.random.fold_in(splits[22], 71), 0)
    project_norm = draw_project_norm(jax.random.fold_in(splits[22], 71), 0)
    upstream_direct = normal_values(splits[18], (CLIPS, HALF_FRAMES, HALF_HEIGHT, HALF_WIDTH, DIRECT), 1.0, 6.0, ((0, 8), (4, 4)))
    upstream_wide = normal_values(splits[19], (CLIPS, HALF_FRAMES, HALF_HEIGHT, HALF_WIDTH, WIDE), 1.0, 6.0, ((0, 8), (4, 4)))
    upstream_spread = normal_values(splits[20], (CLIPS, HALF_FRAMES, HALF_HEIGHT, HALF_WIDTH, SPREAD), 1.0, 6.0, ((0, 8), (4, 4)))
    upstream_project = normal_values(splits[21], (CLIPS, HALF_FRAMES, HALF_HEIGHT, HALF_WIDTH, PROJECT), 1.0, 6.0, ((0, 8), (4, 4)))
    return dict(clip_features=clip_features, visible=visible, direct_early=direct_early, narrow_early=narrow_early, squeeze_early=squeeze_early, project_early=project_early, direct_late=direct_late, narrow_late=narrow_late, squeeze_late=squeeze_late, project_late=project_late, wide_kernels=wide_kernels, spread_kernels=spread_kernels, direct_norm=direct_norm, narrow_norm=narrow_norm, wide_norm=wide_norm, squeeze_norm=squeeze_norm, spread_norm=spread_norm, project_norm=project_norm, upstream_direct=upstream_direct, upstream_wide=upstream_wide, upstream_spread=upstream_spread, upstream_project=upstream_project)


@jax.custom_vjp
def low(v):
    return lax.optimization_barrier(v.astype(jnp.bfloat16)).astype(jnp.float32)

@jax.custom_vjp
def low_back(v):
    return v

def low_keep(v):
    return (low(v), None)

def low_pass(kept, grad):
    return (grad,)

def back_keep(v):
    return (v, None)

def back_low(kept, grad):
    return (low(grad),)
low.defvjp(low_keep, low_pass)
low_back.defvjp(back_keep, back_low)
EPSILON = 0.001
HIGHEST = lax.Precision.HIGHEST
CUBE_OFFSETS = [(a, b, c) for a in range(3) for b in range(3) for c in range(3)]

def pad_cells(field):
    return jnp.pad(field, ((0, 0), (1, 1), (1, 1), (1, 1), (0, 0)))

def mean_cube(field):
    padded = pad_cells(field)
    frame_count, row_count, column_count = (field.shape[1], field.shape[2], field.shape[3])
    running = jnp.zeros_like(field)
    for a, b, c in CUBE_OFFSETS:
        running = running + padded[:, a:a + frame_count, b:b + row_count, c:c + column_count]
    return running / 27.0

def mean_pairs(field):
    clip_count, frame_count, row_count, column_count, channels = field.shape
    grouped = field.reshape(clip_count, frame_count // 2, 2, row_count // 2, 2, column_count // 2, 2, channels)
    return lax.optimization_barrier(jnp.mean(grouped, axis=(2, 4, 6)))

def pair_mask(visible):
    clip_count, frame_count, row_count, column_count = visible.shape
    grouped = visible.reshape(clip_count, frame_count // 2, 2, row_count // 2, 2, column_count // 2, 2)
    return lax.optimization_barrier(jnp.max(grouped, axis=(2, 4, 6)))

def point_conv(activation, weight):
    return jnp.einsum('cfhwi,io->cfhwo', activation, weight, precision=HIGHEST)

def cube_conv(activation, kernel):
    shaped = kernel.reshape(3, 3, 3, kernel.shape[1], kernel.shape[2])
    return lax.conv_general_dilated(activation, shaped, (1, 1, 1), 'SAME', dimension_numbers=('NDHWC', 'DHWIO', 'NDHWC'), precision=HIGHEST)

def unit_norm(output, affine, masking, voxel_count):
    average = lax.optimization_barrier(jnp.sum(output * masking, axis=(0, 1, 2, 3))) / voxel_count
    centred = output - average
    variance = lax.optimization_barrier(jnp.sum(masking * centred * centred, axis=(0, 1, 2, 3))) / voxel_count
    shifted = affine[0] * centred * lax.rsqrt(variance + EPSILON) + affine[1]
    return jax.nn.silu(shifted) * masking

def inception(activation, masking, voxel_count, weights, affines):
    direct, narrow, squeeze, project, wide_kernel, spread_kernel = weights
    out_direct = unit_norm(low_back(point_conv(activation, direct)), affines[0], masking, voxel_count)
    narrow_low = low(unit_norm(low_back(point_conv(activation, narrow)), affines[1], masking, voxel_count))
    out_wide = unit_norm(low_back(cube_conv(narrow_low, wide_kernel)), affines[2], masking, voxel_count)
    squeeze_low = low(unit_norm(low_back(point_conv(activation, squeeze)), affines[3], masking, voxel_count))
    out_spread = unit_norm(low_back(cube_conv(squeeze_low, spread_kernel)), affines[4], masking, voxel_count)
    out_project = unit_norm(mean_cube(low_back(point_conv(activation, project))), affines[5], masking, voxel_count)
    return (out_direct, out_wide, out_spread, out_project)

def forward_pass(visible, features_flat, direct_early, narrow_early, squeeze_early, project_early, direct_late, narrow_late, squeeze_late, project_late, wide_flat, spread_kernels, direct_norm, narrow_norm, wide_norm, squeeze_norm, spread_norm, project_norm):
    features = jnp.transpose(features_flat.reshape(FEATURES, CLIPS, FRAMES, HEIGHT, WIDTH), (1, 2, 3, 4, 0))
    wide_kernels = jnp.transpose(wide_flat.reshape(2, WIDE, 27, NARROW), (0, 2, 3, 1))
    mask_fine = visible.astype(jnp.float32)[..., None]
    mask_coarse = pair_mask(visible).astype(jnp.float32)[..., None]
    count_fine = jnp.sum(mask_fine)
    count_coarse = jnp.sum(mask_coarse)
    affines = (direct_norm, narrow_norm, wide_norm, squeeze_norm, spread_norm, project_norm)
    early = jax.checkpoint(inception)(features * mask_fine, mask_fine, count_fine, (direct_early, narrow_early, squeeze_early, project_early, wide_kernels[0], spread_kernels[0]), tuple((affine[0] for affine in affines)))
    late_input = jnp.concatenate([low(mean_pairs(field)) for field in early], axis=4)
    late = jax.checkpoint(inception)(late_input, mask_coarse, count_coarse, (direct_late, narrow_late, squeeze_late, project_late, wide_kernels[1], spread_kernels[1]), tuple((affine[1] for affine in affines)))
    return late

def reference(clip_features, visible, direct_early, narrow_early, squeeze_early, project_early, direct_late, narrow_late, squeeze_late, project_late, wide_kernels, spread_kernels, direct_norm, narrow_norm, wide_norm, squeeze_norm, spread_norm, project_norm, upstream_direct, upstream_wide, upstream_spread, upstream_project):
    primals = (clip_features, direct_early, narrow_early, squeeze_early, project_early, direct_late, narrow_late, squeeze_late, project_late, wide_kernels, spread_kernels, direct_norm, narrow_norm, wide_norm, squeeze_norm, spread_norm, project_norm)
    primals = tuple((field.astype(jnp.float32) for field in primals))

    def wrapped(*inputs):
        return forward_pass(visible, *inputs)
    late, pullback = jax.vjp(wrapped, *primals)
    upstream = (upstream_direct.astype(jnp.float32), upstream_wide.astype(jnp.float32), upstream_spread.astype(jnp.float32), upstream_project.astype(jnp.float32))
    grads = pullback(upstream)
    return (late[0].astype(jnp.bfloat16), late[1].astype(jnp.bfloat16), late[2].astype(jnp.bfloat16), late[3].astype(jnp.bfloat16), grads[0], grads[1], grads[2], grads[3], grads[4], grads[5], grads[6], grads[7], grads[8], grads[9], grads[10], grads[11], grads[12], grads[13], grads[14], grads[15], grads[16])
```

```python
import jax
import jax.numpy as jnp
import numpy as np
from jax import lax
from jax.experimental import pallas as pl
from jax.experimental.pallas import tpu as pltpu
from jax.sharding import PartitionSpec as P

F32 = jnp.float32
BF16 = jnp.bfloat16
EPSILON = 0.001
BOTH = ("batch", "ch")
DIRECT, NARROW, WIDE, SQUEEZE, SPREAD, PROJECT = 256, 160, 320, 32, 128, 128
REDUCED = NARROW + SQUEEZE
POINT = DIRECT + REDUCED + PROJECT
CONCAT = DIRECT + WIDE + SPREAD + PROJECT
WIDE_COLUMNS = 27 * NARROW
SPREAD_COLUMNS = 27 * SQUEEZE
POINT_WIDTHS = (DIRECT, NARROW, SQUEEZE, PROJECT)
SLOT = {"d": (0, DIRECT), "r": (256, REDUCED), "w": (512, WIDE), "s": (896, SPREAD), "p": (1024, PROJECT)}
SLOTS = 1152
TILE_ROW = {"d": (0, DIRECT), "w": (2, WIDE), "s": (5, SPREAD), "p": (6, PROJECT)}
OUTER = ("d", "w", "s", "p")
CHUNK = 48


class Geometry:
    def __init__(self, frames, height, width, pitch, block):
        self.frames, self.height, self.width, self.pitch = frames, height, width, pitch
        self.block = block
        self.frame_rows = height * pitch
        self.clip_rows = frames * self.frame_rows
        self.padded_rows = (frames + 2) * self.frame_rows
        self.dense = pitch == width


EARLY = Geometry(4, 12, 12, 12, 0)
LATE = Geometry(2, 6, 6, 8, 1)


def nt(a, b):
    return lax.dot_general(a, b, (((1,), (1,)), ((), ())), preferred_element_type=F32)


def nn(a, b):
    return lax.dot_general(a, b, (((1,), (0,)), ((), ())), preferred_element_type=F32)


def tn(a, b):
    return lax.dot_general(a, b, (((0,), (0,)), ((), ())), preferred_element_type=F32)


def call(kernel, outs, ins, scratch=(), flops=0):
    moved = sum(int(np.prod(s)) * jnp.dtype(d).itemsize for s, d in outs)
    moved += sum(int(np.prod(x.shape)) * x.dtype.itemsize for x in ins)
    return pl.pallas_call(
        kernel,
        out_shape=[jax.ShapeDtypeStruct(s, d) for s, d in outs],
        scratch_shapes=[pltpu.VMEM(s, d) for s, d in scratch],
        compiler_params=pltpu.CompilerParams(vmem_limit_bytes=56 * 2**20),
        cost_estimate=pl.CostEstimate(
            flops=int(flops) or 10 * moved, bytes_accessed=moved, transcendentals=0
        ),
    )(*ins)


def each_chunk(rows, body, init=0, chunk=CHUNK):
    return lax.fori_loop(
        0, rows // chunk, lambda i, carry: body(pl.multiple_of(i * chunk, chunk), carry), init
    )


def row(tile, first, width):
    pieces = [
        tile[first + i : first + i + 1, : min(128, width - 128 * i)] for i in range(-(-width // 128))
    ]
    return pieces[0] if len(pieces) == 1 else jnp.concatenate(pieces, axis=1)


def put_row(ref, first, vector):
    width = vector.shape[1]
    for i in range(-(-width // 128)):
        part = vector[:, 128 * i : min(128 * (i + 1), width)]
        ref[first + i : first + i + 1, : part.shape[1]] = part


def affine_of(aff_ref, block, unit):
    start, width = SLOT[unit]
    return (
        aff_ref[2 * block : 2 * block + 1, start : start + width],
        aff_ref[2 * block + 1 : 2 * block + 2, start : start + width],
    )


def fold8(value):
    total = value[0:8]
    for i in range(1, value.shape[0] // 8):
        total = total + value[8 * i : 8 * i + 8]
    return total


def local_moments(y_ref, m_ref, rows, count):
    width = y_ref.shape[1]

    def first(r, acc):
        return acc + fold8(y_ref[pl.ds(r, CHUNK), :] * m_ref[pl.ds(r, CHUNK), 0:1])

    total = each_chunk(rows, first, jnp.zeros((8, width), F32))
    mean = jnp.sum(total, axis=0, keepdims=True) / count

    def second(r, acc):
        centred = (y_ref[pl.ds(r, CHUNK), :] - mean) * m_ref[pl.ds(r, CHUNK), 0:1]
        return acc + fold8(centred * centred)

    spread = each_chunk(rows, second, jnp.zeros((8, width), F32))
    return mean, jnp.sum(spread, axis=0, keepdims=True)


def combine_moments(payload, counts, first, second, size):
    means = payload[:, first : first + size, :]
    total = jnp.sum(counts, axis=0)
    mean = jnp.sum(means * counts, axis=0) / total
    offset = means - mean[None]
    spread = jnp.sum(payload[:, second : second + size, :] + counts * offset * offset, axis=0)
    return mean, lax.rsqrt(spread / total + EPSILON)


def send_tile(pay_ref, tile_ref):
    pay_ref[...] = jnp.broadcast_to(tile_ref[...][None], pay_ref.shape)


def shifted(value, offset):
    if offset == 0:
        return value
    return pltpu.roll(value, (-offset) % value.shape[0], 0)


def cell_index(geo, shape):
    r = lax.broadcasted_iota(jnp.int32, shape, 0).astype(F32)
    line = jnp.floor((r + 0.5) * (1.0 / geo.pitch))
    column = r - geo.pitch * line
    frame = jnp.floor((line + 0.5) * (1.0 / geo.height))
    return line - geo.height * frame, column


def edge_masks(geo, width):
    line, column = cell_index(geo, (geo.clip_rows, width))
    return (
        {e: (line + e > -0.5) & (line + e < geo.height - 0.5) for e in (-1, 1)},
        {e: (column + e > -0.5) & (column + e < geo.width - 0.5) for e in (-1, 1)},
    )


def gather_cells(geo, value, masks, sign, store):
    lines, columns = masks
    for b, dw in enumerate((-1, 0, 1)):
        moved = shifted(value, sign * dw)
        if dw and geo.dense:
            moved = jnp.where(columns[sign * dw], moved, 0.0)
        for a, dh in enumerate((-1, 0, 1)):
            placed = shifted(moved, sign * dh * geo.pitch)
            if dh:
                placed = jnp.where(lines[sign * dh], placed, 0.0)
            store(3 * a + b, placed)


def frame_shift(geo, value, offset):
    if offset == 0:
        return value
    size = geo.frame_rows
    blank = jnp.zeros((size, value.shape[1]), value.dtype)
    if offset > 0:
        return jnp.concatenate([value[size:], blank], axis=0)
    return jnp.concatenate([blank, value[:-size]], axis=0)


def mean_cells(geo, value, masks):
    lines, columns = masks
    total = value
    for e in (-1, 1):
        moved = shifted(value, e)
        total = total + (jnp.where(columns[e], moved, 0.0) if geo.dense else moved)
    again = total
    for e in (-1, 1):
        again = again + jnp.where(lines[e], shifted(total, e * geo.pitch), 0.0)
    return (again + frame_shift(geo, again, 1) + frame_shift(geo, again, -1)) / 27.0


def clear_edges(geo, ref, clip):
    base = clip * geo.padded_rows
    size = geo.frame_rows
    blank = jnp.zeros((size, ref.shape[1]), ref.dtype)
    ref[base : base + size, :] = blank
    ref[base + geo.padded_rows - size : base + geo.padded_rows, :] = blank


def assemble_points(w_ref, scratch, groups):
    for s in range(groups):
        part = w_ref[s].astype(F32)
        at = start = 0
        for width in POINT_WIDTHS:
            own = width // groups
            scratch[start + s * own : start + (s + 1) * own, :] = part[at : at + own, :]
            at += own
            start += width


def split_points(value, scratch, groups):
    size = POINT // groups
    for s in range(groups):
        at = start = 0
        for width in POINT_WIDTHS:
            own = width // groups
            scratch[s * size + at : s * size + at + own, :] = value[
                start + s * own : start + (s + 1) * own, :
            ]
            at += own
            start += width


def prepare_kernel(groups, x_ref, o_ref):
    width = o_ref.shape[2]
    for s in range(groups):
        o_ref[s] = x_ref[:, s * width : (s + 1) * width]


def early_first_kernel(
    groups, x_ref, w_ref, m_ref, mc_ref, a_ref, wt_ref, y_ref, pay_ref, xs, ws, tile
):
    depth, rows = x_ref.shape[1], x_ref.shape[2]
    for s in range(groups):
        xs[s * depth : (s + 1) * depth, :] = x_ref[s].astype(F32)
    for j in range(0, rows, 128):
        size = min(128, rows - j)
        turned = jnp.transpose(xs[:, j : j + size])
        a_ref[j : j + size, :] = (turned * m_ref[j : j + size, 0:1]).astype(BF16)
    assemble_points(w_ref, ws, groups)
    wt_ref[...] = ws[...].astype(BF16)
    y_ref[...] = nt(a_ref[...], wt_ref[DIRECT : DIRECT + REDUCED, :])
    tile[...] = jnp.zeros_like(tile)
    count = jnp.sum(m_ref[...], axis=0, keepdims=True)
    coarse = jnp.sum(mc_ref[...], axis=0, keepdims=True)
    mean, spread = local_moments(y_ref, m_ref, rows, count[:, 0:1])
    put_row(tile, 0, mean)
    put_row(tile, 2, count)
    put_row(tile, 3, coarse)
    put_row(tile, 4, spread)
    send_tile(pay_ref, tile)


def other_points_kernel(geo, clips, a_ref, wt_ref, m_ref, yd_ref, yp_ref, tile):
    yd_ref[...] = nt(a_ref[...], wt_ref[:DIRECT, :])
    projected = nt(a_ref[...], wt_ref[DIRECT + REDUCED :, :])
    masks = edge_masks(geo, PROJECT)
    for c in range(clips):
        rows = slice(c * geo.clip_rows, (c + 1) * geo.clip_rows)
        yp_ref[rows, :] = mean_cells(geo, projected[rows], masks)
    tile[...] = jnp.zeros_like(tile)
    count = jnp.sum(m_ref[...], axis=0, keepdims=True)[:, 0:1]
    for unit, ref in (("d", yd_ref), ("p", yp_ref)):
        mean, spread = local_moments(ref, m_ref, clips * geo.clip_rows, count)
        put_row(tile, TILE_ROW[unit][0], mean)
        put_row(tile, 8 + TILE_ROW[unit][0], spread)


def second_kernel(
    geo, clips, count_row, g_ref, counts_ref, aff_ref, y_ref, m_ref, kw_ref, ks_ref, pd_ref,
    bn_ref, bs_ref, yw_ref, ys_ref, pay_ref, st_ref, us, tile
):
    rows = clips * geo.clip_rows
    counts = counts_ref[:, count_row : count_row + 1, :]
    means, rstds = combine_moments(g_ref[...], counts, 0, 4, 2)
    st_ref[...] = jnp.zeros_like(st_ref)
    st_ref[0:2, :] = means
    st_ref[2:3, :] = jnp.sum(counts, axis=0)
    st_ref[4:6, :] = rstds
    mean, rstd = row(means, 0, REDUCED), row(rstds, 0, REDUCED)
    scale, shift = affine_of(aff_ref, geo.block, "r")

    def activate(r, carry):
        at = pl.ds(r, CHUNK)
        h = scale * ((y_ref[at, :] - mean) * rstd) + shift
        us[at, :] = h * jax.nn.sigmoid(h) * m_ref[at, 0:1]
        return carry

    each_chunk(rows, activate)
    masks = edge_masks(geo, REDUCED)
    size = geo.frame_rows
    for c in range(clips):
        base = c * geo.padded_rows
        clear_edges(geo, bn_ref, c)
        clear_edges(geo, bs_ref, c)

        def store(j, placed):
            at = slice(base + size, base + size + geo.clip_rows)
            bn_ref[at, NARROW * j : NARROW * (j + 1)] = placed[:, :NARROW].astype(BF16)
            bs_ref[at, SQUEEZE * j : SQUEEZE * (j + 1)] = placed[:, NARROW:].astype(BF16)

        gather_cells(geo, us[c * geo.clip_rows : (c + 1) * geo.clip_rows, :], masks, 1, store)
    for c in range(clips):
        base = c * geo.padded_rows
        out = slice(c * geo.clip_rows, (c + 1) * geo.clip_rows)
        for b_ref, k_ref, o_ref in ((bn_ref, kw_ref, yw_ref), (bs_ref, ks_ref, ys_ref)):
            width = b_ref.shape[1]
            total = None
            for t in range(3):
                term = nt(
                    b_ref[base + size * t : base + size * t + geo.clip_rows, :],
                    k_ref[:, width * t : width * (t + 1)],
                )
                total = term if total is None else total + term
            o_ref[out, :] = total
    tile[...] = pd_ref[...]
    own = jnp.sum(m_ref[...], axis=0, keepdims=True)[:, 0:1]
    for unit, ref in (("w", yw_ref), ("s", ys_ref)):
        mean, spread = local_moments(ref, m_ref, rows, own)
        put_row(tile, TILE_ROW[unit][0], mean)
        put_row(tile, 8 + TILE_ROW[unit][0], spread)
    send_tile(pay_ref, tile)


def outer_stats(st, unit):
    first, width = TILE_ROW[unit]
    return row(st, first, width), row(st, 8 + first, width)


def pool_kernel(
    groups, clips, g_ref, counts_ref, aff_ref, yd_ref, yw_ref, ys_ref, yp_ref, m_ref, pool_ref,
    w_ref, mc_ref, a_ref, wt_ref, y_ref, pay_ref, st_ref, high, low, ws, tile
):
    means, rstds = combine_moments(g_ref[...], counts_ref[:, 2:3, :], 0, 8, 8)
    st_ref[0:8, :] = means
    st_ref[8:16, :] = rstds
    st = st_ref[...]
    at_column = 0
    for unit, ref in zip(OUTER, (yd_ref, yw_ref, ys_ref, yp_ref)):
        width = TILE_ROW[unit][1]
        mean, rstd = outer_stats(st, unit)
        scale, shift = affine_of(aff_ref, 0, unit)

        def activate(r, carry):
            at = pl.ds(r, CHUNK)
            h = scale * ((ref[at, :] - mean) * rstd) + shift
            u = h * jax.nn.sigmoid(h) * m_ref[at, 0:1]
            top = u.astype(BF16)
            high[at, :width] = top
            low[at, :width] = (u - top.astype(F32)).astype(BF16)
            return carry

        each_chunk(clips * EARLY.clip_rows, activate)
        for c in range(clips):
            rows = slice(c * EARLY.clip_rows, (c + 1) * EARLY.clip_rows)
            pooled = nn(pool_ref[...], high[rows, :width]) + nn(pool_ref[...], low[rows, :width])
            out = slice(c * LATE.clip_rows, (c + 1) * LATE.clip_rows)
            a_ref[out, at_column : at_column + width] = pooled.astype(BF16)
        at_column += width
    assemble_points(w_ref, ws, groups)
    wt_ref[...] = ws[...].astype(BF16)
    y_ref[...] = nt(a_ref[...], wt_ref[DIRECT : DIRECT + REDUCED, :])
    tile[...] = jnp.zeros_like(tile)
    own = jnp.sum(mc_ref[...], axis=0, keepdims=True)
    mean, spread = local_moments(y_ref, mc_ref, clips * LATE.clip_rows, own[:, 0:1])
    put_row(tile, 0, mean)
    put_row(tile, 4, spread)
    send_tile(pay_ref, tile)


def local_backward(y_ref, dz_of, m_ref, mean, rstd, scale, shift, dh_ref, out_ref, rows):
    width = y_ref.shape[1]

    def body(r, carry):
        at = pl.ds(r, CHUNK)
        masking = m_ref[at, 0:1]
        xhat = (y_ref[at, :] - mean) * rstd
        h = scale * xhat + shift
        gate = jax.nn.sigmoid(h)
        if out_ref is not None:
            out_ref[at, :] = (h * gate * masking).astype(out_ref.dtype)
        dh = dz_of(at) * masking * gate * (1.0 + h * (1.0 - gate))
        dh_ref[at, :] = dh
        return carry[0] + fold8(dh * xhat), carry[1] + fold8(dh)

    blank = jnp.zeros((8, width), F32)
    first, second = each_chunk(rows, body, (blank, blank))
    return jnp.sum(first, axis=0, keepdims=True), jnp.sum(second, axis=0, keepdims=True)


def late_outputs_kernel(
    clips, g_ref, counts_ref, aff_ref, yd_ref, yw_ref, ys_ref, yp_ref, mc_ref,
    ud_ref, uw_ref, us_ref, up_ref,
    od_ref, ow_ref, os_ref, op_ref, dd_ref, dw_ref, ds_ref, dp_ref, pay_ref, st_ref, tile
):
    means, rstds = combine_moments(g_ref[...], counts_ref[:, 3:4, :], 0, 8, 8)
    st_ref[0:8, :] = means
    st_ref[8:16, :] = rstds
    st = st_ref[...]
    tile[...] = jnp.zeros_like(tile)
    for unit, y_ref, up, o_ref, dh_ref in zip(
        OUTER,
        (yd_ref, yw_ref, ys_ref, yp_ref),
        (ud_ref, uw_ref, us_ref, up_ref),
        (od_ref, ow_ref, os_ref, op_ref),
        (dd_ref, dw_ref, ds_ref, dp_ref),
    ):
        mean, rstd = outer_stats(st, unit)
        scale, shift = affine_of(aff_ref, 1, unit)
        sums = local_backward(
            y_ref, lambda at: up[at, :].astype(F32), m_ref=mc_ref, mean=mean, rstd=rstd,
            scale=scale, shift=shift, dh_ref=dh_ref, out_ref=o_ref, rows=clips * LATE.clip_rows,
        )
        put_row(tile, TILE_ROW[unit][0], sums[0])
        put_row(tile, 8 + TILE_ROW[unit][0], sums[1])
    send_tile(pay_ref, tile)


def finish_rows(dh, y, masking, mean, rstd, scale, scale_sum, shift_sum, count):
    xhat = (y - mean) * rstd
    return scale * rstd * (dh - (shift_sum + xhat * scale_sum) / count) * masking


def inner_backward_kernel(
    geo, clips, g_ref, st_ref, str_ref, aff_ref, dw_ref, ds_ref, yw_ref, ys_ref, yr_ref, kw_ref,
    ks_ref, m_ref, gw_ref, gs_ref, dh_ref, pay_ref, sums_ref, pad_w, pad_s, kt_w, kt_s, dz, tile
):
    rows = clips * geo.clip_rows
    size = geo.frame_rows
    sums_ref[...] = jnp.sum(g_ref[...], axis=0)
    sums, st, st_r = sums_ref[...], st_ref[...], str_ref[...]
    count = st_r[2:3, 0:1]
    for unit, d_ref, y_ref, o_ref, pad in (
        ("w", dw_ref, yw_ref, gw_ref, pad_w),
        ("s", ds_ref, ys_ref, gs_ref, pad_s),
    ):
        first, width = TILE_ROW[unit]
        mean, rstd = outer_stats(st, unit)
        scale, _ = affine_of(aff_ref, geo.block, unit)
        scale_sum, shift_sum = row(sums, first, width), row(sums, 8 + first, width)

        def finish(r, carry):
            at = pl.ds(r, CHUNK)
            dy = finish_rows(
                d_ref[at, :], y_ref[at, :], m_ref[at, 0:1], mean, rstd, scale, scale_sum,
                shift_sum, count,
            )
            o_ref[at, :] = dy.astype(BF16)
            return carry

        each_chunk(rows, finish)
        masks = edge_masks(geo, width)
        for c in range(clips):
            base = c * geo.padded_rows
            clear_edges(geo, pad, c)

            def store(j, placed):
                at = slice(base + size, base + size + geo.clip_rows)
                pad[at, width * j : width * (j + 1)] = placed.astype(BF16)

            value = o_ref[c * geo.clip_rows : (c + 1) * geo.clip_rows, :].astype(F32)
            gather_cells(geo, value, masks, -1, store)
    for k_ref, kt, width, depth in ((kw_ref, kt_w, WIDE, NARROW), (ks_ref, kt_s, SPREAD, SQUEEZE)):
        for t in range(3):
            for j in range(9):
                at = (9 * t + j) * depth
                kt[t, width * j : width * (j + 1), :] = k_ref[:, at : at + depth]
    for pad, kt, depth, start in ((pad_w, kt_w, NARROW, 0), (pad_s, kt_s, SQUEEZE, NARROW)):
        for c in range(clips):
            base = c * geo.padded_rows
            total = None
            for t in range(3):
                at = base + size * (2 - t)
                term = nn(pad[at : at + geo.clip_rows, :], kt[t])
                total = term if total is None else total + term
            dz[c * geo.clip_rows : (c + 1) * geo.clip_rows, start : start + depth] = total
    scale, shift = affine_of(aff_ref, geo.block, "r")
    first, second = local_backward(
        yr_ref, lambda at: dz[at, :], m_ref=m_ref, mean=row(st_r, 0, REDUCED),
        rstd=row(st_r, 4, REDUCED), scale=scale, shift=shift, dh_ref=dh_ref, out_ref=None, rows=rows,
    )
    tile[...] = jnp.zeros_like(tile)
    put_row(tile, 0, first)
    put_row(tile, 4, second)
    send_tile(pay_ref, tile)


def kernel_grad_kernel(geo, clips, gw_ref, gs_ref, bn_ref, bs_ref, ow_ref, os_ref):
    size = geo.frame_rows
    for g_ref, b_ref, o_ref in ((gw_ref, bn_ref, ow_ref), (gs_ref, bs_ref, os_ref)):
        width = b_ref.shape[1]
        for t in range(3):
            total = None
            for c in range(clips):
                at = c * geo.padded_rows + size * t
                term = tn(
                    g_ref[c * geo.clip_rows : (c + 1) * geo.clip_rows, :],
                    b_ref[at : at + geo.clip_rows, :],
                )
                total = term if total is None else total + term
            o_ref[:, width * t : width * (t + 1)] = total.astype(BF16)


def point_gradients(
    geo, clips, g_ref, sums_ref, st_ref, str_ref, aff_ref, dr_ref, dd_ref, dp_ref, yr_ref, yd_ref,
    yp_ref, m_ref, gy_ref, sumr_ref, held
):
    rows = clips * geo.clip_rows
    sumr_ref[...] = jnp.sum(g_ref[...], axis=0)
    sums, sums_r, st, st_r = sums_ref[...], sumr_ref[...], st_ref[...], str_ref[...]
    count = st_r[2:3, 0:1]
    scale_d, _ = affine_of(aff_ref, geo.block, "d")
    scale_r, _ = affine_of(aff_ref, geo.block, "r")
    scale_p, _ = affine_of(aff_ref, geo.block, "p")
    mean_d, rstd_d = outer_stats(st, "d")
    mean_p, rstd_p = outer_stats(st, "p")
    mean_r, rstd_r = row(st_r, 0, REDUCED), row(st_r, 4, REDUCED)

    def pair(unit):
        first, width = TILE_ROW[unit]
        return row(sums, first, width), row(sums, 8 + first, width)

    pair_d, pair_p = pair("d"), pair("p")
    pair_r = (row(sums_r, 0, REDUCED), row(sums_r, 4, REDUCED))

    def finish(r, carry):
        at = pl.ds(r, CHUNK)
        masking = m_ref[at, 0:1]
        gy_ref[at, :DIRECT] = finish_rows(
            dd_ref[at, :], yd_ref[at, :], masking, mean_d, rstd_d, scale_d, *pair_d, count
        ).astype(BF16)
        gy_ref[at, DIRECT : DIRECT + REDUCED] = finish_rows(
            dr_ref[at, :], yr_ref[at, :], masking, mean_r, rstd_r, scale_r, *pair_r, count
        ).astype(BF16)
        held[at, :] = finish_rows(
            dp_ref[at, :], yp_ref[at, :], masking, mean_p, rstd_p, scale_p, *pair_p, count
        )
        return carry

    each_chunk(rows, finish)
    masks = edge_masks(geo, PROJECT)
    for c in range(clips):
        at = slice(c * geo.clip_rows, (c + 1) * geo.clip_rows)
        gy_ref[at, DIRECT + REDUCED :] = mean_cells(geo, held[at, :], masks).astype(BF16)


def late_input_kernel(
    clips, g_ref, sums_ref, st_ref, str_ref, aff_ref, dr_ref, dd_ref, dp_ref, yr_ref, yd_ref, yp_ref,
    mc_ref, wt_ref, spread_ref, est_ref, ed_ref, ew_ref, es_ref, ep_ref, m_ref,
    gy_ref, hd_ref, hw_ref, hs_ref, hp_ref, pay_ref, sumr_ref, held, grad, wide, tile
):
    point_gradients(
        LATE, clips, g_ref, sums_ref, st_ref, str_ref, aff_ref, dr_ref, dd_ref, dp_ref, yr_ref,
        yd_ref, yp_ref, mc_ref, gy_ref, sumr_ref, held,
    )
    grad[...] = nn(gy_ref[...], wt_ref[...]).astype(BF16)
    st = est_ref[...]
    tile[...] = jnp.zeros_like(tile)
    column = 0
    for unit, y_ref, dh_ref in zip(
        OUTER, (ed_ref, ew_ref, es_ref, ep_ref), (hd_ref, hw_ref, hs_ref, hp_ref)
    ):
        width = TILE_ROW[unit][1]
        for c in range(clips):
            wide[c * EARLY.clip_rows : (c + 1) * EARLY.clip_rows, :width] = nn(
                spread_ref[...],
                grad[c * LATE.clip_rows : (c + 1) * LATE.clip_rows, column : column + width],
            )
        column += width
        mean, rstd = outer_stats(st, unit)
        scale, shift = affine_of(aff_ref, 0, unit)
        sums = local_backward(
            y_ref, lambda at: wide[at, :width], m_ref=m_ref, mean=mean, rstd=rstd, scale=scale,
            shift=shift, dh_ref=dh_ref, out_ref=None, rows=clips * EARLY.clip_rows,
        )
        put_row(tile, TILE_ROW[unit][0], sums[0])
        put_row(tile, 8 + TILE_ROW[unit][0], sums[1])
    send_tile(pay_ref, tile)


def early_input_kernel(
    groups, clips, g_ref, sums_ref, st_ref, str_ref, aff_ref, dr_ref, dd_ref, dp_ref, yr_ref, yd_ref,
    yp_ref, m_ref, wt_ref, gy_ref, x_ref, sumr_ref, held
):
    point_gradients(
        EARLY, clips, g_ref, sums_ref, st_ref, str_ref, aff_ref, dr_ref, dd_ref, dp_ref, yr_ref,
        yd_ref, yp_ref, m_ref, gy_ref, sumr_ref, held,
    )
    depth = x_ref.shape[1]
    rows = clips * EARLY.clip_rows
    for j in range(0, rows, 128):
        size = min(128, rows - j)
        grad = nn(gy_ref[j : j + size, :], wt_ref[...]) * m_ref[j : j + size, 0:1]
        turned = jnp.transpose(grad)
        for s in range(groups):
            x_ref[s, :, j : j + size] = turned[s * depth : (s + 1) * depth, :].astype(BF16)


def point_grad_kernel(groups, gy_ref, a_ref, o_ref, scratch):
    split_points(tn(gy_ref[...], a_ref[...]), scratch, groups)
    o_ref[...] = scratch[...].astype(BF16)


def feature_kernel(groups, x_ref, o_ref):
    width = x_ref.shape[2]
    for s in range(groups):
        o_ref[:, s * width : (s + 1) * width] = x_ref[s].astype(F32)


def pool_matrix():
    matrix = np.zeros((LATE.clip_rows, EARLY.clip_rows), np.float32)
    for f in range(EARLY.frames):
        for h in range(EARLY.height):
            for w in range(EARLY.width):
                cell = (f // 2) * LATE.frame_rows + (h // 2) * LATE.pitch + w // 2
                matrix[cell, (f * EARLY.height + h) * EARLY.width + w] = 0.125
    return matrix


def pad_late(field):
    padded = jnp.pad(field, ((0, 0), (0, 0), (0, 0), (0, LATE.pitch - LATE.width), (0, 0)))
    return padded.reshape(-1, field.shape[4])


def shards(
    clip_features, visible, direct_early, narrow_early, squeeze_early, project_early, direct_late,
    narrow_late, squeeze_late, project_late, wide_kernels, spread_kernels, direct_norm, narrow_norm,
    wide_norm, squeeze_norm, spread_norm, project_norm, upstream_direct, upstream_wide,
    upstream_spread, upstream_project,
):
    groups = lax.axis_size("ch")
    devices = groups * lax.axis_size("batch")
    me = lax.axis_index("ch")
    held_clips = visible.shape[0]
    clips = held_clips // groups
    rows = clips * EARLY.clip_rows
    late_rows = clips * LATE.clip_rows
    depth = clip_features.shape[0]
    features = depth * groups

    def exchange(payload):
        return lax.all_to_all(payload, BOTH, 0, 0)

    (pieces,) = call(
        lambda *refs: prepare_kernel(groups, *refs), [((groups, depth, rows), BF16)], [clip_features]
    )
    arrived = lax.all_to_all(pieces, "ch", 0, 0)
    own_visible = lax.dynamic_slice_in_dim(visible, me * clips, clips, 0)
    fine = own_visible.astype(F32).reshape(rows, 1)
    mask = jnp.broadcast_to(fine, (rows, 128))
    cells = own_visible.reshape(clips, 2, 2, 6, 2, 6, 2).max(axis=(2, 4, 6)).astype(F32)
    coarse = jnp.broadcast_to(pad_late(cells[..., None]), (late_rows, 128))

    def gathered(value):
        return lax.all_gather(value, "ch", axis=0, tiled=True)

    def stacked_points(parts):
        local = jnp.concatenate([part.T for part in parts], axis=0)
        return lax.all_gather(local, "ch", axis=0)

    early_points = stacked_points((direct_early, narrow_early, squeeze_early, project_early))
    norms = (direct_norm, narrow_norm, squeeze_norm, wide_norm, spread_norm, project_norm)
    joined = lax.all_gather(jnp.concatenate(norms, axis=2), "ch", axis=0).astype(F32)
    units, at = [], 0
    for norm in norms:
        width = norm.shape[2]
        piece = jnp.moveaxis(joined[..., at : at + width], 0, 2)
        units.append(piece.reshape(4, groups * width))
        at += width
    affine = jnp.concatenate(
        [
            units[0], units[1], units[2], jnp.zeros((4, 64), F32), units[3], jnp.zeros((4, 64), F32),
            units[4], units[5],
        ],
        axis=1,
    )
    wide_rows = wide_kernels.reshape(2, -1, WIDE_COLUMNS)
    spread_rows = jnp.transpose(
        spread_kernels.reshape(2, SPREAD_COLUMNS, spread_kernels.shape[3]), (0, 2, 1)
    )
    kw_early = gathered(wide_rows[0])
    ks_early = gathered(spread_rows[0])
    late_points = stacked_points((direct_late, narrow_late, squeeze_late, project_late))
    kw_late = gathered(wide_rows[1])
    ks_late = gathered(spread_rows[1])

    upstream = (upstream_direct, upstream_wide, upstream_spread, upstream_project)
    up_joined = jnp.concatenate(upstream, axis=4)
    up_parts = up_joined.reshape((groups, clips) + up_joined.shape[1:])
    up_arrived = lax.all_to_all(up_parts, "ch", 0, 0)
    ups, at = [], 0
    for part in upstream:
        width = part.shape[4]
        piece = jnp.moveaxis(up_arrived[..., at : at + width], 0, 4)
        ups.append(pad_late(piece.reshape(piece.shape[:4] + (groups * width,))))
        at += width

    pool = jnp.asarray(pool_matrix(), BF16)
    spread_back = jnp.asarray(pool_matrix().T, BF16)

    act, wt, yr, pay = call(
        lambda *refs: early_first_kernel(groups, *refs),
        [
            ((rows, features), BF16), ((POINT, features), BF16), ((rows, REDUCED), F32),
            ((devices, 8, 128), F32),
        ],
        [arrived, early_points, mask, coarse],
        [((features, rows), F32), ((POINT, features), F32), ((8, 128), F32)],
    )
    counts = exchange(pay)
    yd, yp, tile = call(
        lambda *refs: other_points_kernel(EARLY, clips, *refs),
        [((rows, DIRECT), F32), ((rows, PROJECT), F32), ((16, 128), F32)],
        [act, wt, mask],
    )

    def second(geo, count_row, g, y, masking, kw, ks, other):
        own = clips * geo.clip_rows
        padded = clips * geo.padded_rows
        return call(
            lambda *refs: second_kernel(geo, clips, count_row, *refs),
            [
                ((padded, 9 * NARROW), BF16), ((padded, 9 * SQUEEZE), BF16), ((own, WIDE), F32),
                ((own, SPREAD), F32), ((devices, 16, 128), F32), ((8, 128), F32),
            ],
            [g, counts, affine, y, masking, kw, ks, other],
            [((own, REDUCED), F32), ((16, 128), F32)],
        )

    bn, bs, yw, ys, pay, st_r = second(EARLY, 2, counts, yr, mask, kw_early, ks_early, tile)
    g = exchange(pay)
    late_act, late_wt, lyr, pay, st = call(
        lambda *refs: pool_kernel(groups, clips, *refs),
        [
            ((late_rows, CONCAT), BF16), ((POINT, CONCAT), BF16), ((late_rows, REDUCED), F32),
            ((devices, 8, 128), F32), ((16, 128), F32),
        ],
        [g, counts, affine, yd, yw, ys, yp, mask, pool, late_points, coarse],
        [((rows, 384), BF16), ((rows, 384), BF16), ((POINT, CONCAT), F32), ((8, 128), F32)],
    )
    g = exchange(pay)
    lyd, lyp, tile = call(
        lambda *refs: other_points_kernel(LATE, clips, *refs),
        [((late_rows, DIRECT), F32), ((late_rows, PROJECT), F32), ((16, 128), F32)],
        [late_act, late_wt, coarse],
    )
    lbn, lbs, lyw, lys, pay, lst_r = second(LATE, 3, g, lyr, coarse, kw_late, ks_late, tile)
    g = exchange(pay)
    widths = [TILE_ROW[unit][1] for unit in OUTER]
    res = call(
        lambda *refs: late_outputs_kernel(clips, *refs),
        [((late_rows, w), BF16) for w in widths]
        + [((late_rows, w), F32) for w in widths]
        + [((devices, 16, 128), F32), ((16, 128), F32)],
        [g, counts, affine, lyd, lyw, lys, lyp, coarse] + ups,
        [((16, 128), F32)],
    )
    outs, (hd, hw, hs, hp), (pay, lst) = res[:4], res[4:8], res[8:]
    g = exchange(pay)

    def inner(geo, g, st, st_r, hw, hs, yw, ys, yr, kw, ks, masking):
        own = clips * geo.clip_rows
        padded = clips * geo.padded_rows
        return call(
            lambda *refs: inner_backward_kernel(geo, clips, *refs),
            [
                ((own, WIDE), BF16), ((own, SPREAD), BF16), ((own, REDUCED), F32),
                ((devices, 8, 128), F32), ((16, 128), F32),
            ],
            [g, st, st_r, affine, hw, hs, yw, ys, yr, kw, ks, masking],
            [
                ((padded, 9 * WIDE), BF16), ((padded, 9 * SPREAD), BF16),
                ((3, 9 * WIDE, NARROW), BF16), ((3, 9 * SPREAD, SQUEEZE), BF16),
                ((own, REDUCED), F32), ((8, 128), F32),
            ],
        )

    def kernel_grads(geo, gw, gs, bn, bs):
        return call(
            lambda *refs: kernel_grad_kernel(geo, clips, *refs),
            [((WIDE, WIDE_COLUMNS), BF16), ((SPREAD, SPREAD_COLUMNS), BF16)],
            [gw, gs, bn, bs],
        )

    def point_grads(gy, act):
        return call(
            lambda *refs: point_grad_kernel(groups, *refs),
            [((POINT, act.shape[1]), BF16)],
            [gy, act],
            [((POINT, act.shape[1]), F32)],
        )[0]

    def reduced(value):
        part = lax.psum_scatter(value, "ch", scatter_dimension=0, tiled=True)
        return lax.psum(part, "batch")

    gw, gs, hr, pay, late_sums = inner(
        LATE, g, lst, lst_r, hw, hs, lyw, lys, lyr, kw_late, ks_late, coarse
    )
    g = exchange(pay)
    late_kw_grad, late_ks_grad = kernel_grads(LATE, gw, gs, lbn, lbs)
    gy, ed, ew, es, ep, pay, late_sums_r = call(
        lambda *refs: late_input_kernel(clips, *refs),
        [((late_rows, POINT), BF16)]
        + [((rows, w), F32) for w in widths]
        + [((devices, 16, 128), F32), ((8, 128), F32)],
        [g, late_sums, lst, lst_r, affine, hr, hd, hp, lyr, lyd, lyp, coarse, late_wt, spread_back,
         st, yd, yw, ys, yp, mask],
        [((late_rows, PROJECT), F32), ((late_rows, CONCAT), BF16), ((rows, WIDE), F32), ((16, 128), F32)],
    )
    g = exchange(pay)
    late_point_grad = point_grads(gy, late_act)
    gw, gs, hr, pay, sums = inner(EARLY, g, st, st_r, ew, es, yw, ys, yr, kw_early, ks_early, mask)
    g = exchange(pay)
    kw_grad, ks_grad = kernel_grads(EARLY, gw, gs, bn, bs)
    gy, x_grad, sums_r = call(
        lambda *refs: early_input_kernel(groups, clips, *refs),
        [((rows, POINT), BF16), ((groups, depth, rows), BF16), ((8, 128), F32)],
        [g, sums, st, st_r, affine, hr, ed, ep, yr, yd, yp, mask, wt],
        [((rows, PROJECT), F32)],
    )
    x_arrived = lax.all_to_all(x_grad, "ch", 0, 0)
    point_grad = point_grads(gy, act)
    (feature_grad,) = call(
        lambda *refs: feature_kernel(groups, *refs),
        [((depth, groups * rows), F32)],
        [x_arrived],
    )

    out_parts = []
    for o in outs:
        cells = o.reshape(clips, LATE.frames, LATE.height, LATE.pitch, -1)[:, :, :, : LATE.width]
        out_parts.append(cells.reshape(cells.shape[:4] + (groups, -1)))
    out_joined = jnp.moveaxis(jnp.concatenate(out_parts, axis=5), 4, 0)
    out_arrived = lax.all_to_all(out_joined, "ch", 0, 0)
    out_arrived = out_arrived.reshape((held_clips,) + out_arrived.shape[2:])
    outputs, at = [], 0
    for part in upstream:
        outputs.append(out_arrived[..., at : at + part.shape[4]])
        at += part.shape[4]

    def point_outputs(value, parts):
        value = reduced(value).astype(F32)
        result, at = [], 0
        for part in parts:
            width = part.shape[1]
            result.append(value[at : at + width].T)
            at += width
        return result

    early_grads = point_outputs(
        point_grad, (direct_early, narrow_early, squeeze_early, project_early)
    )
    late_grads = point_outputs(late_point_grad, (direct_late, narrow_late, squeeze_late, project_late))
    wide_grad = jnp.stack([reduced(kw_grad), reduced(late_kw_grad)]).astype(F32)
    wide_grad = wide_grad.reshape(wide_kernels.shape)
    spread_grad = jnp.stack([reduced(ks_grad), reduced(late_ks_grad)]).astype(F32)
    spread_grad = jnp.transpose(spread_grad, (0, 2, 1)).reshape(spread_kernels.shape)

    def outer_pair(tile, unit):
        first, width = TILE_ROW[unit]
        return [
            jnp.stack([tile[k : k + 3].reshape(-1)[:width] for k in (base, base + 8)])
            for base in (first,)
        ][0]

    def inner_pair(tile, low, high):
        return jnp.stack([tile[k : k + 2].reshape(-1)[low:high] for k in (0, 4)])

    def own_part(early_pair, late_pair):
        both = jnp.stack([early_pair, late_pair])
        size = both.shape[2] // groups
        return lax.dynamic_slice_in_dim(both, me * size, size, 2)

    norm_grads = [
        own_part(outer_pair(sums, "d"), outer_pair(late_sums, "d")),
        own_part(inner_pair(sums_r, 0, NARROW), inner_pair(late_sums_r, 0, NARROW)),
        own_part(outer_pair(sums, "w"), outer_pair(late_sums, "w")),
        own_part(inner_pair(sums_r, NARROW, REDUCED), inner_pair(late_sums_r, NARROW, REDUCED)),
        own_part(outer_pair(sums, "s"), outer_pair(late_sums, "s")),
        own_part(outer_pair(sums, "p"), outer_pair(late_sums, "p")),
    ]
    return tuple(outputs) + (feature_grad,) + tuple(early_grads) + tuple(late_grads) + (
        wide_grad, spread_grad,
    ) + tuple(norm_grads)


def solution(mesh):
    columns = P(None, "ch")
    norm = P(None, None, "ch")
    clips = P("batch", None, None, None, "ch")
    kernels = P(None, None, None, "ch")
    return jax.shard_map(
        shards,
        mesh=mesh,
        in_specs=(P("ch", "batch"), P("batch", None, None, None)) + (columns,) * 9 + (kernels,)
        + (norm,) * 6 + (clips,) * 4,
        out_specs=(clips,) * 4 + (P("ch", "batch"),) + (columns,) * 9 + (kernels,) + (norm,) * 6,
        check_vma=False,
    )
```

```python
import jax
import jax.numpy as jnp
import numpy as np
from jax import lax
from jax.experimental import pallas as pl
from jax.experimental.pallas import tpu as pltpu
from jax.sharding import PartitionSpec as P

F32 = jnp.float32
BF16 = jnp.bfloat16
EPSILON = 0.001
FLOPS_A_US = 1.1e9
BOTH = ("batch", "ch")
DIRECT, NARROW, WIDE, SQUEEZE, SPREAD, PROJECT = 256, 160, 320, 32, 128, 128
REDUCED = NARROW + SQUEEZE
POINT = DIRECT + REDUCED + PROJECT
CONCAT = DIRECT + WIDE + SPREAD + PROJECT
WIDE_COLUMNS = 27 * NARROW
SPREAD_COLUMNS = 27 * SQUEEZE
POINT_WIDTHS = (DIRECT, NARROW, SQUEEZE, PROJECT)
SLOT = {"d": (0, DIRECT), "r": (256, REDUCED), "w": (512, WIDE), "s": (896, SPREAD), "p": (1024, PROJECT)}
SLOTS = 1152
NORM_ORDER = ((0, DIRECT), (256, NARROW), (256 + NARROW, SQUEEZE), (512, WIDE), (896, SPREAD), (1024, PROJECT))
TILE_ROW = {"d": (0, DIRECT), "w": (2, WIDE), "s": (5, SPREAD), "p": (6, PROJECT)}
OUTER = ("d", "w", "s", "p")
CHUNK = 48


class Geometry:
    def __init__(self, frames, height, width, pitch, block):
        self.frames, self.height, self.width, self.pitch = frames, height, width, pitch
        self.block = block
        self.frame_rows = height * pitch
        self.clip_rows = frames * self.frame_rows
        self.padded_rows = (frames + 2) * self.frame_rows
        self.dense = pitch == width


EARLY = Geometry(4, 12, 12, 12, 0)
LATE = Geometry(2, 6, 6, 8, 1)


def nt(a, b):
    return lax.dot_general(a, b, (((1,), (1,)), ((), ())), preferred_element_type=F32)


def nn(a, b):
    return lax.dot_general(a, b, (((1,), (0,)), ((), ())), preferred_element_type=F32)


def tn(a, b):
    return lax.dot_general(a, b, (((0,), (0,)), ((), ())), preferred_element_type=F32)


def call(kernel, outs, ins, scratch=(), us=0, idle=0):
    moved = sum(int(np.prod(s)) * jnp.dtype(d).itemsize for s, d in outs)
    moved += sum(int(np.prod(x.shape)) * x.dtype.itemsize for x in ins[: len(ins) - idle])

    def spec(k, x):
        if k >= len(ins) - idle:
            return pl.BlockSpec(memory_space=pl.ANY)
        return pl.BlockSpec(memory_space=pltpu.SMEM if x.ndim == 1 else pltpu.VMEM)

    def body(*refs):
        kept = len(ins) - idle
        kernel(*refs[:kept], *refs[len(ins) :])

    return pl.pallas_call(
        body,
        out_shape=[jax.ShapeDtypeStruct(s, d) for s, d in outs],
        in_specs=[spec(k, x) for k, x in enumerate(ins)],
        out_specs=[pl.BlockSpec(memory_space=pltpu.VMEM)] * len(outs),
        scratch_shapes=[pltpu.VMEM(s, d) for s, d in scratch],
        compiler_params=pltpu.CompilerParams(vmem_limit_bytes=56 * 2**20),
        cost_estimate=pl.CostEstimate(
            flops=int(us * FLOPS_A_US) or 10 * moved, bytes_accessed=moved, transcendentals=0
        ),
    )(*ins)


def ordered(value, *behind):
    anywhere = pl.BlockSpec(memory_space=pl.ANY)
    return pl.pallas_call(
        lambda *refs: None,
        out_shape=jax.ShapeDtypeStruct(value.shape, value.dtype),
        in_specs=[anywhere] * (1 + len(behind)),
        out_specs=anywhere,
        input_output_aliases={0: 0},
    )(value, *behind)


def each_chunk(rows, body, init=0, chunk=CHUNK):
    return lax.fori_loop(
        0, rows // chunk, lambda i, carry: body(pl.multiple_of(i * chunk, chunk), carry), init
    )


def row(tile, first, width):
    pieces = [
        tile[first + i : first + i + 1, : min(128, width - 128 * i)] for i in range(-(-width // 128))
    ]
    return pieces[0] if len(pieces) == 1 else jnp.concatenate(pieces, axis=1)


def put_row(ref, first, vector):
    width = vector.shape[1]
    for i in range(-(-width // 128)):
        part = vector[:, 128 * i : min(128 * (i + 1), width)]
        ref[first + i : first + i + 1, : part.shape[1]] = part


def affine_of(aff_ref, block, unit):
    start, width = SLOT[unit]
    return (
        aff_ref[2 * block : 2 * block + 1, start : start + width],
        aff_ref[2 * block + 1 : 2 * block + 2, start : start + width],
    )


def fold8(value):
    total = value[0:8]
    for i in range(1, value.shape[0] // 8):
        total = total + value[8 * i : 8 * i + 8]
    return total


def local_moments(y_ref, m_ref, rows, count):
    width = y_ref.shape[1]

    def first(r, acc):
        return acc + fold8(y_ref[pl.ds(r, CHUNK), :] * m_ref[pl.ds(r, CHUNK), 0:1])

    total = each_chunk(rows, first, jnp.zeros((8, width), F32))
    mean = jnp.sum(total, axis=0, keepdims=True) / count

    def second(r, acc):
        centred = (y_ref[pl.ds(r, CHUNK), :] - mean) * m_ref[pl.ds(r, CHUNK), 0:1]
        return acc + fold8(centred * centred)

    spread = each_chunk(rows, second, jnp.zeros((8, width), F32))
    return mean, jnp.sum(spread, axis=0, keepdims=True)


def combine_moments(payload, counts, first, second, size):
    means = payload[:, first : first + size, :]
    total = jnp.sum(counts, axis=0)
    mean = jnp.sum(means * counts, axis=0) / total
    offset = means - mean[None]
    spread = jnp.sum(payload[:, second : second + size, :] + counts * offset * offset, axis=0)
    return mean, lax.rsqrt(spread / total + EPSILON)


def send_tile(pay_ref, tile_ref):
    pay_ref[...] = jnp.broadcast_to(tile_ref[...][None], pay_ref.shape)


def shifted(value, offset):
    if offset == 0:
        return value
    return pltpu.roll(value, (-offset) % value.shape[0], 0)


def cell_index(geo, shape):
    r = lax.broadcasted_iota(jnp.int32, shape, 0).astype(F32)
    line = jnp.floor((r + 0.5) * (1.0 / geo.pitch))
    column = r - geo.pitch * line
    frame = jnp.floor((line + 0.5) * (1.0 / geo.height))
    return line - geo.height * frame, column


def edge_masks(geo, width):
    line, column = cell_index(geo, (geo.clip_rows, width))
    return (
        {e: (line + e > -0.5) & (line + e < geo.height - 0.5) for e in (-1, 1)},
        {e: (column + e > -0.5) & (column + e < geo.width - 0.5) for e in (-1, 1)},
    )


def gather_cells(geo, value, masks, sign, store):
    lines, columns = masks
    for b, dw in enumerate((-1, 0, 1)):
        moved = shifted(value, sign * dw)
        if dw and geo.dense:
            moved = jnp.where(columns[sign * dw], moved, 0.0)
        for a, dh in enumerate((-1, 0, 1)):
            placed = shifted(moved, sign * dh * geo.pitch)
            if dh:
                placed = jnp.where(lines[sign * dh], placed, 0.0)
            store(3 * a + b, placed)


def frame_shift(geo, value, offset):
    if offset == 0:
        return value
    size = geo.frame_rows
    blank = jnp.zeros((size, value.shape[1]), value.dtype)
    if offset > 0:
        return jnp.concatenate([value[size:], blank], axis=0)
    return jnp.concatenate([blank, value[:-size]], axis=0)


def mean_cells(geo, value, masks):
    lines, columns = masks
    total = value
    for e in (-1, 1):
        moved = shifted(value, e)
        total = total + (jnp.where(columns[e], moved, 0.0) if geo.dense else moved)
    again = total
    for e in (-1, 1):
        again = again + jnp.where(lines[e], shifted(total, e * geo.pitch), 0.0)
    return (again + frame_shift(geo, again, 1) + frame_shift(geo, again, -1)) / 27.0


def clear_edges(geo, ref, clip):
    base = clip * geo.padded_rows
    size = geo.frame_rows
    blank = jnp.zeros((size, ref.shape[1]), ref.dtype)
    ref[base : base + size, :] = blank
    ref[base + geo.padded_rows - size : base + geo.padded_rows, :] = blank


def padded16(size):
    return -(-size // 16) * 16


class Packing:
    def __init__(self, groups, features):
        self.groups = groups
        self.wide, self.spread, self.point = WIDE // groups, SPREAD // groups, POINT // groups
        self.wide_rows = padded16(self.wide)
        self.spread_rows = padded16(self.spread)
        self.point_rows = padded16(self.point)
        self.kernels = 3 * WIDE_TILES * self.wide_rows + 3 * SPREAD_TILES * self.spread_rows
        self.features = features
        self.point_tiles = -(-features // 128)
        self.points = self.point_tiles * self.point_rows

    def kernel_tiles(self):
        at = 0
        for own, size, tiles, columns, wide in (
            (self.wide, self.wide_rows, WIDE_TILES, 9 * NARROW, True),
            (self.spread, self.spread_rows, SPREAD_TILES, 9 * SQUEEZE, False),
        ):
            for t in range(3):
                for u in range(tiles):
                    yield at, own, wide, t, u, min(128, columns - 128 * u)
                    at += size

    def point_blocks(self, start):
        for u in range(self.point_tiles):
            yield start + u * self.point_rows, u, min(128, self.features - 128 * u)

    def point_parts(self):
        at = start = 0
        for width in POINT_WIDTHS:
            own = width // self.groups
            yield at, start, own
            at += own
            start += width


WIDE_TILES = -(-9 * NARROW // 128)
SPREAD_TILES = -(-9 * SQUEEZE // 128)


def fit_tile(value):
    width = value.shape[1]
    if width == 128:
        return value
    return jnp.concatenate([value, jnp.zeros((value.shape[0], 128 - width), value.dtype)], axis=1)


def pack_points(pack, part_refs, o_ref, start, scratch):
    for (at, _, own), ref in zip(pack.point_parts(), part_refs):
        scratch[at : at + own, : pack.features] = ref[...].astype(F32)
    for at, u, width in pack.point_blocks(start):
        o_ref[at : at + pack.point, :] = fit_tile(
            scratch[: pack.point, 128 * u : 128 * u + width].astype(BF16)
        )


def unpack_points(pack, me, piece_refs, start, raw, scratch, wt_ref):
    for k, ref in enumerate(piece_refs):
        for at, u, width in pack.point_blocks(start):
            raw[me ^ k, : pack.point, 128 * u : 128 * u + width] = ref[at : at + pack.point, :width].astype(F32)
    for s in range(pack.groups):
        for at, begin, own in pack.point_parts():
            scratch[begin + s * own : begin + (s + 1) * own, :] = raw[s, at : at + own, : pack.features]
    wt_ref[...] = scratch[...].astype(BF16)


def unpack_kernels(pack, me, piece_refs, kw_ref, ks_ref):
    for k, ref in enumerate(piece_refs):
        for at, own, wide, t, u, _ in pack.kernel_tiles():
            target = kw_ref if wide else ks_ref
            size = target.shape[2]
            target[t, me ^ k, :, 128 * u : 128 * u + 128] = ref[at : at + size, :]


def whole_kernel(ref, t, own):
    if own == ref.shape[2]:
        return ref[t].reshape(ref.shape[1] * own, ref.shape[3])
    parts = [ref[t, s].astype(F32)[:own] for s in range(ref.shape[1])]
    return jnp.concatenate(parts, axis=0).astype(BF16)


def prepare_kernel(pack, x_ref, norm_ref, p0, p1, p2, p3, o_ref, b_ref, scratch, rows):
    width = o_ref.shape[2]
    for s in range(pack.groups):
        o_ref[s] = x_ref[:, s * width : (s + 1) * width]
    pack_points(pack, (p0, p1, p2, p3), b_ref, 0, scratch)
    rows[...] = jnp.zeros_like(rows)
    for u in range(-(-norm_ref.shape[1] // 128)):
        part = norm_ref[:, 128 * u : 128 * (u + 1)].astype(F32)
        rows[4 * u : 4 * u + 4, : part.shape[1]] = part
    b_ref[pack.points :, :] = rows[...].astype(BF16)


def split_kernel(x_ref, a_ref, b_ref):
    tiles = x_ref.shape[1] // 128

    def move(first, count):
        value = x_ref[:, pl.ds(128 * first, 128 * count)].astype(F32)
        for r, ref in ((0, a_ref), (1, b_ref)):
            parts = [value[r : r + 1, 128 * j : 128 * (j + 1)] for j in range(count)]
            ref[pl.ds(first, count), :] = jnp.concatenate(parts, axis=0).astype(BF16)

    def step(i, carry):
        move(pl.multiple_of(16 * i, 16), 16)
        return carry

    lax.fori_loop(0, tiles // 16, step, 0)
    if tiles % 16:
        move(tiles // 16 * 16, tiles % 16)


def pack_kernel(pack, w_ref, s_ref, *refs):
    *part_refs, o_ref, scratch = refs
    for at, own, wide, t, u, width in pack.kernel_tiles():
        source, columns = (w_ref, 9 * NARROW) if wide else (s_ref, 9 * SQUEEZE)
        start = columns * t + 128 * u
        o_ref[at : at + own, :] = fit_tile(source[:, start : start + width])
    if part_refs:
        pack_points(pack, part_refs, o_ref, pack.kernels, scratch)


def early_first_kernel(
    pack, me_ref, x_ref, *refs
):
    groups = pack.groups
    piece_refs = refs[:groups]
    m_ref, mc_ref, a_ref, wt_ref, aff_ref, y_ref, pay_ref, xs, raw, ws, norm_raw, tile = refs[groups:]
    me = me_ref[0]
    depth, rows = x_ref.shape[1], x_ref.shape[2]
    for s in range(groups):
        xs[s * depth : (s + 1) * depth, :] = x_ref[s].astype(F32)
    for j in range(0, rows, 128):
        size = min(128, rows - j)
        turned = jnp.transpose(xs[:, j : j + size])
        a_ref[j : j + size, :] = (turned * m_ref[j : j + size, 0:1]).astype(BF16)
    unpack_points(pack, me, piece_refs, 0, raw, ws, wt_ref)
    for k, ref in enumerate(piece_refs):
        norm_raw[me ^ k] = ref[pack.points :, :].astype(F32)
    at = 0
    for slot, whole in NORM_ORDER:
        own = whole // groups
        for s in range(groups):
            left, u = at % 128, at // 128
            first = min(own, 128 - left)
            to = slot + s * own
            aff_ref[:, to : to + first] = norm_raw[s, 4 * u : 4 * u + 4, left : left + first]
            if first < own:
                aff_ref[:, to + first : to + own] = norm_raw[s, 4 * u + 4 : 4 * u + 8, : own - first]
        at += own
    y_ref[...] = nt(a_ref[...], wt_ref[DIRECT : DIRECT + REDUCED, :])
    tile[...] = jnp.zeros_like(tile)
    count = jnp.sum(m_ref[...], axis=0, keepdims=True)
    coarse = jnp.sum(mc_ref[...], axis=0, keepdims=True)
    mean, spread = local_moments(y_ref, m_ref, rows, count[:, 0:1])
    put_row(tile, 0, mean)
    put_row(tile, 2, count)
    put_row(tile, 3, coarse)
    put_row(tile, 4, spread)
    send_tile(pay_ref, tile)


def other_points_kernel(geo, clips, a_ref, wt_ref, m_ref, yd_ref, yp_ref, tile):
    yd_ref[...] = nt(a_ref[...], wt_ref[:DIRECT, :])
    projected = nt(a_ref[...], wt_ref[DIRECT + REDUCED :, :])
    masks = edge_masks(geo, PROJECT)
    for c in range(clips):
        rows = slice(c * geo.clip_rows, (c + 1) * geo.clip_rows)
        yp_ref[rows, :] = mean_cells(geo, projected[rows], masks)
    tile[...] = jnp.zeros_like(tile)
    count = jnp.sum(m_ref[...], axis=0, keepdims=True)[:, 0:1]
    for unit, ref in (("d", yd_ref), ("p", yp_ref)):
        mean, spread = local_moments(ref, m_ref, clips * geo.clip_rows, count)
        put_row(tile, TILE_ROW[unit][0], mean)
        put_row(tile, 8 + TILE_ROW[unit][0], spread)


def second_kernel(
    geo, clips, pack, count_row, me_ref, g_ref, counts_ref, aff_ref, y_ref, m_ref, pd_ref, *refs
):
    piece_refs = refs[: pack.groups]
    (bn_ref, bs_ref, yw_ref, ys_ref, kw_ref, ks_ref, pay_ref, st_ref, us, tile) = refs[pack.groups :]
    unpack_kernels(pack, me_ref[0], piece_refs, kw_ref, ks_ref)
    rows = clips * geo.clip_rows
    counts = counts_ref[:, count_row : count_row + 1, :]
    means, rstds = combine_moments(g_ref[...], counts, 0, 4, 2)
    st_ref[...] = jnp.zeros_like(st_ref)
    st_ref[0:2, :] = means
    st_ref[2:3, :] = jnp.sum(counts, axis=0)
    st_ref[4:6, :] = rstds
    mean, rstd = row(means, 0, REDUCED), row(rstds, 0, REDUCED)
    scale, shift = affine_of(aff_ref, geo.block, "r")

    def activate(r, carry):
        at = pl.ds(r, CHUNK)
        h = scale * ((y_ref[at, :] - mean) * rstd) + shift
        us[at, :] = h * jax.nn.sigmoid(h) * m_ref[at, 0:1]
        return carry

    each_chunk(rows, activate)
    masks = edge_masks(geo, REDUCED)
    size = geo.frame_rows
    for c in range(clips):
        base = c * geo.padded_rows
        clear_edges(geo, bn_ref, c)
        clear_edges(geo, bs_ref, c)
        inside = slice(base + size, base + size + geo.clip_rows)
        for ref, used in ((bn_ref, 9 * NARROW), (bs_ref, 9 * SQUEEZE)):
            ref[inside, used:] = jnp.zeros((geo.clip_rows, ref.shape[1] - used), BF16)

        def store(j, placed):
            at = slice(base + size, base + size + geo.clip_rows)
            bn_ref[at, NARROW * j : NARROW * (j + 1)] = placed[:, :NARROW].astype(BF16)
            bs_ref[at, SQUEEZE * j : SQUEEZE * (j + 1)] = placed[:, NARROW:].astype(BF16)

        gather_cells(geo, us[c * geo.clip_rows : (c + 1) * geo.clip_rows, :], masks, 1, store)
    for c in range(clips):
        base = c * geo.padded_rows
        out = slice(c * geo.clip_rows, (c + 1) * geo.clip_rows)
        for b_ref, k_ref, o_ref, own in (
            (bn_ref, kw_ref, yw_ref, pack.wide), (bs_ref, ks_ref, ys_ref, pack.spread)
        ):
            total = None
            for t in range(3):
                term = nt(
                    b_ref[base + size * t : base + size * t + geo.clip_rows, :],
                    whole_kernel(k_ref, t, own),
                )
                total = term if total is None else total + term
            o_ref[out, :] = total
    tile[...] = pd_ref[...]
    own = jnp.sum(m_ref[...], axis=0, keepdims=True)[:, 0:1]
    for unit, ref in (("w", yw_ref), ("s", ys_ref)):
        mean, spread = local_moments(ref, m_ref, rows, own)
        put_row(tile, TILE_ROW[unit][0], mean)
        put_row(tile, 8 + TILE_ROW[unit][0], spread)
    send_tile(pay_ref, tile)


def outer_stats(st, unit):
    first, width = TILE_ROW[unit]
    return row(st, first, width), row(st, 8 + first, width)


def pool_kernel(
    pack, clips, me_ref, g_ref, counts_ref, aff_ref, yd_ref, yw_ref, ys_ref, yp_ref, m_ref, pool_ref,
    mc_ref, *refs
):
    piece_refs = refs[: pack.groups]
    a_ref, wt_ref, y_ref, pay_ref, st_ref, high, low, raw, ws, tile = refs[pack.groups :]
    means, rstds = combine_moments(g_ref[...], counts_ref[:, 2:3, :], 0, 8, 8)
    st_ref[0:8, :] = means
    st_ref[8:16, :] = rstds
    st = st_ref[...]
    at_column = 0
    for unit, ref in zip(OUTER, (yd_ref, yw_ref, ys_ref, yp_ref)):
        width = TILE_ROW[unit][1]
        mean, rstd = outer_stats(st, unit)
        scale, shift = affine_of(aff_ref, 0, unit)

        def activate(r, carry):
            at = pl.ds(r, CHUNK)
            h = scale * ((ref[at, :] - mean) * rstd) + shift
            u = h * jax.nn.sigmoid(h) * m_ref[at, 0:1]
            top = u.astype(BF16)
            high[at, :width] = top
            low[at, :width] = (u - top.astype(F32)).astype(BF16)
            return carry

        each_chunk(clips * EARLY.clip_rows, activate)
        for c in range(clips):
            rows = slice(c * EARLY.clip_rows, (c + 1) * EARLY.clip_rows)
            pooled = nn(pool_ref[...], high[rows, :width]) + nn(pool_ref[...], low[rows, :width])
            out = slice(c * LATE.clip_rows, (c + 1) * LATE.clip_rows)
            a_ref[out, at_column : at_column + width] = pooled.astype(BF16)
        at_column += width
    unpack_points(pack, me_ref[0], piece_refs, pack.kernels, raw, ws, wt_ref)
    y_ref[...] = nt(a_ref[...], wt_ref[DIRECT : DIRECT + REDUCED, :])
    tile[...] = jnp.zeros_like(tile)
    own = jnp.sum(mc_ref[...], axis=0, keepdims=True)
    mean, spread = local_moments(y_ref, mc_ref, clips * LATE.clip_rows, own[:, 0:1])
    put_row(tile, 0, mean)
    put_row(tile, 4, spread)
    send_tile(pay_ref, tile)


def local_backward(y_ref, dz_of, m_ref, mean, rstd, scale, shift, dh_ref, out_ref, rows):
    width = y_ref.shape[1]

    def body(r, carry):
        at = pl.ds(r, CHUNK)
        masking = m_ref[at, 0:1]
        xhat = (y_ref[at, :] - mean) * rstd
        h = scale * xhat + shift
        gate = jax.nn.sigmoid(h)
        if out_ref is not None:
            out_ref[at, :] = (h * gate * masking).astype(out_ref.dtype)
        dh = dz_of(at) * masking * gate * (1.0 + h * (1.0 - gate))
        dh_ref[at, :] = dh
        return carry[0] + fold8(dh * xhat), carry[1] + fold8(dh)

    blank = jnp.zeros((8, width), F32)
    first, second = each_chunk(rows, body, (blank, blank))
    return jnp.sum(first, axis=0, keepdims=True), jnp.sum(second, axis=0, keepdims=True)


def late_outputs_kernel(
    clips, g_ref, counts_ref, aff_ref, yd_ref, yw_ref, ys_ref, yp_ref, mc_ref,
    ud_ref, uw_ref, us_ref, up_ref,
    od_ref, ow_ref, os_ref, op_ref, dd_ref, dw_ref, ds_ref, dp_ref, pay_ref, st_ref, tile
):
    means, rstds = combine_moments(g_ref[...], counts_ref[:, 3:4, :], 0, 8, 8)
    st_ref[0:8, :] = means
    st_ref[8:16, :] = rstds
    st = st_ref[...]
    tile[...] = jnp.zeros_like(tile)
    for unit, y_ref, up, o_ref, dh_ref in zip(
        OUTER,
        (yd_ref, yw_ref, ys_ref, yp_ref),
        (ud_ref, uw_ref, us_ref, up_ref),
        (od_ref, ow_ref, os_ref, op_ref),
        (dd_ref, dw_ref, ds_ref, dp_ref),
    ):
        mean, rstd = outer_stats(st, unit)
        scale, shift = affine_of(aff_ref, 1, unit)
        sums = local_backward(
            y_ref, lambda at: up[at, :].astype(F32), m_ref=mc_ref, mean=mean, rstd=rstd,
            scale=scale, shift=shift, dh_ref=dh_ref, out_ref=o_ref, rows=clips * LATE.clip_rows,
        )
        put_row(tile, TILE_ROW[unit][0], sums[0])
        put_row(tile, 8 + TILE_ROW[unit][0], sums[1])
    send_tile(pay_ref, tile)


def finish_rows(dh, y, masking, mean, rstd, scale, scale_sum, shift_sum, count):
    xhat = (y - mean) * rstd
    return scale * rstd * (dh - (shift_sum + xhat * scale_sum) / count) * masking


def finish_kernel(
    geo, clips, g_ref, st_ref, str_ref, aff_ref, dw_ref, ds_ref, yw_ref, ys_ref, m_ref,
    gw_ref, gs_ref, sums_ref
):
    rows = clips * geo.clip_rows
    sums_ref[...] = jnp.sum(g_ref[...], axis=0)
    sums, st = sums_ref[...], st_ref[...]
    count = str_ref[2:3, 0:1]
    for unit, d_ref, y_ref, o_ref in (("w", dw_ref, yw_ref, gw_ref), ("s", ds_ref, ys_ref, gs_ref)):
        first, width = TILE_ROW[unit]
        mean, rstd = outer_stats(st, unit)
        scale, _ = affine_of(aff_ref, geo.block, unit)
        scale_sum, shift_sum = row(sums, first, width), row(sums, 8 + first, width)

        def finish(r, carry):
            at = pl.ds(r, CHUNK)
            dy = finish_rows(
                d_ref[at, :], y_ref[at, :], m_ref[at, 0:1], mean, rstd, scale, scale_sum,
                shift_sum, count,
            )
            o_ref[at, :] = dy.astype(BF16)
            return carry

        each_chunk(rows, finish)


def inner_backward_kernel(
    geo, clips, pack, str_ref, aff_ref, gw_ref, gs_ref, yr_ref, kw_ref, ks_ref, m_ref,
    dh_ref, pay_ref, pad_w, pad_s, kt_w, kt_s, dz, tile
):
    rows = clips * geo.clip_rows
    size = geo.frame_rows
    st_r = str_ref[...]
    for width, g_ref, pad in ((WIDE, gw_ref, pad_w), (SPREAD, gs_ref, pad_s)):
        masks = edge_masks(geo, width)
        for c in range(clips):
            base = c * geo.padded_rows
            clear_edges(geo, pad, c)

            def store(j, placed):
                at = slice(base + size, base + size + geo.clip_rows)
                pad[at, width * j : width * (j + 1)] = placed.astype(BF16)

            value = g_ref[c * geo.clip_rows : (c + 1) * geo.clip_rows, :].astype(F32)
            gather_cells(geo, value, masks, -1, store)
    for k_ref, kt, own, width, depth in (
        (kw_ref, kt_w, pack.wide, WIDE, NARROW), (ks_ref, kt_s, pack.spread, SPREAD, SQUEEZE)
    ):
        for t in range(3):
            whole = whole_kernel(k_ref, t, own)
            for j in range(9):
                kt[t, width * j : width * (j + 1), :] = whole[:, depth * j : depth * (j + 1)]
    for pad, kt, depth, start in ((pad_w, kt_w, NARROW, 0), (pad_s, kt_s, SQUEEZE, NARROW)):
        for c in range(clips):
            base = c * geo.padded_rows
            total = None
            for t in range(3):
                at = base + size * (2 - t)
                term = nn(pad[at : at + geo.clip_rows, :], kt[t])
                total = term if total is None else total + term
            dz[c * geo.clip_rows : (c + 1) * geo.clip_rows, start : start + depth] = total
    scale, shift = affine_of(aff_ref, geo.block, "r")
    first, second = local_backward(
        yr_ref, lambda at: dz[at, :], m_ref=m_ref, mean=row(st_r, 0, REDUCED),
        rstd=row(st_r, 4, REDUCED), scale=scale, shift=shift, dh_ref=dh_ref, out_ref=None, rows=rows,
    )
    tile[...] = jnp.zeros_like(tile)
    put_row(tile, 0, first)
    put_row(tile, 4, second)
    send_tile(pay_ref, tile)


def kernel_grad_kernel(
    geo, clips, pack, me_ref, gw_ref, gs_ref, bn_ref, bs_ref, keep_ref, send_ref, grad_w, grad_s
):
    size = geo.frame_rows
    for g_ref, b_ref, grad in ((gw_ref, bn_ref, grad_w), (gs_ref, bs_ref, grad_s)):
        for t in range(3):
            total = None
            for c in range(clips):
                at = c * geo.padded_rows + size * t
                term = tn(
                    g_ref[c * geo.clip_rows : (c + 1) * geo.clip_rows, :],
                    b_ref[at : at + geo.clip_rows, :],
                )
                total = term if total is None else total + term
            grad[t] = total
    me = me_ref[0]
    for k in range(pack.groups):
        target = (keep_ref, send_ref)[k % 2]
        for at, own, wide, t, u, _ in pack.kernel_tiles():
            source = grad_w if wide else grad_s
            first = pl.multiple_of((me ^ k) * own, 8)
            part = source[t, pl.ds(first, own), 128 * u : 128 * u + 128]
            target[k // 2, at : at + own, :] = part.astype(BF16)


def point_grad_kernel(pack, start, me_ref, gy_ref, a_ref, *refs):
    keep_ref, send_ref, whole, shares = refs[-4:]
    for source, target in zip(refs[:-4], (keep_ref, send_ref)):
        target[:, :start, :] = source[...]
    whole[...] = tn(gy_ref[...], a_ref[...])
    for s in range(pack.groups):
        for at, begin, own in pack.point_parts():
            shares[s, at : at + own, : pack.features] = whole[begin + s * own : begin + (s + 1) * own, :]
    me = me_ref[0]
    for k in range(pack.groups):
        target = (keep_ref, send_ref)[k % 2]
        for at, u, width in pack.point_blocks(start):
            target[k // 2, at : at + pack.point, :] = shares[
                me ^ k, : pack.point, 128 * u : 128 * u + 128
            ].astype(BF16)


def halve_kernel(keep_ref, got_ref, even_ref, odd_ref):
    for q in range(keep_ref.shape[0]):
        target = (even_ref, odd_ref)[q % 2]
        target[q // 2] = (keep_ref[q].astype(F32) + got_ref[q].astype(F32)).astype(BF16)


def add_kernel(keep_ref, got_ref, o_ref):
    o_ref[...] = (keep_ref[0].astype(F32) + got_ref[0].astype(F32)).astype(BF16)


def scatter_kernel(mb_ref, keep_ref, got_ref, *refs):
    *o_refs, held = refs
    held[...] = keep_ref[0].astype(F32) + got_ref[0].astype(F32)
    size = held.shape[0] // len(o_refs)
    for k, o_ref in enumerate(o_refs):
        first = pl.multiple_of((mb_ref[0] ^ k) * size, 8)
        o_ref[...] = held[pl.ds(first, size), :].astype(BF16)


def scatter_halves_kernel(mb_ref, keep_ref, got_ref, even_ref, odd_ref, held):
    held[...] = keep_ref[0].astype(F32) + got_ref[0].astype(F32)
    size = even_ref.shape[1]
    for k in range(2 * even_ref.shape[0]):
        first = pl.multiple_of((mb_ref[0] ^ k) * size, 8)
        (even_ref, odd_ref)[k % 2][k // 2] = held[pl.ds(first, size), :].astype(BF16)


def total_kernel(x_ref, *refs):
    *p_refs, o_ref = refs
    total = x_ref[0].astype(F32)
    for k in range(1, x_ref.shape[0]):
        total = total + x_ref[k].astype(F32)
    other = p_refs[0][...].astype(F32)
    for p_ref in p_refs[1:]:
        other = other + p_ref[...].astype(F32)
    size = total.shape[0]
    o_ref[:, :size, :] = jnp.broadcast_to(total.astype(BF16)[None], (o_ref.shape[0],) + total.shape)
    o_ref[:, size:, :] = jnp.broadcast_to(other.astype(BF16)[None], (o_ref.shape[0],) + other.shape)


def read_kernels(pack, rows, w_ref, s_ref, turned):
    for at, own, wide, t, u, width in pack.kernel_tiles():
        target, columns = (w_ref, 9 * NARROW) if wide else (turned, 9 * SQUEEZE)
        start = columns * t + 128 * u
        target[:, start : start + width] = rows[at : at + own, :width].astype(F32)
    s_ref[...] = jnp.transpose(turned[...])


def read_points(pack, start, rows, o_refs):
    for at, u, width in pack.point_blocks(start):
        block = rows[at : at + pack.point, :].astype(F32)
        for (first, _, own), o_ref in zip(pack.point_parts(), o_refs):
            o_ref[:, 128 * u : 128 * u + width] = block[first : first + own, :width]


def late_gradients_kernel(pack, batches, mb_ref, *refs):
    x_refs = refs[:batches]
    w_ref, s_ref, *o_refs, held, turned = refs[batches:]
    for k, x_ref in enumerate(x_refs):
        held[mb_ref[0] ^ k] = x_ref[...]
    rows = held[...].reshape(-1, 128)
    read_kernels(pack, rows, w_ref, s_ref, turned)
    read_points(pack, pack.kernels, rows, o_refs)


def early_gradients_kernel(pack, size, x_ref, late_ref, w_ref, s_ref, *refs):
    *o_refs, held, points, wide, turned = refs
    rest = x_ref.shape[1] - size
    for b in range(x_ref.shape[0]):
        held[b * size : (b + 1) * size, :] = x_ref[b, :size, :]
        points[b * rest : (b + 1) * rest, :] = x_ref[b, size:, :]
    read_kernels(pack, held, wide, s_ref, turned)
    read_points(pack, 0, points, o_refs)

    def join(g, carry):
        parts = []
        for r in range(4):
            at = pl.ds(4 * g + r, 1)
            parts.append(jnp.concatenate([wide[at, :], late_ref[at, :]], axis=0))
        first = pl.multiple_of(4 * WIDE_COLUMNS * g, 128)
        w_ref[:, pl.ds(first, 4 * WIDE_COLUMNS)] = jnp.concatenate(parts, axis=1)
        return carry

    lax.fori_loop(0, pack.wide // 4, join, 0)


def point_gradients(
    geo, clips, g_ref, sums_ref, st_ref, str_ref, aff_ref, dr_ref, dd_ref, dp_ref, yr_ref, yd_ref,
    yp_ref, m_ref, gy_ref, sumr_ref, held
):
    rows = clips * geo.clip_rows
    sumr_ref[...] = jnp.sum(g_ref[...], axis=0)
    sums, sums_r, st, st_r = sums_ref[...], sumr_ref[...], st_ref[...], str_ref[...]
    count = st_r[2:3, 0:1]
    scale_d, _ = affine_of(aff_ref, geo.block, "d")
    scale_r, _ = affine_of(aff_ref, geo.block, "r")
    scale_p, _ = affine_of(aff_ref, geo.block, "p")
    mean_d, rstd_d = outer_stats(st, "d")
    mean_p, rstd_p = outer_stats(st, "p")
    mean_r, rstd_r = row(st_r, 0, REDUCED), row(st_r, 4, REDUCED)

    def pair(unit):
        first, width = TILE_ROW[unit]
        return row(sums, first, width), row(sums, 8 + first, width)

    pair_d, pair_p = pair("d"), pair("p")
    pair_r = (row(sums_r, 0, REDUCED), row(sums_r, 4, REDUCED))

    def finish(r, carry):
        at = pl.ds(r, CHUNK)
        masking = m_ref[at, 0:1]
        gy_ref[at, :DIRECT] = finish_rows(
            dd_ref[at, :], yd_ref[at, :], masking, mean_d, rstd_d, scale_d, *pair_d, count
        ).astype(BF16)
        gy_ref[at, DIRECT : DIRECT + REDUCED] = finish_rows(
            dr_ref[at, :], yr_ref[at, :], masking, mean_r, rstd_r, scale_r, *pair_r, count
        ).astype(BF16)
        held[at, :] = finish_rows(
            dp_ref[at, :], yp_ref[at, :], masking, mean_p, rstd_p, scale_p, *pair_p, count
        )
        return carry

    each_chunk(rows, finish)
    masks = edge_masks(geo, PROJECT)
    for c in range(clips):
        at = slice(c * geo.clip_rows, (c + 1) * geo.clip_rows)
        gy_ref[at, DIRECT + REDUCED :] = mean_cells(geo, held[at, :], masks).astype(BF16)


def late_input_kernel(
    clips, g_ref, sums_ref, st_ref, str_ref, aff_ref, dr_ref, dd_ref, dp_ref, yr_ref, yd_ref, yp_ref,
    mc_ref, wt_ref, spread_ref, est_ref, ed_ref, ew_ref, es_ref, ep_ref, m_ref,
    gy_ref, hd_ref, hw_ref, hs_ref, hp_ref, pay_ref, sumr_ref, held, grad, wide, tile
):
    point_gradients(
        LATE, clips, g_ref, sums_ref, st_ref, str_ref, aff_ref, dr_ref, dd_ref, dp_ref, yr_ref,
        yd_ref, yp_ref, mc_ref, gy_ref, sumr_ref, held,
    )
    grad[...] = nn(gy_ref[...], wt_ref[...]).astype(BF16)
    st = est_ref[...]
    tile[...] = jnp.zeros_like(tile)
    column = 0
    for unit, y_ref, dh_ref in zip(
        OUTER, (ed_ref, ew_ref, es_ref, ep_ref), (hd_ref, hw_ref, hs_ref, hp_ref)
    ):
        width = TILE_ROW[unit][1]
        for c in range(clips):
            wide[c * EARLY.clip_rows : (c + 1) * EARLY.clip_rows, :width] = nn(
                spread_ref[...],
                grad[c * LATE.clip_rows : (c + 1) * LATE.clip_rows, column : column + width],
            )
        column += width
        mean, rstd = outer_stats(st, unit)
        scale, shift = affine_of(aff_ref, 0, unit)
        sums = local_backward(
            y_ref, lambda at: wide[at, :width], m_ref=m_ref, mean=mean, rstd=rstd, scale=scale,
            shift=shift, dh_ref=dh_ref, out_ref=None, rows=clips * EARLY.clip_rows,
        )
        put_row(tile, TILE_ROW[unit][0], sums[0])
        put_row(tile, 8 + TILE_ROW[unit][0], sums[1])
    send_tile(pay_ref, tile)


def early_input_kernel(
    pack, clips, me_ref, g_ref, sums_ref, st_ref, str_ref, aff_ref, dr_ref, dd_ref, dp_ref, yr_ref,
    yd_ref, yp_ref, m_ref, wt_ref, gy_ref, *refs
):
    x_refs = refs[: pack.groups]
    sumr_ref, held, turned = refs[pack.groups :]
    point_gradients(
        EARLY, clips, g_ref, sums_ref, st_ref, str_ref, aff_ref, dr_ref, dd_ref, dp_ref, yr_ref,
        yd_ref, yp_ref, m_ref, gy_ref, sumr_ref, held,
    )
    depth = turned.shape[1]
    rows = clips * EARLY.clip_rows
    for j in range(0, rows, 128):
        size = min(128, rows - j)
        grad = jnp.transpose(nn(gy_ref[j : j + size, :], wt_ref[...]) * m_ref[j : j + size, 0:1])
        for s in range(pack.groups):
            turned[s, :, j : j + size] = grad[s * depth : (s + 1) * depth, :].astype(BF16)
    for k, x_ref in enumerate(x_refs):
        x_ref[...] = turned[me_ref[0] ^ k]


def feature_kernel(pack, me_ref, *refs):
    *x_refs, o_ref, held = refs
    for k, x_ref in enumerate(x_refs):
        held[me_ref[0] ^ k] = x_ref[...]
    width = held.shape[2]
    for s in range(pack.groups):
        o_ref[:, s * width : (s + 1) * width] = held[s].astype(F32)


def pool_matrix():
    matrix = np.zeros((LATE.clip_rows, EARLY.clip_rows), np.float32)
    for f in range(EARLY.frames):
        for h in range(EARLY.height):
            for w in range(EARLY.width):
                cell = (f // 2) * LATE.frame_rows + (h // 2) * LATE.pitch + w // 2
                matrix[cell, (f * EARLY.height + h) * EARLY.width + w] = 0.125
    return matrix


def pad_late(field):
    padded = jnp.pad(field, ((0, 0), (0, 0), (0, 0), (0, LATE.pitch - LATE.width), (0, 0)))
    return padded.reshape(-1, field.shape[4])


def shards(
    clip_features, visible, direct_early, narrow_early, squeeze_early, project_early, direct_late,
    narrow_late, squeeze_late, project_late, wide_kernels, spread_kernels, direct_norm, narrow_norm,
    wide_norm, squeeze_norm, spread_norm, project_norm, upstream_direct, upstream_wide,
    upstream_spread, upstream_project,
):
    groups = lax.axis_size("ch")
    batches = lax.axis_size("batch")
    devices = groups * batches
    me = lax.axis_index("ch")
    me_ref = jnp.reshape(me, (1,)).astype(jnp.int32)
    held_clips = visible.shape[0]
    clips = held_clips // groups
    rows = clips * EARLY.clip_rows
    late_rows = clips * LATE.clip_rows
    depth = clip_features.shape[0]
    features = depth * groups
    pack = Packing(groups, features)
    late_pack = Packing(groups, CONCAT)

    def exchange(payload):
        return lax.all_to_all(payload, BOTH, 0, 0)

    def swap(value, bit):
        return lax.ppermute(value, "ch", [(i, i ^ bit) for i in range(groups)])

    class Shares:
        def __init__(self, own):
            self.pieces, self.bit = {0: own}, groups // 2
            self.step()

        def step(self):
            for k in list(self.pieces):
                self.pieces[k | self.bit] = swap(self.pieces[k], self.bit)
            self.bit //= 2

        def all(self, *behind):
            if behind:
                last = max(self.pieces)
                self.pieces[last] = ordered(self.pieces[last], *behind)
            while self.bit:
                self.step()
            return [self.pieces[k] for k in range(groups)]

    early_parts = (direct_early, narrow_early, squeeze_early, project_early)
    late_parts = (direct_late, narrow_late, squeeze_late, project_late)
    norms = (direct_norm, narrow_norm, squeeze_norm, wide_norm, spread_norm, project_norm)
    norm_rows = jnp.concatenate(norms, axis=2).reshape(4, -1)
    norm_space = padded16(4 * -(-norm_rows.shape[1] // 128))
    pieces, early_points = call(
        lambda *refs: prepare_kernel(pack, *refs),
        [((groups, depth, rows), BF16), ((pack.points + norm_space, 128), BF16)],
        [clip_features, norm_rows] + [part.T for part in early_parts],
        [((pack.point_rows, pack.point_tiles * 128), F32), ((norm_space, 128), F32)],
        us=2.5,
    )
    arrived = lax.all_to_all(pieces, "ch", 0, 0)
    point_shares = Shares(early_points).all()
    flat_rows = wide_kernels.shape[1] // 128
    halves = call(split_kernel, [((flat_rows, 128), BF16)] * 2, [wide_kernels, pieces], us=4.8, idle=1)
    spread_rows = jnp.transpose(
        spread_kernels.reshape(2, SPREAD_COLUMNS, spread_kernels.shape[3]), (0, 2, 1)
    )

    def packed(use, block, parts, behind):
        size = use.kernels + (use.points if parts else 0)
        return call(
            lambda *refs: pack_kernel(use, *refs),
            [((size, 128), BF16)],
            [halves[block].reshape(-1, WIDE_COLUMNS), spread_rows[block]]
            + [part.T for part in parts] + list(behind),
            [((use.point_rows, use.point_tiles * 128), F32)],
            idle=len(behind),
            us=2.5,
        )[0]

    early_shares = Shares(ordered(packed(pack, 0, (), ()), point_shares[-1], arrived)).all()
    own_visible = lax.dynamic_slice_in_dim(visible, me * clips, clips, 0)
    fine = own_visible.astype(F32).reshape(rows, 1)
    mask = jnp.broadcast_to(fine, (rows, 128))
    cells = own_visible.reshape(clips, 2, 2, 6, 2, 6, 2).max(axis=(2, 4, 6)).astype(F32)
    coarse = jnp.broadcast_to(pad_late(cells[..., None]), (late_rows, 128))

    upstream = (upstream_direct, upstream_wide, upstream_spread, upstream_project)
    up_joined = jnp.concatenate(upstream, axis=4)
    up_parts = up_joined.reshape((groups, clips) + up_joined.shape[1:])
    up_arrived = lax.all_to_all(up_parts, "ch", 0, 0)
    ups, at = [], 0
    for part in upstream:
        width = part.shape[4]
        piece = jnp.moveaxis(up_arrived[..., at : at + width], 0, 4)
        ups.append(pad_late(piece.reshape(piece.shape[:4] + (groups * width,))))
        at += width

    pool = jnp.asarray(pool_matrix(), BF16)
    spread_back = jnp.asarray(pool_matrix().T, BF16)

    act, wt, affine, yr, pay = call(
        lambda *refs: early_first_kernel(pack, *refs),
        [
            ((rows, features), BF16), ((POINT, features), BF16), ((4, SLOTS), F32),
            ((rows, REDUCED), F32), ((devices, 8, 128), F32),
        ],
        [me_ref, arrived] + point_shares + [mask, coarse],
        [
            ((features, rows), F32), ((groups, pack.point_rows, pack.point_tiles * 128), F32),
            ((POINT, features), F32), ((groups, norm_space, 128), F32), ((8, 128), F32),
        ],
        us=8.6,
    )
    late_share = packed(late_pack, 1, late_parts, (act,))
    counts = exchange(pay)
    late_shares = Shares(ordered(late_share, counts))
    yd, yp, tile = call(
        lambda *refs: other_points_kernel(EARLY, clips, *refs),
        [((rows, DIRECT), F32), ((rows, PROJECT), F32), ((16, 128), F32)],
        [act, wt, mask],
        us=12,
    )

    def second(geo, count_row, g, y, masking, pieces, other):
        own = clips * geo.clip_rows
        padded = clips * geo.padded_rows
        return call(
            lambda *refs: second_kernel(geo, clips, pack, count_row, *refs),
            [
                ((padded, 128 * WIDE_TILES), BF16), ((padded, 128 * SPREAD_TILES), BF16),
                ((own, WIDE), F32), ((own, SPREAD), F32),
                ((3, groups, pack.wide_rows, 128 * WIDE_TILES), BF16),
                ((3, groups, pack.spread_rows, 128 * SPREAD_TILES), BF16),
                ((devices, 16, 128), F32), ((8, 128), F32),
            ],
            [me_ref, g, counts, affine, y, masking, other] + pieces,
            [((own, REDUCED), F32), ((16, 128), F32)],
            us=25 if geo is EARLY else 9,
        )

    bn, bs, yw, ys, kw, ks, pay, st_r = second(EARLY, 2, counts, yr, mask, early_shares, tile)
    g = exchange(pay)
    late_shares = late_shares.all(st_r)
    late_act, late_wt, lyr, pay, st = call(
        lambda *refs: pool_kernel(late_pack, clips, *refs),
        [
            ((late_rows, CONCAT), BF16), ((POINT, CONCAT), BF16), ((late_rows, REDUCED), F32),
            ((devices, 8, 128), F32), ((16, 128), F32),
        ],
        [me_ref, g, counts, affine, yd, yw, ys, yp, mask, pool, coarse] + late_shares,
        [
            ((rows, 384), BF16), ((rows, 384), BF16),
            ((groups, late_pack.point_rows, late_pack.point_tiles * 128), F32),
            ((POINT, CONCAT), F32), ((8, 128), F32),
        ],
        us=15,
    )
    g = exchange(pay)
    lyd, lyp, tile = call(
        lambda *refs: other_points_kernel(LATE, clips, *refs),
        [((late_rows, DIRECT), F32), ((late_rows, PROJECT), F32), ((16, 128), F32)],
        [late_act, late_wt, coarse],
        us=3.7,
    )
    lbn, lbs, lyw, lys, lkw, lks, pay, lst_r = second(LATE, 3, g, lyr, coarse, late_shares, tile)
    g = exchange(pay)
    widths = [TILE_ROW[unit][1] for unit in OUTER]
    res = call(
        lambda *refs: late_outputs_kernel(clips, *refs),
        [((late_rows, w), BF16) for w in widths]
        + [((late_rows, w), F32) for w in widths]
        + [((devices, 16, 128), F32), ((16, 128), F32)],
        [g, counts, affine, lyd, lyw, lys, lyp, coarse] + ups,
        [((16, 128), F32)],
        us=4,
    )
    outs, (hd, hw, hs, hp), (pay, lst) = res[:4], res[4:8], res[8:]
    g = exchange(pay)

    out_parts = []
    for o in outs:
        cells = o.reshape(clips, LATE.frames, LATE.height, LATE.pitch, -1)[:, :, :, : LATE.width]
        out_parts.append(cells.reshape(cells.shape[:4] + (groups, -1)))
    out_joined = jnp.moveaxis(jnp.concatenate(out_parts, axis=5), 4, 0)
    def finish(geo, g, st, st_r, hw, hs, yw, ys, masking, behind=()):
        own = clips * geo.clip_rows
        return call(
            lambda *refs: finish_kernel(geo, clips, *refs),
            [((own, WIDE), BF16), ((own, SPREAD), BF16), ((16, 128), F32)],
            [g, st, st_r, affine, hw, hs, yw, ys, masking] + list(behind),
            idle=len(behind),
            us=7 if geo is EARLY else 2.5,
        )

    def inner(geo, st_r, gw, gs, yr, kw, ks, masking, behind=()):
        own = clips * geo.clip_rows
        padded = clips * geo.padded_rows
        return call(
            lambda *refs: inner_backward_kernel(geo, clips, pack, *refs),
            [((own, REDUCED), F32), ((devices, 8, 128), F32)],
            [st_r, affine, gw, gs, yr, kw, ks, masking] + list(behind),
            [
                ((padded, 9 * WIDE), BF16), ((padded, 9 * SPREAD), BF16),
                ((3, 9 * WIDE, NARROW), BF16), ((3, 9 * SPREAD, SQUEEZE), BF16),
                ((own, REDUCED), F32), ((8, 128), F32),
            ],
            idle=len(behind),
            us=16 if geo is EARLY else 5.6,
        )

    unit = 16 * batches

    def kernel_grads(geo, size, gw, gs, bn, bs):
        return call(
            lambda *refs: kernel_grad_kernel(geo, clips, pack, *refs),
            [((groups // 2, size, 128), BF16)] * 2,
            [me_ref, gw, gs, bn, bs],
            [((3, WIDE, 128 * WIDE_TILES), F32), ((3, SPREAD, 128 * SPREAD_TILES), F32)],
            us=10 if geo is EARLY else 5,
        )

    def point_grads(use, start, size, gy, act, others=()):
        return call(
            lambda *refs: point_grad_kernel(use, start, *refs),
            [((groups // 2, size, 128), BF16)] * 2,
            [me_ref, gy, act] + list(others),
            [((POINT, use.features), F32), ((groups, use.point_rows, use.point_tiles * 128), F32)],
            us=4.5,
        )

    class Reduction:
        def __init__(self, keep, send):
            self.keep, self.bit = keep, 1
            self.got = swap(send, 1)

        def halve(self, *behind):
            while 2 * self.bit < groups:
                shape = (self.keep.shape[0] // 2,) + self.keep.shape[1:]
                self.keep, send = call(
                    halve_kernel, [(shape, BF16)] * 2, [self.keep, self.got] + list(behind),
                    idle=len(behind),
                    us=2.5,
                )
                self.bit *= 2
                self.got = swap(send, self.bit)
            return self.keep

        def add(self, *behind):
            return call(
                add_kernel, [(self.keep.shape[1:], BF16)], [self.keep, self.got] + list(behind),
                idle=len(behind),
                us=2,
            )[0]

    mb_ref = jnp.reshape(lax.axis_index("batch"), (1,)).astype(jnp.int32)

    def batch_swap(value, bit):
        return lax.ppermute(value, "batch", [(i, i ^ bit) for i in range(batches)])

    def whole_units(size):
        return -(-size // unit) * unit

    gw, gs, late_sums = finish(LATE, g, lst, lst_r, hw, hs, lyw, lys, coarse)
    hr, pay = inner(LATE, lst_r, gw, gs, lyr, lkw, lks, coarse)
    g = exchange(pay)
    late_halves = kernel_grads(LATE, pack.kernels, gw, gs, lbn, lbs)
    out_arrived = ordered(lax.all_to_all(out_joined, "ch", 0, 0))
    gy, ed, ew, es, ep, pay, late_sums_r = call(
        lambda *refs: late_input_kernel(clips, *refs),
        [((late_rows, POINT), BF16)]
        + [((rows, w), F32) for w in widths]
        + [((devices, 16, 128), F32), ((8, 128), F32)],
        [g, late_sums, lst, lst_r, affine, hr, hd, hp, lyr, lyd, lyp, coarse, late_wt, spread_back,
         st, yd, yw, ys, yp, mask, late_halves[1], out_arrived],
        [((late_rows, PROJECT), F32), ((late_rows, CONCAT), BF16), ((rows, WIDE), F32), ((16, 128), F32)],
        idle=2,
        us=15,
    )
    g = exchange(pay)
    late_size = whole_units(late_pack.kernels + late_pack.points)
    late_halves = point_grads(late_pack, late_pack.kernels, late_size, gy, late_act, late_halves)
    late_sum = Reduction(*late_halves)
    gw, gs, sums = finish(EARLY, g, st, st_r, ew, es, yw, ys, mask, late_halves[1:])
    halves = kernel_grads(EARLY, whole_units(pack.kernels), gw, gs, bn, bs)
    early_sum = Reduction(*halves)
    kept = late_sum.halve(halves[1])
    hr, pay = inner(EARLY, st_r, gw, gs, yr, kw, ks, mask, behind=(halves[1], kept))
    g = exchange(pay)
    kept = early_sum.halve(hr)
    late_piece = late_sum.keep.shape[1] // batches
    late_keep, late_send = call(
        scatter_halves_kernel,
        [((batches // 2, late_piece, 128), BF16)] * 2,
        [mb_ref, late_sum.keep, late_sum.got, hr],
        [(late_sum.keep.shape[1:], F32)],
        us=3,
        idle=1,
    )

    class BatchHalves(Reduction):
        def __init__(self, keep, send):
            self.keep, self.bit = keep, 1
            self.got = batch_swap(send, 1)

        def step(self, *behind):
            shape = (self.keep.shape[0] // 2,) + self.keep.shape[1:]
            self.keep, send = call(
                halve_kernel, [(shape, BF16)] * 2, [self.keep, self.got] + list(behind),
                idle=len(behind), us=1.5,
            )
            self.bit *= 2
            self.got = batch_swap(send, self.bit)
            return self.keep

    late_sum = BatchHalves(late_keep, late_send)
    gy, *x_parts, sums_r = call(
        lambda *refs: early_input_kernel(pack, clips, *refs),
        [((rows, POINT), BF16)] + [((depth, rows), BF16)] * groups + [((8, 128), F32)],
        [me_ref, g, sums, st, st_r, affine, hr, ed, ep, yr, yd, yp, mask, wt, kept, late_keep],
        [((rows, PROJECT), F32), ((groups, depth, rows), BF16)],
        idle=2,
        us=8.5,
    )
    x_parts = [x_parts[0]] + [swap(x_parts[k], k) for k in range(1, groups)]
    point_halves = point_grads(pack, 0, whole_units(pack.points), gy, act)
    point_sum = Reduction(*point_halves)
    kept = late_sum.step(point_halves[1])
    own = early_sum.add(point_halves[1], kept)
    parts = lax.all_to_all(own.reshape(batches, -1, 128), "batch", 0, 0)
    kept = point_sum.halve(own)
    late_kept = late_sum.step(kept)
    while 2 * late_sum.bit < batches:
        late_kept = late_sum.step()
    (feature_grad,) = call(
        lambda *refs: feature_kernel(pack, *refs),
        [((depth, groups * rows), F32)],
        [me_ref] + x_parts + [own, late_kept],
        [((groups, depth, rows), BF16)],
        idle=2,
        us=2,
    )
    points_size = kept.shape[1] // batches
    pieces = call(
        scatter_kernel,
        [((points_size, 128), BF16)] * batches,
        [mb_ref, point_sum.keep, point_sum.got],
        [(kept.shape[1:], F32)],
        us=1.5,
    )
    pieces = [pieces[0]] + [batch_swap(pieces[k], k) for k in range(1, batches)]
    late_own = late_sum.add(pieces[0])
    late_pieces, bit = {0: late_own}, batches // 2
    while bit:
        for k in list(late_pieces):
            late_pieces[k | bit] = batch_swap(late_pieces[k], bit)
        bit //= 2
    late_pieces = [late_pieces[k] for k in range(batches)]
    kernels_size = parts.shape[1]
    (parts,) = call(
        total_kernel,
        [((batches, kernels_size + points_size, 128), BF16)],
        [parts] + list(pieces) + [feature_grad],
        us=2,
        idle=1,
    )
    early_total = lax.all_to_all(parts, "batch", 0, 0)
    out_arrived = out_arrived.reshape((held_clips,) + out_arrived.shape[2:])
    outputs, at = [], 0
    for part in upstream:
        outputs.append(out_arrived[..., at : at + part.shape[4]])
        at += part.shape[4]

    late_wide, late_spread, *late_grads = call(
        lambda *refs: late_gradients_kernel(late_pack, batches, *refs),
        [((pack.wide, WIDE_COLUMNS), F32), ((SPREAD_COLUMNS, pack.spread), F32)]
        + [(part.shape[::-1], F32) for part in late_parts],
        [mb_ref] + late_pieces,
        [((batches, late_piece, 128), BF16), ((pack.spread, SPREAD_COLUMNS), F32)],
        us=4,
    )
    wide_grad, early_spread, *early_grads = call(
        lambda *refs: early_gradients_kernel(pack, kernels_size, *refs),
        [(wide_kernels.shape, F32), ((SPREAD_COLUMNS, pack.spread), F32)]
        + [(part.shape[::-1], F32) for part in early_parts],
        [early_total, late_wide],
        [
            ((batches * kernels_size, 128), BF16), ((batches * points_size, 128), BF16),
            ((pack.wide, WIDE_COLUMNS), F32), ((pack.spread, SPREAD_COLUMNS), F32),
        ],
        us=8,
    )
    early_grads = [part.T for part in early_grads]
    late_grads = [part.T for part in late_grads]
    spread_grad = jnp.stack(
        [part.reshape(spread_kernels.shape[1:]) for part in (early_spread, late_spread)]
    )

    def outer_pair(tile, unit):
        first, width = TILE_ROW[unit]
        return jnp.stack([tile[k : k + 3].reshape(-1)[:width] for k in (first, first + 8)])

    def inner_pair(tile, low, high):
        return jnp.stack([tile[k : k + 2].reshape(-1)[low:high] for k in (0, 4)])

    def own_part(early_pair, late_pair):
        both = jnp.stack([early_pair, late_pair])
        size = both.shape[2] // groups
        return lax.dynamic_slice_in_dim(both, me * size, size, 2)

    norm_grads = [
        own_part(outer_pair(sums, "d"), outer_pair(late_sums, "d")),
        own_part(inner_pair(sums_r, 0, NARROW), inner_pair(late_sums_r, 0, NARROW)),
        own_part(outer_pair(sums, "w"), outer_pair(late_sums, "w")),
        own_part(inner_pair(sums_r, NARROW, REDUCED), inner_pair(late_sums_r, NARROW, REDUCED)),
        own_part(outer_pair(sums, "s"), outer_pair(late_sums, "s")),
        own_part(outer_pair(sums, "p"), outer_pair(late_sums, "p")),
    ]
    return tuple(outputs) + (feature_grad,) + tuple(early_grads) + tuple(late_grads) + (
        wide_grad, spread_grad,
    ) + tuple(norm_grads)


def solution(mesh):
    columns = P(None, "ch")
    norm = P(None, None, "ch")
    clips = P("batch", None, None, None, "ch")
    kernels = P(None, None, None, "ch")
    return jax.shard_map(
        shards,
        mesh=mesh,
        in_specs=(P("ch", "batch"), P("batch", None, None, None)) + (columns,) * 9 + (kernels,)
        + (norm,) * 6 + (clips,) * 4,
        out_specs=(clips,) * 4 + (P("ch", "batch"),) + (columns,) * 9 + (kernels,) + (norm,) * 6,
        check_vma=False,
    )
```

```python
import jax
import jax.numpy as jnp
import numpy as np
from jax import lax
from jax.experimental import pallas as pl
from jax.experimental.pallas import tpu as pltpu
from jax.sharding import PartitionSpec as P

F32 = jnp.float32
BF16 = jnp.bfloat16
EPSILON = 0.001
FLOPS_A_US = 1.1e9
BOTH = ("batch", "ch")
DIRECT, NARROW, WIDE, SQUEEZE, SPREAD, PROJECT = 256, 160, 320, 32, 128, 128
REDUCED = NARROW + SQUEEZE
POINT = DIRECT + REDUCED + PROJECT
CONCAT = DIRECT + WIDE + SPREAD + PROJECT
WIDE_COLUMNS = 27 * NARROW
SPREAD_COLUMNS = 27 * SQUEEZE
POINT_WIDTHS = (DIRECT, NARROW, SQUEEZE, PROJECT)
SLOT = {"d": (0, DIRECT), "r": (256, REDUCED), "w": (512, WIDE), "s": (896, SPREAD), "p": (1024, PROJECT)}
SLOTS = 1152
NORM_ORDER = ((0, DIRECT), (256, NARROW), (256 + NARROW, SQUEEZE), (512, WIDE), (896, SPREAD), (1024, PROJECT))
TILE_ROW = {"d": (0, DIRECT), "w": (2, WIDE), "s": (5, SPREAD), "p": (6, PROJECT)}
OUTER = ("d", "w", "s", "p")
CHUNK = 96


class Geometry:
    def __init__(self, frames, height, width, pitch, block):
        self.frames, self.height, self.width, self.pitch = frames, height, width, pitch
        self.block = block
        self.frame_rows = height * pitch
        self.clip_rows = frames * self.frame_rows
        self.padded_rows = (frames + 2) * self.frame_rows
        self.dense = pitch == width


EARLY = Geometry(4, 12, 12, 12, 0)
LATE = Geometry(2, 6, 6, 8, 1)


def nt(a, b):
    return lax.dot_general(a, b, (((1,), (1,)), ((), ())), preferred_element_type=F32)


def nn(a, b):
    return lax.dot_general(a, b, (((1,), (0,)), ((), ())), preferred_element_type=F32)


def tn(a, b):
    return lax.dot_general(a, b, (((0,), (0,)), ((), ())), preferred_element_type=F32)


def call(kernel, outs, ins, scratch=(), us=0, idle=0):
    moved = sum(int(np.prod(s)) * jnp.dtype(d).itemsize for s, d in outs)
    moved += sum(int(np.prod(x.shape)) * x.dtype.itemsize for x in ins[: len(ins) - idle])

    def spec(k, x):
        if k >= len(ins) - idle:
            return pl.BlockSpec(memory_space=pl.ANY)
        return pl.BlockSpec(memory_space=pltpu.SMEM if x.ndim == 1 else pltpu.VMEM)

    def body(*refs):
        kept = len(ins) - idle
        kernel(*refs[:kept], *refs[len(ins) :])

    return pl.pallas_call(
        body,
        out_shape=[jax.ShapeDtypeStruct(s, d) for s, d in outs],
        in_specs=[spec(k, x) for k, x in enumerate(ins)],
        out_specs=[pl.BlockSpec(memory_space=pltpu.VMEM)] * len(outs),
        scratch_shapes=[pltpu.VMEM(s, d) for s, d in scratch],
        compiler_params=pltpu.CompilerParams(vmem_limit_bytes=56 * 2**20),
        cost_estimate=pl.CostEstimate(
            flops=int(us * FLOPS_A_US) or 10 * moved, bytes_accessed=moved, transcendentals=0
        ),
    )(*ins)


def ordered(value, *behind):
    anywhere = pl.BlockSpec(memory_space=pl.ANY)
    return pl.pallas_call(
        lambda *refs: None,
        out_shape=jax.ShapeDtypeStruct(value.shape, value.dtype),
        in_specs=[anywhere] * (1 + len(behind)),
        out_specs=anywhere,
        input_output_aliases={0: 0},
    )(value, *behind)


def each_chunk(rows, body, init=0, chunk=CHUNK):
    return lax.fori_loop(
        0, rows // chunk, lambda i, carry: body(pl.multiple_of(i * chunk, chunk), carry), init
    )


def wide_mask(m_ref, at, width):
    part = m_ref[at, :]
    if width <= 128:
        return part[:, :width]
    return jnp.concatenate([part] * -(-width // 128), axis=1)[:, :width]


def row(tile, first, width):
    pieces = [
        tile[first + i : first + i + 1, : min(128, width - 128 * i)] for i in range(-(-width // 128))
    ]
    return pieces[0] if len(pieces) == 1 else jnp.concatenate(pieces, axis=1)


def put_row(ref, first, vector):
    width = vector.shape[1]
    for i in range(-(-width // 128)):
        part = vector[:, 128 * i : min(128 * (i + 1), width)]
        ref[first + i : first + i + 1, : part.shape[1]] = part


def affine_of(aff_ref, block, unit):
    start, width = SLOT[unit]
    return (
        aff_ref[2 * block : 2 * block + 1, start : start + width],
        aff_ref[2 * block + 1 : 2 * block + 2, start : start + width],
    )


def fold8(value):
    total = value[0:8]
    for i in range(1, value.shape[0] // 8):
        total = total + value[8 * i : 8 * i + 8]
    return total


def local_moments(y_ref, m_ref, rows, count):
    width = y_ref.shape[1]

    def first(r, acc):
        at = pl.ds(r, CHUNK)
        return acc + fold8(y_ref[at, :] * wide_mask(m_ref, at, width))

    total = each_chunk(rows, first, jnp.zeros((8, width), F32))
    mean = jnp.sum(total, axis=0, keepdims=True) / count

    def second(r, acc):
        at = pl.ds(r, CHUNK)
        centred = (y_ref[at, :] - mean) * wide_mask(m_ref, at, width)
        return acc + fold8(centred * centred)

    spread = each_chunk(rows, second, jnp.zeros((8, width), F32))
    return mean, jnp.sum(spread, axis=0, keepdims=True)


def combine_moments(payload, counts, first, second, size):
    means = payload[:, first : first + size, :]
    total = jnp.sum(counts, axis=0)
    mean = jnp.sum(means * counts, axis=0) / total
    offset = means - mean[None]
    spread = jnp.sum(payload[:, second : second + size, :] + counts * offset * offset, axis=0)
    return mean, lax.rsqrt(spread / total + EPSILON)


def send_tile(pay_ref, tile_ref):
    pay_ref[...] = jnp.broadcast_to(tile_ref[...][None], pay_ref.shape)


def shifted(value, offset):
    if offset == 0:
        return value
    return pltpu.roll(value, (-offset) % value.shape[0], 0)


def cell_index(geo, shape):
    r = lax.broadcasted_iota(jnp.int32, shape, 0).astype(F32)
    line = jnp.floor((r + 0.5) * (1.0 / geo.pitch))
    column = r - geo.pitch * line
    frame = jnp.floor((line + 0.5) * (1.0 / geo.height))
    return line - geo.height * frame, column


def edge_masks(geo, width):
    line, column = cell_index(geo, (geo.clip_rows, width))
    return (
        {e: (line + e > -0.5) & (line + e < geo.height - 0.5) for e in (-1, 1)},
        {e: (column + e > -0.5) & (column + e < geo.width - 0.5) for e in (-1, 1)},
    )


def gather_cells(geo, value, masks, sign, store):
    lines, columns = masks
    for b, dw in enumerate((-1, 0, 1)):
        moved = shifted(value, sign * dw)
        if dw and geo.dense:
            moved = jnp.where(columns[sign * dw], moved, 0.0)
        for a, dh in enumerate((-1, 0, 1)):
            placed = shifted(moved, sign * dh * geo.pitch)
            if dh:
                placed = jnp.where(lines[sign * dh], placed, 0.0)
            store(3 * a + b, placed)


def frame_shift(geo, value, offset):
    if offset == 0:
        return value
    size = geo.frame_rows
    blank = jnp.zeros((size, value.shape[1]), value.dtype)
    if offset > 0:
        return jnp.concatenate([value[size:], blank], axis=0)
    return jnp.concatenate([blank, value[:-size]], axis=0)


def mean_cells(geo, value, masks):
    lines, columns = masks
    total = value
    for e in (-1, 1):
        moved = shifted(value, e)
        total = total + (jnp.where(columns[e], moved, 0.0) if geo.dense else moved)
    again = total
    for e in (-1, 1):
        again = again + jnp.where(lines[e], shifted(total, e * geo.pitch), 0.0)
    return (again + frame_shift(geo, again, 1) + frame_shift(geo, again, -1)) / 27.0


def clear_edges(geo, ref, clip):
    base = clip * geo.padded_rows
    size = geo.frame_rows
    blank = jnp.zeros((size, ref.shape[1]), ref.dtype)
    ref[base : base + size, :] = blank
    ref[base + geo.padded_rows - size : base + geo.padded_rows, :] = blank


def padded16(size):
    return -(-size // 16) * 16


class Packing:
    def __init__(self, groups, features):
        self.groups = groups
        self.wide, self.spread, self.point = WIDE // groups, SPREAD // groups, POINT // groups
        self.wide_rows = padded16(self.wide)
        self.spread_rows = padded16(self.spread)
        self.point_rows = padded16(self.point)
        self.kernels = 3 * WIDE_TILES * self.wide_rows + 3 * SPREAD_TILES * self.spread_rows
        self.features = features
        self.point_tiles = -(-features // 128)
        self.points = self.point_tiles * self.point_rows

    def kernel_tiles(self):
        at = 0
        for own, size, tiles, columns, wide in (
            (self.wide, self.wide_rows, WIDE_TILES, 9 * NARROW, True),
            (self.spread, self.spread_rows, SPREAD_TILES, 9 * SQUEEZE, False),
        ):
            for t in range(3):
                for u in range(tiles):
                    yield at, own, wide, t, u, min(128, columns - 128 * u)
                    at += size

    def point_blocks(self, start):
        for u in range(self.point_tiles):
            yield start + u * self.point_rows, u, min(128, self.features - 128 * u)

    def point_parts(self):
        at = start = 0
        for width in POINT_WIDTHS:
            own = width // self.groups
            yield at, start, own
            at += own
            start += width


WIDE_TILES = -(-9 * NARROW // 128)
SPREAD_TILES = -(-9 * SQUEEZE // 128)


def fit_tile(value):
    width = value.shape[1]
    if width == 128:
        return value
    return jnp.concatenate([value, jnp.zeros((value.shape[0], 128 - width), value.dtype)], axis=1)


def pack_points(pack, part_refs, o_ref, start, scratch):
    for (at, _, own), ref in zip(pack.point_parts(), part_refs):
        scratch[at : at + own, : pack.features] = ref[...].astype(F32)
    for at, u, width in pack.point_blocks(start):
        o_ref[at : at + pack.point, :] = fit_tile(
            scratch[: pack.point, 128 * u : 128 * u + width].astype(BF16)
        )


def unpack_points(pack, me, piece_refs, start, raw, scratch, wt_ref):
    for k, ref in enumerate(piece_refs):
        for at, u, width in pack.point_blocks(start):
            raw[me ^ k, : pack.point, 128 * u : 128 * u + width] = ref[at : at + pack.point, :width].astype(F32)
    for s in range(pack.groups):
        for at, begin, own in pack.point_parts():
            scratch[begin + s * own : begin + (s + 1) * own, :] = raw[s, at : at + own, : pack.features]
    wt_ref[...] = scratch[...].astype(BF16)


def unpack_kernels(pack, me, piece_refs, kw_ref, ks_ref):
    for k, ref in enumerate(piece_refs):
        for at, own, wide, t, u, _ in pack.kernel_tiles():
            target = kw_ref if wide else ks_ref
            size = target.shape[2]
            target[t, me ^ k, :, 128 * u : 128 * u + 128] = ref[at : at + size, :]


def whole_kernel(ref, t, own):
    if own == ref.shape[2]:
        return ref[t].reshape(ref.shape[1] * own, ref.shape[3])
    parts = [ref[t, s].astype(F32)[:own] for s in range(ref.shape[1])]
    return jnp.concatenate(parts, axis=0).astype(BF16)


def prepare_kernel(pack, x_ref, norm_ref, p0, p1, p2, p3, o_ref, b_ref, scratch, rows):
    width = o_ref.shape[2]
    for s in range(pack.groups):
        o_ref[s] = x_ref[:, s * width : (s + 1) * width]
    pack_points(pack, (p0, p1, p2, p3), b_ref, 0, scratch)
    rows[...] = jnp.zeros_like(rows)
    for u in range(-(-norm_ref.shape[1] // 128)):
        part = norm_ref[:, 128 * u : 128 * (u + 1)].astype(F32)
        rows[4 * u : 4 * u + 4, : part.shape[1]] = part
    b_ref[pack.points :, :] = rows[...].astype(BF16)


def split_kernel(x_ref, a_ref, b_ref):
    tiles = x_ref.shape[1] // 128

    def move(first, count):
        value = x_ref[:, pl.ds(128 * first, 128 * count)].astype(F32)
        for r, ref in ((0, a_ref), (1, b_ref)):
            parts = [value[r : r + 1, 128 * j : 128 * (j + 1)] for j in range(count)]
            ref[pl.ds(first, count), :] = jnp.concatenate(parts, axis=0).astype(BF16)

    def step(i, carry):
        move(pl.multiple_of(16 * i, 16), 16)
        return carry

    lax.fori_loop(0, tiles // 16, step, 0)
    if tiles % 16:
        move(tiles // 16 * 16, tiles % 16)


def pack_kernel(pack, w_ref, s_ref, *refs):
    *part_refs, o_ref, scratch = refs
    for at, own, wide, t, u, width in pack.kernel_tiles():
        source, columns = (w_ref, 9 * NARROW) if wide else (s_ref, 9 * SQUEEZE)
        start = columns * t + 128 * u
        o_ref[at : at + own, :] = fit_tile(source[:, start : start + width])
    if part_refs:
        pack_points(pack, part_refs, o_ref, pack.kernels, scratch)


def early_first_kernel(
    pack, me_ref, x_ref, *refs
):
    groups = pack.groups
    piece_refs = refs[:groups]
    m_ref, mc_ref, a_ref, wt_ref, aff_ref, y_ref, pay_ref, xs, raw, ws, norm_raw, tile = refs[groups:]
    me = me_ref[0]
    depth, rows = x_ref.shape[1], x_ref.shape[2]
    for s in range(groups):
        xs[s * depth : (s + 1) * depth, :] = x_ref[s].astype(F32)
    for j in range(0, rows, 128):
        size = min(128, rows - j)
        turned = jnp.transpose(xs[:, j : j + size])
        a_ref[j : j + size, :] = (turned * wide_mask(m_ref, slice(j, j + size), turned.shape[1])).astype(BF16)
    unpack_points(pack, me, piece_refs, 0, raw, ws, wt_ref)
    for k, ref in enumerate(piece_refs):
        norm_raw[me ^ k] = ref[pack.points :, :].astype(F32)
    at = 0
    for slot, whole in NORM_ORDER:
        own = whole // groups
        for s in range(groups):
            left, u = at % 128, at // 128
            first = min(own, 128 - left)
            to = slot + s * own
            aff_ref[:, to : to + first] = norm_raw[s, 4 * u : 4 * u + 4, left : left + first]
            if first < own:
                aff_ref[:, to + first : to + own] = norm_raw[s, 4 * u + 4 : 4 * u + 8, : own - first]
        at += own
    y_ref[...] = nt(a_ref[...], wt_ref[DIRECT : DIRECT + REDUCED, :])
    tile[...] = jnp.zeros_like(tile)
    count = jnp.sum(m_ref[...], axis=0, keepdims=True)
    coarse = jnp.sum(mc_ref[...], axis=0, keepdims=True)
    mean, spread = local_moments(y_ref, m_ref, rows, count[:, 0:1])
    put_row(tile, 0, mean)
    put_row(tile, 2, count)
    put_row(tile, 3, coarse)
    put_row(tile, 4, spread)
    send_tile(pay_ref, tile)


def other_points_kernel(geo, clips, a_ref, wt_ref, m_ref, yd_ref, yp_ref, tile):
    yd_ref[...] = nt(a_ref[...], wt_ref[:DIRECT, :])
    projected = nt(a_ref[...], wt_ref[DIRECT + REDUCED :, :])
    masks = edge_masks(geo, PROJECT)
    for c in range(clips):
        rows = slice(c * geo.clip_rows, (c + 1) * geo.clip_rows)
        yp_ref[rows, :] = mean_cells(geo, projected[rows], masks)
    tile[...] = jnp.zeros_like(tile)
    count = jnp.sum(m_ref[...], axis=0, keepdims=True)[:, 0:1]
    for unit, ref in (("d", yd_ref), ("p", yp_ref)):
        mean, spread = local_moments(ref, m_ref, clips * geo.clip_rows, count)
        put_row(tile, TILE_ROW[unit][0], mean)
        put_row(tile, 8 + TILE_ROW[unit][0], spread)


def second_kernel(
    geo, clips, pack, count_row, me_ref, g_ref, counts_ref, aff_ref, y_ref, m_ref, pd_ref, *refs
):
    piece_refs = refs[: pack.groups]
    (bn_ref, bs_ref, yw_ref, ys_ref, kw_ref, ks_ref, pay_ref, st_ref, us, tile) = refs[pack.groups :]
    unpack_kernels(pack, me_ref[0], piece_refs, kw_ref, ks_ref)
    rows = clips * geo.clip_rows
    counts = counts_ref[:, count_row : count_row + 1, :]
    means, rstds = combine_moments(g_ref[...], counts, 0, 4, 2)
    st_ref[...] = jnp.zeros_like(st_ref)
    st_ref[0:2, :] = means
    st_ref[2:3, :] = jnp.sum(counts, axis=0)
    st_ref[4:6, :] = rstds
    mean, rstd = row(means, 0, REDUCED), row(rstds, 0, REDUCED)
    scale, shift = affine_of(aff_ref, geo.block, "r")

    def activate(r, carry):
        at = pl.ds(r, CHUNK)
        h = scale * ((y_ref[at, :] - mean) * rstd) + shift
        us[at, :] = h * jax.nn.sigmoid(h) * wide_mask(m_ref, at, REDUCED)
        return carry

    each_chunk(rows, activate)
    masks = edge_masks(geo, REDUCED)
    size = geo.frame_rows
    for c in range(clips):
        base = c * geo.padded_rows
        clear_edges(geo, bn_ref, c)
        clear_edges(geo, bs_ref, c)
        inside = slice(base + size, base + size + geo.clip_rows)
        for ref, used in ((bn_ref, 9 * NARROW), (bs_ref, 9 * SQUEEZE)):
            ref[inside, used:] = jnp.zeros((geo.clip_rows, ref.shape[1] - used), BF16)

        def store(j, placed):
            at = slice(base + size, base + size + geo.clip_rows)
            bn_ref[at, NARROW * j : NARROW * (j + 1)] = placed[:, :NARROW].astype(BF16)
            bs_ref[at, SQUEEZE * j : SQUEEZE * (j + 1)] = placed[:, NARROW:].astype(BF16)

        gather_cells(geo, us[c * geo.clip_rows : (c + 1) * geo.clip_rows, :], masks, 1, store)
    for c in range(clips):
        base = c * geo.padded_rows
        out = slice(c * geo.clip_rows, (c + 1) * geo.clip_rows)
        for b_ref, k_ref, o_ref, own in (
            (bn_ref, kw_ref, yw_ref, pack.wide), (bs_ref, ks_ref, ys_ref, pack.spread)
        ):
            total = None
            for t in range(3):
                term = nt(
                    b_ref[base + size * t : base + size * t + geo.clip_rows, :],
                    whole_kernel(k_ref, t, own),
                )
                total = term if total is None else total + term
            o_ref[out, :] = total
    tile[...] = pd_ref[...]
    own = jnp.sum(m_ref[...], axis=0, keepdims=True)[:, 0:1]
    for unit, ref in (("w", yw_ref), ("s", ys_ref)):
        mean, spread = local_moments(ref, m_ref, rows, own)
        put_row(tile, TILE_ROW[unit][0], mean)
        put_row(tile, 8 + TILE_ROW[unit][0], spread)
    send_tile(pay_ref, tile)


def outer_stats(st, unit):
    first, width = TILE_ROW[unit]
    return row(st, first, width), row(st, 8 + first, width)


def pool_kernel(
    pack, clips, me_ref, g_ref, counts_ref, aff_ref, yd_ref, yw_ref, ys_ref, yp_ref, m_ref, pool_ref,
    mc_ref, *refs
):
    piece_refs = refs[: pack.groups]
    a_ref, wt_ref, y_ref, pay_ref, st_ref, high, low, raw, ws, tile = refs[pack.groups :]
    means, rstds = combine_moments(g_ref[...], counts_ref[:, 2:3, :], 0, 8, 8)
    st_ref[0:8, :] = means
    st_ref[8:16, :] = rstds
    st = st_ref[...]
    at_column = 0
    for unit, ref in zip(OUTER, (yd_ref, yw_ref, ys_ref, yp_ref)):
        width = TILE_ROW[unit][1]
        mean, rstd = outer_stats(st, unit)
        scale, shift = affine_of(aff_ref, 0, unit)

        def activate(r, carry):
            at = pl.ds(r, CHUNK)
            h = scale * ((ref[at, :] - mean) * rstd) + shift
            u = h * jax.nn.sigmoid(h) * wide_mask(m_ref, at, width)
            top = u.astype(BF16)
            high[at, :width] = top
            low[at, :width] = (u - top.astype(F32)).astype(BF16)
            return carry

        each_chunk(clips * EARLY.clip_rows, activate)
        for c in range(clips):
            rows = slice(c * EARLY.clip_rows, (c + 1) * EARLY.clip_rows)
            pooled = nn(pool_ref[...], high[rows, :width]) + nn(pool_ref[...], low[rows, :width])
            out = slice(c * LATE.clip_rows, (c + 1) * LATE.clip_rows)
            a_ref[out, at_column : at_column + width] = pooled.astype(BF16)
        at_column += width
    unpack_points(pack, me_ref[0], piece_refs, pack.kernels, raw, ws, wt_ref)
    y_ref[...] = nt(a_ref[...], wt_ref[DIRECT : DIRECT + REDUCED, :])
    tile[...] = jnp.zeros_like(tile)
    own = jnp.sum(mc_ref[...], axis=0, keepdims=True)
    mean, spread = local_moments(y_ref, mc_ref, clips * LATE.clip_rows, own[:, 0:1])
    put_row(tile, 0, mean)
    put_row(tile, 4, spread)
    send_tile(pay_ref, tile)


def local_backward(y_ref, dz_of, m_ref, mean, rstd, scale, shift, dh_ref, out_ref, rows):
    width = y_ref.shape[1]

    def body(r, carry):
        at = pl.ds(r, CHUNK)
        masking = wide_mask(m_ref, at, width)
        xhat = (y_ref[at, :] - mean) * rstd
        h = scale * xhat + shift
        gate = jax.nn.sigmoid(h)
        if out_ref is not None:
            out_ref[at, :] = (h * gate * masking).astype(out_ref.dtype)
        dh = dz_of(at) * masking * gate * (1.0 + h * (1.0 - gate))
        dh_ref[at, :] = dh
        return carry[0] + fold8(dh * xhat), carry[1] + fold8(dh)

    blank = jnp.zeros((8, width), F32)
    first, second = each_chunk(rows, body, (blank, blank))
    return jnp.sum(first, axis=0, keepdims=True), jnp.sum(second, axis=0, keepdims=True)


def late_outputs_kernel(
    clips, g_ref, counts_ref, aff_ref, yd_ref, yw_ref, ys_ref, yp_ref, mc_ref,
    ud_ref, uw_ref, us_ref, up_ref,
    od_ref, ow_ref, os_ref, op_ref, dd_ref, dw_ref, ds_ref, dp_ref, pay_ref, st_ref, tile
):
    means, rstds = combine_moments(g_ref[...], counts_ref[:, 3:4, :], 0, 8, 8)
    st_ref[0:8, :] = means
    st_ref[8:16, :] = rstds
    st = st_ref[...]
    tile[...] = jnp.zeros_like(tile)
    for unit, y_ref, up, o_ref, dh_ref in zip(
        OUTER,
        (yd_ref, yw_ref, ys_ref, yp_ref),
        (ud_ref, uw_ref, us_ref, up_ref),
        (od_ref, ow_ref, os_ref, op_ref),
        (dd_ref, dw_ref, ds_ref, dp_ref),
    ):
        mean, rstd = outer_stats(st, unit)
        scale, shift = affine_of(aff_ref, 1, unit)
        sums = local_backward(
            y_ref, lambda at: up[at, :].astype(F32), m_ref=mc_ref, mean=mean, rstd=rstd,
            scale=scale, shift=shift, dh_ref=dh_ref, out_ref=o_ref, rows=clips * LATE.clip_rows,
        )
        put_row(tile, TILE_ROW[unit][0], sums[0])
        put_row(tile, 8 + TILE_ROW[unit][0], sums[1])
    send_tile(pay_ref, tile)


def finish_rows(dh, y, masking, mean, rstd, scale, scale_sum, shift_sum, count):
    xhat = (y - mean) * rstd
    return scale * rstd * (dh - (shift_sum + xhat * scale_sum) / count) * masking


def finish_kernel(
    geo, clips, g_ref, st_ref, str_ref, aff_ref, dw_ref, ds_ref, yw_ref, ys_ref, m_ref,
    gw_ref, gs_ref, sums_ref
):
    rows = clips * geo.clip_rows
    sums_ref[...] = jnp.sum(g_ref[...], axis=0)
    sums, st = sums_ref[...], st_ref[...]
    count = str_ref[2:3, 0:1]
    for unit, d_ref, y_ref, o_ref in (("w", dw_ref, yw_ref, gw_ref), ("s", ds_ref, ys_ref, gs_ref)):
        first, width = TILE_ROW[unit]
        mean, rstd = outer_stats(st, unit)
        scale, _ = affine_of(aff_ref, geo.block, unit)
        scale_sum, shift_sum = row(sums, first, width), row(sums, 8 + first, width)

        def finish(r, carry):
            at = pl.ds(r, CHUNK)
            dy = finish_rows(
                d_ref[at, :], y_ref[at, :], wide_mask(m_ref, at, width), mean, rstd, scale, scale_sum,
                shift_sum, count,
            )
            o_ref[at, :] = dy.astype(BF16)
            return carry

        each_chunk(rows, finish)


def inner_backward_kernel(
    geo, clips, pack, str_ref, aff_ref, gw_ref, gs_ref, yr_ref, kw_ref, ks_ref, m_ref,
    dh_ref, pay_ref, pad_w, pad_s, kt_w, kt_s, dz, tile
):
    rows = clips * geo.clip_rows
    size = geo.frame_rows
    st_r = str_ref[...]
    for width, g_ref, pad in ((WIDE, gw_ref, pad_w), (SPREAD, gs_ref, pad_s)):
        masks = edge_masks(geo, width)
        for c in range(clips):
            base = c * geo.padded_rows
            clear_edges(geo, pad, c)

            def store(j, placed):
                at = slice(base + size, base + size + geo.clip_rows)
                pad[at, width * j : width * (j + 1)] = placed.astype(BF16)

            value = g_ref[c * geo.clip_rows : (c + 1) * geo.clip_rows, :].astype(F32)
            gather_cells(geo, value, masks, -1, store)
    for k_ref, kt, own, width, depth in (
        (kw_ref, kt_w, pack.wide, WIDE, NARROW), (ks_ref, kt_s, pack.spread, SPREAD, SQUEEZE)
    ):
        for t in range(3):
            whole = whole_kernel(k_ref, t, own)
            for j in range(9):
                kt[t, width * j : width * (j + 1), :] = whole[:, depth * j : depth * (j + 1)]
    for pad, kt, depth, start in ((pad_w, kt_w, NARROW, 0), (pad_s, kt_s, SQUEEZE, NARROW)):
        for c in range(clips):
            base = c * geo.padded_rows
            total = None
            for t in range(3):
                at = base + size * (2 - t)
                term = nn(pad[at : at + geo.clip_rows, :], kt[t])
                total = term if total is None else total + term
            dz[c * geo.clip_rows : (c + 1) * geo.clip_rows, start : start + depth] = total
    scale, shift = affine_of(aff_ref, geo.block, "r")
    first, second = local_backward(
        yr_ref, lambda at: dz[at, :], m_ref=m_ref, mean=row(st_r, 0, REDUCED),
        rstd=row(st_r, 4, REDUCED), scale=scale, shift=shift, dh_ref=dh_ref, out_ref=None, rows=rows,
    )
    tile[...] = jnp.zeros_like(tile)
    put_row(tile, 0, first)
    put_row(tile, 4, second)
    send_tile(pay_ref, tile)


def kernel_grad_kernel(
    geo, clips, pack, halves, me_ref, gw_ref, gs_ref, bn_ref, bs_ref, *refs
):
    send_ref, grad_w, grad_s = refs[-3:]
    if halves:
        keep_ref = refs[-4]
        for source, target in zip(refs[:-4], (keep_ref, send_ref)):
            target[:, pack.kernels : pack.kernels + source.shape[1], :] = source[...]
    size = geo.frame_rows
    for g_ref, b_ref, grad in ((gw_ref, bn_ref, grad_w), (gs_ref, bs_ref, grad_s)):
        for t in range(3):
            total = None
            for c in range(clips):
                at = c * geo.padded_rows + size * t
                term = tn(
                    g_ref[c * geo.clip_rows : (c + 1) * geo.clip_rows, :],
                    b_ref[at : at + geo.clip_rows, :],
                )
                total = term if total is None else total + term
            grad[t] = total
    me = me_ref[0]
    for k in range(pack.groups):
        target, place = ((keep_ref, send_ref)[k % 2], k // 2) if halves else (send_ref, me ^ k)
        for at, own, wide, t, u, _ in pack.kernel_tiles():
            source = grad_w if wide else grad_s
            first = pl.multiple_of((me ^ k) * own, 8)
            part = source[t, pl.ds(first, own), 128 * u : 128 * u + 128]
            target[place, at : at + own, :] = part.astype(BF16)


def point_grad_kernel(pack, me_ref, gy_ref, a_ref, keep_ref, send_ref, whole, shares):
    whole[...] = tn(gy_ref[...], a_ref[...])
    for s in range(pack.groups):
        for at, begin, own in pack.point_parts():
            shares[s, at : at + own, : pack.features] = whole[begin + s * own : begin + (s + 1) * own, :]
    me = me_ref[0]
    for k in range(pack.groups):
        target = (keep_ref, send_ref)[k % 2]
        for at, u, width in pack.point_blocks(0):
            target[k // 2, at : at + pack.point, :] = shares[
                me ^ k, : pack.point, 128 * u : 128 * u + 128
            ].astype(BF16)


def halve_kernel(keep_ref, got_ref, even_ref, odd_ref):
    for q in range(keep_ref.shape[0]):
        target = (even_ref, odd_ref)[q % 2]
        target[q // 2] = (keep_ref[q].astype(F32) + got_ref[q].astype(F32)).astype(BF16)


def add_kernel(keep_ref, got_ref, o_ref):
    o_ref[...] = (keep_ref[0].astype(F32) + got_ref[0].astype(F32)).astype(BF16)


def scatter_halves_kernel(mb_ref, x_ref, even_ref, odd_ref, held):
    held[...] = x_ref[...].astype(F32)
    size = even_ref.shape[1]
    for k in range(2 * even_ref.shape[0]):
        first = pl.multiple_of((mb_ref[0] ^ k) * size, 8)
        (even_ref, odd_ref)[k % 2][k // 2] = held[pl.ds(first, size), :].astype(BF16)


def total_kernel(x_ref, o_ref):
    total = x_ref[0].astype(F32)
    for k in range(1, x_ref.shape[0]):
        total = total + x_ref[k].astype(F32)
    o_ref[...] = jnp.broadcast_to(total.astype(BF16)[None], o_ref.shape)


def read_kernels(pack, rows, w_ref, s_ref, turned):
    for at, own, wide, t, u, width in pack.kernel_tiles():
        target, columns = (w_ref, 9 * NARROW) if wide else (turned, 9 * SQUEEZE)
        start = columns * t + 128 * u
        target[:, start : start + width] = rows[at : at + own, :width].astype(F32)
    s_ref[...] = jnp.transpose(turned[...])


def read_points(pack, start, rows, o_refs):
    for at, u, width in pack.point_blocks(start):
        block = rows[at : at + pack.point, :].astype(F32)
        for (first, _, own), o_ref in zip(pack.point_parts(), o_refs):
            o_ref[:, 128 * u : 128 * u + width] = block[first : first + own, :width]


def late_gradients_kernel(pack, batches, mb_ref, *refs):
    x_refs = refs[:batches]
    w_ref, s_ref, held, turned = refs[batches:]
    for k, x_ref in enumerate(x_refs):
        held[mb_ref[0] ^ k] = x_ref[...]
    read_kernels(pack, held[...].reshape(-1, 128), w_ref, s_ref, turned)


def points_out_kernel(pack, x_ref, *o_refs):
    read_points(pack, 0, x_ref[...].reshape(-1, 128), o_refs)


def early_gradients_kernel(pack, late_pack, x_ref, late_ref, w_ref, s_ref, *refs):
    *o_refs, wide, turned = refs
    rows = x_ref[...].reshape(-1, 128)
    read_kernels(pack, rows, wide, s_ref, turned)
    read_points(late_pack, pack.kernels, rows, o_refs)

    def join(g, carry):
        parts = []
        for r in range(4):
            at = pl.ds(4 * g + r, 1)
            parts.append(jnp.concatenate([wide[at, :], late_ref[at, :]], axis=0))
        first = pl.multiple_of(4 * WIDE_COLUMNS * g, 128)
        w_ref[:, pl.ds(first, 4 * WIDE_COLUMNS)] = jnp.concatenate(parts, axis=1)
        return carry

    lax.fori_loop(0, pack.wide // 4, join, 0)


def point_gradients(
    geo, clips, g_ref, sums_ref, st_ref, str_ref, aff_ref, dr_ref, dd_ref, dp_ref, yr_ref, yd_ref,
    yp_ref, m_ref, gy_ref, sumr_ref, held
):
    rows = clips * geo.clip_rows
    sumr_ref[...] = jnp.sum(g_ref[...], axis=0)
    sums, sums_r, st, st_r = sums_ref[...], sumr_ref[...], st_ref[...], str_ref[...]
    count = st_r[2:3, 0:1]
    scale_d, _ = affine_of(aff_ref, geo.block, "d")
    scale_r, _ = affine_of(aff_ref, geo.block, "r")
    scale_p, _ = affine_of(aff_ref, geo.block, "p")
    mean_d, rstd_d = outer_stats(st, "d")
    mean_p, rstd_p = outer_stats(st, "p")
    mean_r, rstd_r = row(st_r, 0, REDUCED), row(st_r, 4, REDUCED)

    def pair(unit):
        first, width = TILE_ROW[unit]
        return row(sums, first, width), row(sums, 8 + first, width)

    pair_d, pair_p = pair("d"), pair("p")
    pair_r = (row(sums_r, 0, REDUCED), row(sums_r, 4, REDUCED))

    def finish(r, carry):
        at = pl.ds(r, CHUNK)
        gy_ref[at, :DIRECT] = finish_rows(
            dd_ref[at, :], yd_ref[at, :], wide_mask(m_ref, at, DIRECT), mean_d, rstd_d, scale_d, *pair_d, count
        ).astype(BF16)
        gy_ref[at, DIRECT : DIRECT + REDUCED] = finish_rows(
            dr_ref[at, :], yr_ref[at, :], wide_mask(m_ref, at, REDUCED), mean_r, rstd_r, scale_r, *pair_r, count
        ).astype(BF16)
        held[at, :] = finish_rows(
            dp_ref[at, :], yp_ref[at, :], m_ref[at, :], mean_p, rstd_p, scale_p, *pair_p, count
        )
        return carry

    each_chunk(rows, finish)
    masks = edge_masks(geo, PROJECT)
    for c in range(clips):
        at = slice(c * geo.clip_rows, (c + 1) * geo.clip_rows)
        gy_ref[at, DIRECT + REDUCED :] = mean_cells(geo, held[at, :], masks).astype(BF16)


def late_input_kernel(
    clips, g_ref, sums_ref, st_ref, str_ref, aff_ref, dr_ref, dd_ref, dp_ref, yr_ref, yd_ref, yp_ref,
    mc_ref, wt_ref, spread_ref, est_ref, ed_ref, ew_ref, es_ref, ep_ref, m_ref,
    gy_ref, hd_ref, hw_ref, hs_ref, hp_ref, pay_ref, sumr_ref, held, grad, wide, tile
):
    point_gradients(
        LATE, clips, g_ref, sums_ref, st_ref, str_ref, aff_ref, dr_ref, dd_ref, dp_ref, yr_ref,
        yd_ref, yp_ref, mc_ref, gy_ref, sumr_ref, held,
    )
    grad[...] = nn(gy_ref[...], wt_ref[...]).astype(BF16)
    st = est_ref[...]
    tile[...] = jnp.zeros_like(tile)
    column = 0
    for unit, y_ref, dh_ref in zip(
        OUTER, (ed_ref, ew_ref, es_ref, ep_ref), (hd_ref, hw_ref, hs_ref, hp_ref)
    ):
        width = TILE_ROW[unit][1]
        for c in range(clips):
            wide[c * EARLY.clip_rows : (c + 1) * EARLY.clip_rows, :width] = nn(
                spread_ref[...],
                grad[c * LATE.clip_rows : (c + 1) * LATE.clip_rows, column : column + width],
            )
        column += width
        mean, rstd = outer_stats(st, unit)
        scale, shift = affine_of(aff_ref, 0, unit)
        sums = local_backward(
            y_ref, lambda at: wide[at, :width], m_ref=m_ref, mean=mean, rstd=rstd, scale=scale,
            shift=shift, dh_ref=dh_ref, out_ref=None, rows=clips * EARLY.clip_rows,
        )
        put_row(tile, TILE_ROW[unit][0], sums[0])
        put_row(tile, 8 + TILE_ROW[unit][0], sums[1])
    send_tile(pay_ref, tile)


def early_input_kernel(
    pack, clips, me_ref, g_ref, sums_ref, st_ref, str_ref, aff_ref, dr_ref, dd_ref, dp_ref, yr_ref,
    yd_ref, yp_ref, m_ref, wt_ref, gy_ref, *refs
):
    x_refs = refs[: pack.groups]
    sumr_ref, held, turned = refs[pack.groups :]
    point_gradients(
        EARLY, clips, g_ref, sums_ref, st_ref, str_ref, aff_ref, dr_ref, dd_ref, dp_ref, yr_ref,
        yd_ref, yp_ref, m_ref, gy_ref, sumr_ref, held,
    )
    depth = turned.shape[1]
    rows = clips * EARLY.clip_rows
    for j in range(0, rows, 128):
        size = min(128, rows - j)
        grad = jnp.transpose(nn(gy_ref[j : j + size, :], wt_ref[...]) * wide_mask(m_ref, slice(j, j + size), wt_ref.shape[1]))
        for s in range(pack.groups):
            turned[s, :, j : j + size] = grad[s * depth : (s + 1) * depth, :].astype(BF16)
    for k, x_ref in enumerate(x_refs):
        x_ref[...] = turned[me_ref[0] ^ k]


def feature_kernel(pack, me_ref, *refs):
    *x_refs, o_ref, held = refs
    for k, x_ref in enumerate(x_refs):
        held[me_ref[0] ^ k] = x_ref[...]
    width = held.shape[2]
    for s in range(pack.groups):
        o_ref[:, s * width : (s + 1) * width] = held[s].astype(F32)


def pool_matrix():
    matrix = np.zeros((LATE.clip_rows, EARLY.clip_rows), np.float32)
    for f in range(EARLY.frames):
        for h in range(EARLY.height):
            for w in range(EARLY.width):
                cell = (f // 2) * LATE.frame_rows + (h // 2) * LATE.pitch + w // 2
                matrix[cell, (f * EARLY.height + h) * EARLY.width + w] = 0.125
    return matrix


def pad_late(field):
    padded = jnp.pad(field, ((0, 0), (0, 0), (0, 0), (0, LATE.pitch - LATE.width), (0, 0)))
    return padded.reshape(-1, field.shape[4])


def shards(
    clip_features, visible, direct_early, narrow_early, squeeze_early, project_early, direct_late,
    narrow_late, squeeze_late, project_late, wide_kernels, spread_kernels, direct_norm, narrow_norm,
    wide_norm, squeeze_norm, spread_norm, project_norm, upstream_direct, upstream_wide,
    upstream_spread, upstream_project,
):
    groups = lax.axis_size("ch")
    batches = lax.axis_size("batch")
    devices = groups * batches
    me = lax.axis_index("ch")
    me_ref = jnp.reshape(me, (1,)).astype(jnp.int32)
    held_clips = visible.shape[0]
    clips = held_clips // groups
    rows = clips * EARLY.clip_rows
    late_rows = clips * LATE.clip_rows
    depth = clip_features.shape[0]
    features = depth * groups
    pack = Packing(groups, features)
    late_pack = Packing(groups, CONCAT)

    def exchange(payload):
        return lax.all_to_all(payload, BOTH, 0, 0)

    def swap(value, bit):
        return lax.ppermute(value, "ch", [(i, i ^ bit) for i in range(groups)])

    class Shares:
        def __init__(self, own):
            self.pieces, self.bit = {0: own}, groups // 2
            self.step()

        def step(self):
            for k in list(self.pieces):
                self.pieces[k | self.bit] = swap(self.pieces[k], self.bit)
            self.bit //= 2

        def all(self, *behind):
            if behind:
                last = max(self.pieces)
                self.pieces[last] = ordered(self.pieces[last], *behind)
            while self.bit:
                self.step()
            return [self.pieces[k] for k in range(groups)]

    early_parts = (direct_early, narrow_early, squeeze_early, project_early)
    late_parts = (direct_late, narrow_late, squeeze_late, project_late)
    norms = (direct_norm, narrow_norm, squeeze_norm, wide_norm, spread_norm, project_norm)
    norm_rows = jnp.concatenate(norms, axis=2).reshape(4, -1)
    norm_space = padded16(4 * -(-norm_rows.shape[1] // 128))
    pieces, early_points = call(
        lambda *refs: prepare_kernel(pack, *refs),
        [((groups, depth, rows), BF16), ((pack.points + norm_space, 128), BF16)],
        [clip_features, norm_rows] + [part.T for part in early_parts],
        [((pack.point_rows, pack.point_tiles * 128), F32), ((norm_space, 128), F32)],
        us=2.5,
    )
    arrived = lax.all_to_all(pieces, "ch", 0, 0)
    point_shares = Shares(early_points).all()
    flat_rows = wide_kernels.shape[1] // 128
    halves = call(split_kernel, [((flat_rows, 128), BF16)] * 2, [wide_kernels, pieces], us=4.8, idle=1)
    spread_rows = jnp.transpose(
        spread_kernels.reshape(2, SPREAD_COLUMNS, spread_kernels.shape[3]), (0, 2, 1)
    )

    def packed(use, block, parts, behind):
        size = use.kernels + (use.points if parts else 0)
        return call(
            lambda *refs: pack_kernel(use, *refs),
            [((size, 128), BF16)],
            [halves[block].reshape(-1, WIDE_COLUMNS), spread_rows[block]]
            + [part.T for part in parts] + list(behind),
            [((use.point_rows, use.point_tiles * 128), F32)],
            idle=len(behind),
            us=2.5,
        )[0]

    early_shares = Shares(ordered(packed(pack, 0, (), ()), point_shares[-1], arrived)).all()
    own_visible = lax.dynamic_slice_in_dim(visible, me * clips, clips, 0)
    fine = own_visible.astype(F32).reshape(rows, 1)
    mask = jnp.broadcast_to(fine, (rows, 128))
    cells = own_visible.reshape(clips, 2, 2, 6, 2, 6, 2).max(axis=(2, 4, 6)).astype(F32)
    coarse = jnp.broadcast_to(pad_late(cells[..., None]), (late_rows, 128))

    upstream = (upstream_direct, upstream_wide, upstream_spread, upstream_project)
    up_joined = jnp.concatenate(upstream, axis=4)
    up_parts = up_joined.reshape((groups, clips) + up_joined.shape[1:])
    up_arrived = lax.all_to_all(up_parts, "ch", 0, 0)
    ups, at = [], 0
    for part in upstream:
        width = part.shape[4]
        piece = jnp.moveaxis(up_arrived[..., at : at + width], 0, 4)
        ups.append(pad_late(piece.reshape(piece.shape[:4] + (groups * width,))))
        at += width

    pool = jnp.asarray(pool_matrix(), BF16)
    spread_back = jnp.asarray(pool_matrix().T, BF16)

    act, wt, affine, yr, pay = call(
        lambda *refs: early_first_kernel(pack, *refs),
        [
            ((rows, features), BF16), ((POINT, features), BF16), ((4, SLOTS), F32),
            ((rows, REDUCED), F32), ((devices, 8, 128), F32),
        ],
        [me_ref, arrived] + point_shares + [mask, coarse],
        [
            ((features, rows), F32), ((groups, pack.point_rows, pack.point_tiles * 128), F32),
            ((POINT, features), F32), ((groups, norm_space, 128), F32), ((8, 128), F32),
        ],
        us=8.6,
    )
    late_share = packed(late_pack, 1, late_parts, (act,))
    counts = exchange(pay)
    late_shares = Shares(ordered(late_share, counts))
    yd, yp, tile = call(
        lambda *refs: other_points_kernel(EARLY, clips, *refs),
        [((rows, DIRECT), F32), ((rows, PROJECT), F32), ((16, 128), F32)],
        [act, wt, mask],
        us=12,
    )

    def second(geo, count_row, g, y, masking, pieces, other):
        own = clips * geo.clip_rows
        padded = clips * geo.padded_rows
        return call(
            lambda *refs: second_kernel(geo, clips, pack, count_row, *refs),
            [
                ((padded, 128 * WIDE_TILES), BF16), ((padded, 128 * SPREAD_TILES), BF16),
                ((own, WIDE), F32), ((own, SPREAD), F32),
                ((3, groups, pack.wide_rows, 128 * WIDE_TILES), BF16),
                ((3, groups, pack.spread_rows, 128 * SPREAD_TILES), BF16),
                ((devices, 16, 128), F32), ((8, 128), F32),
            ],
            [me_ref, g, counts, affine, y, masking, other] + pieces,
            [((own, REDUCED), F32), ((16, 128), F32)],
            us=25 if geo is EARLY else 9,
        )

    bn, bs, yw, ys, kw, ks, pay, st_r = second(EARLY, 2, counts, yr, mask, early_shares, tile)
    g = exchange(pay)
    late_shares = late_shares.all(st_r)
    late_act, late_wt, lyr, pay, st = call(
        lambda *refs: pool_kernel(late_pack, clips, *refs),
        [
            ((late_rows, CONCAT), BF16), ((POINT, CONCAT), BF16), ((late_rows, REDUCED), F32),
            ((devices, 8, 128), F32), ((16, 128), F32),
        ],
        [me_ref, g, counts, affine, yd, yw, ys, yp, mask, pool, coarse] + late_shares,
        [
            ((rows, 384), BF16), ((rows, 384), BF16),
            ((groups, late_pack.point_rows, late_pack.point_tiles * 128), F32),
            ((POINT, CONCAT), F32), ((8, 128), F32),
        ],
        us=15,
    )
    g = exchange(pay)
    lyd, lyp, tile = call(
        lambda *refs: other_points_kernel(LATE, clips, *refs),
        [((late_rows, DIRECT), F32), ((late_rows, PROJECT), F32), ((16, 128), F32)],
        [late_act, late_wt, coarse],
        us=3.7,
    )
    lbn, lbs, lyw, lys, lkw, lks, pay, lst_r = second(LATE, 3, g, lyr, coarse, late_shares, tile)
    g = exchange(pay)
    widths = [TILE_ROW[unit][1] for unit in OUTER]
    res = call(
        lambda *refs: late_outputs_kernel(clips, *refs),
        [((late_rows, w), BF16) for w in widths]
        + [((late_rows, w), F32) for w in widths]
        + [((devices, 16, 128), F32), ((16, 128), F32)],
        [g, counts, affine, lyd, lyw, lys, lyp, coarse] + ups,
        [((16, 128), F32)],
        us=4,
    )
    outs, (hd, hw, hs, hp), (pay, lst) = res[:4], res[4:8], res[8:]
    g = exchange(pay)

    out_parts = []
    for o in outs:
        cells = o.reshape(clips, LATE.frames, LATE.height, LATE.pitch, -1)[:, :, :, : LATE.width]
        out_parts.append(cells.reshape(cells.shape[:4] + (groups, -1)))
    out_joined = jnp.moveaxis(jnp.concatenate(out_parts, axis=5), 4, 0)
    def finish(geo, g, st, st_r, hw, hs, yw, ys, masking, behind=()):
        own = clips * geo.clip_rows
        return call(
            lambda *refs: finish_kernel(geo, clips, *refs),
            [((own, WIDE), BF16), ((own, SPREAD), BF16), ((16, 128), F32)],
            [g, st, st_r, affine, hw, hs, yw, ys, masking] + list(behind),
            idle=len(behind),
            us=7 if geo is EARLY else 2.5,
        )

    def inner(geo, st_r, gw, gs, yr, kw, ks, masking, behind=()):
        own = clips * geo.clip_rows
        padded = clips * geo.padded_rows
        return call(
            lambda *refs: inner_backward_kernel(geo, clips, pack, *refs),
            [((own, REDUCED), F32), ((devices, 8, 128), F32)],
            [st_r, affine, gw, gs, yr, kw, ks, masking] + list(behind),
            [
                ((padded, 9 * WIDE), BF16), ((padded, 9 * SPREAD), BF16),
                ((3, 9 * WIDE, NARROW), BF16), ((3, 9 * SPREAD, SQUEEZE), BF16),
                ((own, REDUCED), F32), ((8, 128), F32),
            ],
            idle=len(behind),
            us=16 if geo is EARLY else 5.6,
        )

    unit = 16 * batches

    def kernel_grads(geo, size, gw, gs, bn, bs, halves, others=()):
        outs = [(groups // 2, size, 128)] * 2 if halves else [(groups, size, 128)]
        return call(
            lambda *refs: kernel_grad_kernel(geo, clips, pack, halves, *refs),
            [(shape, BF16) for shape in outs],
            [me_ref, gw, gs, bn, bs] + list(others),
            [((3, WIDE, 128 * WIDE_TILES), F32), ((3, SPREAD, 128 * SPREAD_TILES), F32)],
            us=10 if geo is EARLY else 5,
        )

    def point_grads(use, size, gy, act, behind=()):
        return call(
            lambda *refs: point_grad_kernel(use, *refs),
            [((groups // 2, size, 128), BF16)] * 2,
            [me_ref, gy, act] + list(behind),
            [((POINT, use.features), F32), ((groups, use.point_rows, use.point_tiles * 128), F32)],
            us=4.5,
            idle=len(behind),
        )

    class Reduction:
        def __init__(self, keep, send):
            self.keep, self.bit = keep, 1
            self.got = swap(send, 1)

        def halve(self, *behind):
            while 2 * self.bit < groups:
                shape = (self.keep.shape[0] // 2,) + self.keep.shape[1:]
                self.keep, send = call(
                    halve_kernel, [(shape, BF16)] * 2, [self.keep, self.got] + list(behind),
                    idle=len(behind),
                    us=2.5,
                )
                self.bit *= 2
                self.got = swap(send, self.bit)
            return self.keep

        def add(self, *behind):
            return call(
                add_kernel, [(self.keep.shape[1:], BF16)], [self.keep, self.got] + list(behind),
                idle=len(behind),
                us=2,
            )[0]

    mb_ref = jnp.reshape(lax.axis_index("batch"), (1,)).astype(jnp.int32)

    def batch_swap(value, bit):
        return lax.ppermute(value, "batch", [(i, i ^ bit) for i in range(batches)])

    def whole_units(size):
        return -(-size // unit) * unit

    gw, gs, late_sums = finish(LATE, g, lst, lst_r, hw, hs, lyw, lys, coarse)
    hr, pay = inner(LATE, lst_r, gw, gs, lyr, lkw, lks, coarse)
    g = exchange(pay)
    (late_kernels,) = kernel_grads(LATE, whole_units(pack.kernels), gw, gs, lbn, lbs, False)
    late_share = lax.psum_scatter(late_kernels, "ch", scatter_dimension=0)
    out_arrived = ordered(lax.all_to_all(out_joined, "ch", 0, 0))
    gy, ed, ew, es, ep, pay, late_sums_r = call(
        lambda *refs: late_input_kernel(clips, *refs),
        [((late_rows, POINT), BF16)]
        + [((rows, w), F32) for w in widths]
        + [((devices, 16, 128), F32), ((8, 128), F32)],
        [g, late_sums, lst, lst_r, affine, hr, hd, hp, lyr, lyd, lyp, coarse, late_wt, spread_back,
         st, yd, yw, ys, yp, mask, late_kernels, out_arrived],
        [((late_rows, PROJECT), F32), ((late_rows, CONCAT), BF16), ((rows, WIDE), F32), ((16, 128), F32)],
        idle=2,
        us=15,
    )
    g = exchange(pay)
    late_points = point_grads(late_pack, late_pack.points, gy, late_act)
    gw, gs, sums = finish(EARLY, g, st, st_r, ew, es, yw, ys, mask, late_points[1:])
    halves = kernel_grads(
        EARLY, whole_units(pack.kernels + late_pack.points), gw, gs, bn, bs, True, late_points
    )
    early_sum = Reduction(*halves)

    class BatchHalves(Reduction):
        def __init__(self, keep, send):
            self.keep, self.bit = keep, 1
            self.got = batch_swap(send, 1)

        def step(self, *behind):
            shape = (self.keep.shape[0] // 2,) + self.keep.shape[1:]
            self.keep, send = call(
                halve_kernel, [(shape, BF16)] * 2, [self.keep, self.got] + list(behind),
                idle=len(behind), us=1.5,
            )
            self.bit *= 2
            self.got = batch_swap(send, self.bit)
            return self.keep

        def spread(self, *behind):
            own = self.add(*behind)
            self.pieces, self.bit = {0: own}, batches // 2
            return own

        def double(self):
            got = {k | self.bit: batch_swap(self.pieces[k], self.bit) for k in self.pieces}
            self.pieces.update(got)
            self.bit //= 2
            return list(got.values())

    late_piece = late_share.shape[0] // batches
    late_halves = call(
        scatter_halves_kernel,
        [((batches // 2, late_piece, 128), BF16)] * 2,
        [mb_ref, late_share, halves[1]],
        [(late_share.shape, F32)],
        us=3,
        idle=1,
    )
    late_sum = BatchHalves(*late_halves)
    kept = early_sum.halve(late_halves[1])
    hr, pay = inner(EARLY, st_r, gw, gs, yr, kw, ks, mask, behind=(kept,))
    g = exchange(pay)
    late_kept = late_sum.step(hr)
    own = early_sum.add(late_kept)
    parts = lax.all_to_all(own.reshape(batches, -1, 128), "batch", 0, 0)
    late_kept = own
    while 2 * late_sum.bit < batches:
        late_kept = late_sum.step(own)
    gy, *x_parts, sums_r = call(
        lambda *refs: early_input_kernel(pack, clips, *refs),
        [((rows, POINT), BF16)] + [((depth, rows), BF16)] * groups + [((8, 128), F32)],
        [me_ref, g, sums, st, st_r, affine, hr, ed, ep, yr, yd, yp, mask, wt, late_kept],
        [((rows, PROJECT), F32), ((groups, depth, rows), BF16)],
        idle=1,
        us=8.5,
    )
    x_parts = [x_parts[0]] + [swap(x_parts[k], k) for k in range(1, groups)]
    late_own = late_sum.spread(gy)
    point_halves = point_grads(pack, whole_units(pack.points), gy, act, (late_own,))
    point_sum = Reduction(*point_halves)
    kept = point_sum.halve()
    (feature_grad,) = call(
        lambda *refs: feature_kernel(pack, *refs),
        [((depth, groups * rows), F32)],
        [me_ref] + x_parts + [kept],
        [((groups, depth, rows), BF16)],
        idle=1,
        us=2,
    )
    got = late_sum.double()
    (parts,) = call(
        total_kernel,
        [(parts.shape, BF16)],
        [parts, feature_grad] + got,
        us=2,
        idle=1 + len(got),
    )
    early_total = lax.all_to_all(parts, "batch", 0, 0)
    while late_sum.bit:
        late_sum.double()
    late_pieces = [late_sum.pieces[k] for k in range(batches)]
    late_wide, late_spread = call(
        lambda *refs: late_gradients_kernel(pack, batches, *refs),
        [((pack.wide, WIDE_COLUMNS), F32), ((SPREAD_COLUMNS, pack.spread), F32)],
        [mb_ref] + late_pieces,
        [((batches, late_piece, 128), BF16), ((pack.spread, SPREAD_COLUMNS), F32)],
        us=3,
    )
    point_own = point_sum.add(early_total)
    point_parts = lax.all_to_all(point_own.reshape(batches, -1, 128), "batch", 0, 0)
    (point_parts,) = call(
        total_kernel, [(point_parts.shape, BF16)], [point_parts, late_wide], us=1, idle=1
    )
    point_total = lax.all_to_all(point_parts, "batch", 0, 0)
    out_arrived = out_arrived.reshape((held_clips,) + out_arrived.shape[2:])
    outputs, at = [], 0
    for part in upstream:
        outputs.append(out_arrived[..., at : at + part.shape[4]])
        at += part.shape[4]

    wide_grad, early_spread, *late_grads = call(
        lambda *refs: early_gradients_kernel(pack, late_pack, *refs),
        [(wide_kernels.shape, F32), ((SPREAD_COLUMNS, pack.spread), F32)]
        + [(part.shape[::-1], F32) for part in late_parts],
        [early_total, late_wide],
        [((pack.wide, WIDE_COLUMNS), F32), ((pack.spread, SPREAD_COLUMNS), F32)],
        us=8,
    )
    early_grads = call(
        lambda *refs: points_out_kernel(pack, *refs),
        [(part.shape[::-1], F32) for part in early_parts],
        [point_total],
        us=1.5,
    )
    early_grads = [part.T for part in early_grads]
    late_grads = [part.T for part in late_grads]
    spread_grad = jnp.stack(
        [part.reshape(spread_kernels.shape[1:]) for part in (early_spread, late_spread)]
    )

    def outer_pair(tile, unit):
        first, width = TILE_ROW[unit]
        return jnp.stack([tile[k : k + 3].reshape(-1)[:width] for k in (first, first + 8)])

    def inner_pair(tile, low, high):
        return jnp.stack([tile[k : k + 2].reshape(-1)[low:high] for k in (0, 4)])

    def own_part(early_pair, late_pair):
        both = jnp.stack([early_pair, late_pair])
        size = both.shape[2] // groups
        return lax.dynamic_slice_in_dim(both, me * size, size, 2)

    norm_grads = [
        own_part(outer_pair(sums, "d"), outer_pair(late_sums, "d")),
        own_part(inner_pair(sums_r, 0, NARROW), inner_pair(late_sums_r, 0, NARROW)),
        own_part(outer_pair(sums, "w"), outer_pair(late_sums, "w")),
        own_part(inner_pair(sums_r, NARROW, REDUCED), inner_pair(late_sums_r, NARROW, REDUCED)),
        own_part(outer_pair(sums, "s"), outer_pair(late_sums, "s")),
        own_part(outer_pair(sums, "p"), outer_pair(late_sums, "p")),
    ]
    return tuple(outputs) + (feature_grad,) + tuple(early_grads) + tuple(late_grads) + (
        wide_grad, spread_grad,
    ) + tuple(norm_grads)


def solution(mesh):
    columns = P(None, "ch")
    norm = P(None, None, "ch")
    clips = P("batch", None, None, None, "ch")
    kernels = P(None, None, None, "ch")
    return jax.shard_map(
        shards,
        mesh=mesh,
        in_specs=(P("ch", "batch"), P("batch", None, None, None)) + (columns,) * 9 + (kernels,)
        + (norm,) * 6 + (clips,) * 4,
        out_specs=(clips,) * 4 + (P("ch", "batch"),) + (columns,) * 9 + (kernels,) + (norm,) * 6,
        check_vma=False,
    )
```

```python
import jax
import jax.numpy as jnp
import numpy as np
from jax import lax
from jax.experimental import pallas as pl
from jax.experimental.pallas import tpu as pltpu
from jax.sharding import PartitionSpec as P

F32 = jnp.float32
BF16 = jnp.bfloat16
EPSILON = 0.001
FLOPS_A_US = 1.1e9
BOTH = ("batch", "ch")
DIRECT, NARROW, WIDE, SQUEEZE, SPREAD, PROJECT = 256, 160, 320, 32, 128, 128
REDUCED = NARROW + SQUEEZE
POINT = DIRECT + REDUCED + PROJECT
CONCAT = DIRECT + WIDE + SPREAD + PROJECT
WIDE_COLUMNS = 27 * NARROW
SPREAD_COLUMNS = 27 * SQUEEZE
POINT_WIDTHS = (DIRECT, NARROW, SQUEEZE, PROJECT)
SLOT = {"d": (0, DIRECT), "r": (256, REDUCED), "w": (512, WIDE), "s": (896, SPREAD), "p": (1024, PROJECT)}
SLOTS = 1152
NORM_ORDER = ((0, DIRECT), (256, NARROW), (256 + NARROW, SQUEEZE), (512, WIDE), (896, SPREAD), (1024, PROJECT))
TILE_ROW = {"d": (0, DIRECT), "w": (2, WIDE), "s": (5, SPREAD), "p": (6, PROJECT)}
OUTER = ("d", "w", "s", "p")
CHUNK = 96


class Geometry:
    def __init__(self, frames, height, width, pitch, block):
        self.frames, self.height, self.width, self.pitch = frames, height, width, pitch
        self.block = block
        self.frame_rows = height * pitch
        self.clip_rows = frames * self.frame_rows
        self.padded_rows = (frames + 2) * self.frame_rows
        self.dense = pitch == width


EARLY = Geometry(4, 12, 12, 12, 0)
LATE = Geometry(2, 6, 6, 8, 1)


def nt(a, b):
    return lax.dot_general(a, b, (((1,), (1,)), ((), ())), preferred_element_type=F32)


def nn(a, b):
    return lax.dot_general(a, b, (((1,), (0,)), ((), ())), preferred_element_type=F32)


def tn(a, b):
    return lax.dot_general(a, b, (((0,), (0,)), ((), ())), preferred_element_type=F32)


def call(kernel, outs, ins, scratch=(), us=0, idle=0):
    moved = sum(int(np.prod(s)) * jnp.dtype(d).itemsize for s, d in outs)
    moved += sum(int(np.prod(x.shape)) * x.dtype.itemsize for x in ins[: len(ins) - idle])

    def spec(k, x):
        if k >= len(ins) - idle:
            return pl.BlockSpec(memory_space=pl.ANY)
        return pl.BlockSpec(memory_space=pltpu.SMEM if x.ndim == 1 else pltpu.VMEM)

    def body(*refs):
        kept = len(ins) - idle
        kernel(*refs[:kept], *refs[len(ins) :])

    return pl.pallas_call(
        body,
        out_shape=[jax.ShapeDtypeStruct(s, d) for s, d in outs],
        in_specs=[spec(k, x) for k, x in enumerate(ins)],
        out_specs=[pl.BlockSpec(memory_space=pltpu.VMEM)] * len(outs),
        scratch_shapes=[pltpu.VMEM(s, d) for s, d in scratch],
        compiler_params=pltpu.CompilerParams(vmem_limit_bytes=56 * 2**20),
        cost_estimate=pl.CostEstimate(
            flops=int(us * FLOPS_A_US) or 10 * moved, bytes_accessed=moved, transcendentals=0
        ),
    )(*ins)


def ordered(value, *behind):
    anywhere = pl.BlockSpec(memory_space=pl.ANY)
    return pl.pallas_call(
        lambda *refs: None,
        out_shape=jax.ShapeDtypeStruct(value.shape, value.dtype),
        in_specs=[anywhere] * (1 + len(behind)),
        out_specs=anywhere,
        input_output_aliases={0: 0},
    )(value, *behind)


def each_chunk(rows, body, init=0, chunk=CHUNK):
    return lax.fori_loop(
        0, rows // chunk, lambda i, carry: body(pl.multiple_of(i * chunk, chunk), carry), init
    )


def wide_mask(m_ref, at, width):
    part = m_ref[at, :]
    if width <= 128:
        return part[:, :width]
    return jnp.concatenate([part] * -(-width // 128), axis=1)[:, :width]


def row(tile, first, width):
    pieces = [
        tile[first + i : first + i + 1, : min(128, width - 128 * i)] for i in range(-(-width // 128))
    ]
    return pieces[0] if len(pieces) == 1 else jnp.concatenate(pieces, axis=1)


def put_row(ref, first, vector):
    width = vector.shape[1]
    for i in range(-(-width // 128)):
        part = vector[:, 128 * i : min(128 * (i + 1), width)]
        ref[first + i : first + i + 1, : part.shape[1]] = part


def affine_of(aff_ref, block, unit):
    start, width = SLOT[unit]
    return (
        aff_ref[2 * block : 2 * block + 1, start : start + width],
        aff_ref[2 * block + 1 : 2 * block + 2, start : start + width],
    )


def fold8(value):
    total = value[0:8]
    for i in range(1, value.shape[0] // 8):
        total = total + value[8 * i : 8 * i + 8]
    return total


def local_moments(y_ref, m_ref, rows, count):
    width = y_ref.shape[1]

    def first(r, acc):
        at = pl.ds(r, CHUNK)
        return acc + fold8(y_ref[at, :] * wide_mask(m_ref, at, width))

    total = each_chunk(rows, first, jnp.zeros((8, width), F32))
    mean = jnp.sum(total, axis=0, keepdims=True) / count

    def second(r, acc):
        at = pl.ds(r, CHUNK)
        centred = (y_ref[at, :] - mean) * wide_mask(m_ref, at, width)
        return acc + fold8(centred * centred)

    spread = each_chunk(rows, second, jnp.zeros((8, width), F32))
    return mean, jnp.sum(spread, axis=0, keepdims=True)


def combine_moments(payload, counts, first, second, size):
    means = payload[:, first : first + size, :]
    total = jnp.sum(counts, axis=0)
    mean = jnp.sum(means * counts, axis=0) / total
    offset = means - mean[None]
    spread = jnp.sum(payload[:, second : second + size, :] + counts * offset * offset, axis=0)
    return mean, lax.rsqrt(spread / total + EPSILON)


def send_tile(pay_ref, tile_ref):
    pay_ref[...] = jnp.broadcast_to(tile_ref[...][None], pay_ref.shape)


def shifted(value, offset):
    if offset == 0:
        return value
    return pltpu.roll(value, (-offset) % value.shape[0], 0)


def cell_index(geo, shape):
    r = lax.broadcasted_iota(jnp.int32, shape, 0).astype(F32)
    line = jnp.floor((r + 0.5) * (1.0 / geo.pitch))
    column = r - geo.pitch * line
    frame = jnp.floor((line + 0.5) * (1.0 / geo.height))
    return line - geo.height * frame, column


def edge_masks(geo, width):
    line, column = cell_index(geo, (geo.clip_rows, width))
    return (
        {e: (line + e > -0.5) & (line + e < geo.height - 0.5) for e in (-1, 1)},
        {e: (column + e > -0.5) & (column + e < geo.width - 0.5) for e in (-1, 1)},
    )


def gather_cells(geo, value, masks, sign, store):
    lines, columns = masks
    for b, dw in enumerate((-1, 0, 1)):
        moved = shifted(value, sign * dw)
        if dw and geo.dense:
            moved = jnp.where(columns[sign * dw], moved, 0.0)
        for a, dh in enumerate((-1, 0, 1)):
            placed = shifted(moved, sign * dh * geo.pitch)
            if dh:
                placed = jnp.where(lines[sign * dh], placed, 0.0)
            store(3 * a + b, placed)


def frame_shift(geo, value, offset):
    if offset == 0:
        return value
    size = geo.frame_rows
    blank = jnp.zeros((size, value.shape[1]), value.dtype)
    if offset > 0:
        return jnp.concatenate([value[size:], blank], axis=0)
    return jnp.concatenate([blank, value[:-size]], axis=0)


def mean_cells(geo, value, masks):
    lines, columns = masks
    total = value
    for e in (-1, 1):
        moved = shifted(value, e)
        total = total + (jnp.where(columns[e], moved, 0.0) if geo.dense else moved)
    again = total
    for e in (-1, 1):
        again = again + jnp.where(lines[e], shifted(total, e * geo.pitch), 0.0)
    return (again + frame_shift(geo, again, 1) + frame_shift(geo, again, -1)) / 27.0


def clear_edges(geo, ref, clip):
    base = clip * geo.padded_rows
    size = geo.frame_rows
    blank = jnp.zeros((size, ref.shape[1]), ref.dtype)
    ref[base : base + size, :] = blank
    ref[base + geo.padded_rows - size : base + geo.padded_rows, :] = blank


def padded16(size):
    return -(-size // 16) * 16


class Packing:
    def __init__(self, groups, features):
        self.groups = groups
        self.wide, self.spread, self.point = WIDE // groups, SPREAD // groups, POINT // groups
        self.wide_rows = padded16(self.wide)
        self.spread_rows = padded16(self.spread)
        self.point_rows = padded16(self.point)
        self.kernels = 3 * WIDE_TILES * self.wide_rows + 3 * SPREAD_TILES * self.spread_rows
        self.features = features
        self.point_tiles = -(-features // 128)
        self.points = self.point_tiles * self.point_rows

    def kernel_tiles(self):
        at = 0
        for own, size, tiles, columns, wide in (
            (self.wide, self.wide_rows, WIDE_TILES, 9 * NARROW, True),
            (self.spread, self.spread_rows, SPREAD_TILES, 9 * SQUEEZE, False),
        ):
            for t in range(3):
                for u in range(tiles):
                    yield at, own, wide, t, u, min(128, columns - 128 * u)
                    at += size

    def point_blocks(self, start):
        for u in range(self.point_tiles):
            yield start + u * self.point_rows, u, min(128, self.features - 128 * u)

    def point_parts(self):
        at = start = 0
        for width in POINT_WIDTHS:
            own = width // self.groups
            yield at, start, own
            at += own
            start += width


WIDE_TILES = -(-9 * NARROW // 128)
SPREAD_TILES = -(-9 * SQUEEZE // 128)


def fit_tile(value):
    width = value.shape[1]
    if width == 128:
        return value
    return jnp.concatenate([value, jnp.zeros((value.shape[0], 128 - width), value.dtype)], axis=1)


def pack_points(pack, part_refs, o_ref, start, scratch):
    for (at, _, own), ref in zip(pack.point_parts(), part_refs):
        scratch[at : at + own, : pack.features] = ref[...].astype(F32)
    for at, u, width in pack.point_blocks(start):
        o_ref[at : at + pack.point, :] = fit_tile(
            scratch[: pack.point, 128 * u : 128 * u + width].astype(BF16)
        )


def unpack_points(pack, me, piece_refs, start, raw, scratch, wt_ref):
    for k, ref in enumerate(piece_refs):
        for at, u, width in pack.point_blocks(start):
            raw[me ^ k, : pack.point, 128 * u : 128 * u + width] = ref[at : at + pack.point, :width].astype(F32)
    for s in range(pack.groups):
        for at, begin, own in pack.point_parts():
            scratch[begin + s * own : begin + (s + 1) * own, :] = raw[s, at : at + own, : pack.features]
    wt_ref[...] = scratch[...].astype(BF16)


def unpack_kernels(pack, me, piece_refs, kw_ref, ks_ref):
    for k, ref in enumerate(piece_refs):
        for at, own, wide, t, u, _ in pack.kernel_tiles():
            target = kw_ref if wide else ks_ref
            size = target.shape[2]
            target[t, me ^ k, :, 128 * u : 128 * u + 128] = ref[at : at + size, :]


def whole_kernel(ref, t, own):
    if own == ref.shape[2]:
        return ref[t].reshape(ref.shape[1] * own, ref.shape[3])
    parts = [ref[t, s].astype(F32)[:own] for s in range(ref.shape[1])]
    return jnp.concatenate(parts, axis=0).astype(BF16)


def prepare_kernel(pack, x_ref, norm_ref, p0, p1, p2, p3, o_ref, b_ref, scratch, rows):
    width = o_ref.shape[2]
    for s in range(pack.groups):
        o_ref[s] = x_ref[:, s * width : (s + 1) * width]
    pack_points(pack, (p0, p1, p2, p3), b_ref, 0, scratch)
    rows[...] = jnp.zeros_like(rows)
    for u in range(-(-norm_ref.shape[1] // 128)):
        part = norm_ref[:, 128 * u : 128 * (u + 1)].astype(F32)
        rows[4 * u : 4 * u + 4, : part.shape[1]] = part
    b_ref[pack.points :, :] = rows[...].astype(BF16)


def split_kernel(x_ref, a_ref, b_ref):
    tiles = x_ref.shape[1] // 128

    def move(first, count):
        value = x_ref[:, pl.ds(128 * first, 128 * count)].astype(F32)
        for r, ref in ((0, a_ref), (1, b_ref)):
            parts = [value[r : r + 1, 128 * j : 128 * (j + 1)] for j in range(count)]
            ref[pl.ds(first, count), :] = jnp.concatenate(parts, axis=0).astype(BF16)

    def step(i, carry):
        move(pl.multiple_of(16 * i, 16), 16)
        return carry

    lax.fori_loop(0, tiles // 16, step, 0)
    if tiles % 16:
        move(tiles // 16 * 16, tiles % 16)


def pack_kernel(pack, w_ref, s_ref, o_ref):
    for at, own, wide, t, u, width in pack.kernel_tiles():
        source, columns = (w_ref, 9 * NARROW) if wide else (s_ref, 9 * SQUEEZE)
        start = columns * t + 128 * u
        o_ref[at : at + own, :] = fit_tile(source[:, start : start + width])


def pack_late_kernel(pack, p0, p1, p2, p3, o_ref, scratch):
    pack_points(pack, (p0, p1, p2, p3), o_ref, 0, scratch)


def early_first_kernel(
    pack, me_ref, x_ref, *refs
):
    groups = pack.groups
    piece_refs = refs[:groups]
    m_ref, mc_ref, a_ref, wt_ref, aff_ref, y_ref, pay_ref, xs, raw, ws, norm_raw, tile = refs[groups:]
    me = me_ref[0]
    depth, rows = x_ref.shape[1], x_ref.shape[2]
    for s in range(groups):
        xs[s * depth : (s + 1) * depth, :] = x_ref[s].astype(F32)
    for j in range(0, rows, 128):
        size = min(128, rows - j)
        turned = jnp.transpose(xs[:, j : j + size])
        a_ref[j : j + size, :] = (turned * wide_mask(m_ref, slice(j, j + size), turned.shape[1])).astype(BF16)
    unpack_points(pack, me, piece_refs, 0, raw, ws, wt_ref)
    for k, ref in enumerate(piece_refs):
        norm_raw[me ^ k] = ref[pack.points :, :].astype(F32)
    at = 0
    for slot, whole in NORM_ORDER:
        own = whole // groups
        for s in range(groups):
            left, u = at % 128, at // 128
            first = min(own, 128 - left)
            to = slot + s * own
            aff_ref[:, to : to + first] = norm_raw[s, 4 * u : 4 * u + 4, left : left + first]
            if first < own:
                aff_ref[:, to + first : to + own] = norm_raw[s, 4 * u + 4 : 4 * u + 8, : own - first]
        at += own
    y_ref[...] = nt(a_ref[...], wt_ref[DIRECT : DIRECT + REDUCED, :])
    tile[...] = jnp.zeros_like(tile)
    count = jnp.sum(m_ref[...], axis=0, keepdims=True)
    coarse = jnp.sum(mc_ref[...], axis=0, keepdims=True)
    mean, spread = local_moments(y_ref, m_ref, rows, count[:, 0:1])
    put_row(tile, 0, mean)
    put_row(tile, 2, count)
    put_row(tile, 3, coarse)
    put_row(tile, 4, spread)
    send_tile(pay_ref, tile)


def other_points_kernel(geo, clips, a_ref, wt_ref, m_ref, yd_ref, yp_ref, tile):
    yd_ref[...] = nt(a_ref[...], wt_ref[:DIRECT, :])
    projected = nt(a_ref[...], wt_ref[DIRECT + REDUCED :, :])
    masks = edge_masks(geo, PROJECT)
    for c in range(clips):
        rows = slice(c * geo.clip_rows, (c + 1) * geo.clip_rows)
        yp_ref[rows, :] = mean_cells(geo, projected[rows], masks)
    tile[...] = jnp.zeros_like(tile)
    count = jnp.sum(m_ref[...], axis=0, keepdims=True)[:, 0:1]
    for unit, ref in (("d", yd_ref), ("p", yp_ref)):
        mean, spread = local_moments(ref, m_ref, clips * geo.clip_rows, count)
        put_row(tile, TILE_ROW[unit][0], mean)
        put_row(tile, 8 + TILE_ROW[unit][0], spread)


def second_kernel(
    geo, clips, pack, count_row, me_ref, g_ref, counts_ref, aff_ref, y_ref, m_ref, pd_ref, *refs
):
    piece_refs = refs[: pack.groups]
    (bn_ref, bs_ref, yw_ref, ys_ref, kw_ref, ks_ref, pay_ref, st_ref, us, tile) = refs[pack.groups :]
    unpack_kernels(pack, me_ref[0], piece_refs, kw_ref, ks_ref)
    rows = clips * geo.clip_rows
    counts = counts_ref[:, count_row : count_row + 1, :]
    means, rstds = combine_moments(g_ref[...], counts, 0, 4, 2)
    st_ref[...] = jnp.zeros_like(st_ref)
    st_ref[0:2, :] = means
    st_ref[2:3, :] = jnp.sum(counts, axis=0)
    st_ref[4:6, :] = rstds
    mean, rstd = row(means, 0, REDUCED), row(rstds, 0, REDUCED)
    scale, shift = affine_of(aff_ref, geo.block, "r")

    def activate(r, carry):
        at = pl.ds(r, CHUNK)
        h = scale * ((y_ref[at, :] - mean) * rstd) + shift
        us[at, :] = h * jax.nn.sigmoid(h) * wide_mask(m_ref, at, REDUCED)
        return carry

    each_chunk(rows, activate)
    masks = edge_masks(geo, REDUCED)
    size = geo.frame_rows
    for c in range(clips):
        base = c * geo.padded_rows
        clear_edges(geo, bn_ref, c)
        clear_edges(geo, bs_ref, c)
        inside = slice(base + size, base + size + geo.clip_rows)
        for ref, used in ((bn_ref, 9 * NARROW), (bs_ref, 9 * SQUEEZE)):
            ref[inside, used:] = jnp.zeros((geo.clip_rows, ref.shape[1] - used), BF16)

        def store(j, placed):
            at = slice(base + size, base + size + geo.clip_rows)
            bn_ref[at, NARROW * j : NARROW * (j + 1)] = placed[:, :NARROW].astype(BF16)
            bs_ref[at, SQUEEZE * j : SQUEEZE * (j + 1)] = placed[:, NARROW:].astype(BF16)

        gather_cells(geo, us[c * geo.clip_rows : (c + 1) * geo.clip_rows, :], masks, 1, store)
    for c in range(clips):
        base = c * geo.padded_rows
        out = slice(c * geo.clip_rows, (c + 1) * geo.clip_rows)
        for b_ref, k_ref, o_ref, own in (
            (bn_ref, kw_ref, yw_ref, pack.wide), (bs_ref, ks_ref, ys_ref, pack.spread)
        ):
            total = None
            for t in range(3):
                term = nt(
                    b_ref[base + size * t : base + size * t + geo.clip_rows, :],
                    whole_kernel(k_ref, t, own),
                )
                total = term if total is None else total + term
            o_ref[out, :] = total
    tile[...] = pd_ref[...]
    own = jnp.sum(m_ref[...], axis=0, keepdims=True)[:, 0:1]
    for unit, ref in (("w", yw_ref), ("s", ys_ref)):
        mean, spread = local_moments(ref, m_ref, rows, own)
        put_row(tile, TILE_ROW[unit][0], mean)
        put_row(tile, 8 + TILE_ROW[unit][0], spread)
    send_tile(pay_ref, tile)


def outer_stats(st, unit):
    first, width = TILE_ROW[unit]
    return row(st, first, width), row(st, 8 + first, width)


def pool_kernel(
    pack, clips, me_ref, g_ref, counts_ref, aff_ref, yd_ref, yw_ref, ys_ref, yp_ref, m_ref, pool_ref,
    mc_ref, *refs
):
    piece_refs = refs[: pack.groups]
    a_ref, wt_ref, y_ref, pay_ref, st_ref, high, low, raw, ws, tile = refs[pack.groups :]
    means, rstds = combine_moments(g_ref[...], counts_ref[:, 2:3, :], 0, 8, 8)
    st_ref[0:8, :] = means
    st_ref[8:16, :] = rstds
    st = st_ref[...]
    at_column = 0
    for unit, ref in zip(OUTER, (yd_ref, yw_ref, ys_ref, yp_ref)):
        width = TILE_ROW[unit][1]
        mean, rstd = outer_stats(st, unit)
        scale, shift = affine_of(aff_ref, 0, unit)

        def activate(r, carry):
            at = pl.ds(r, CHUNK)
            h = scale * ((ref[at, :] - mean) * rstd) + shift
            u = h * jax.nn.sigmoid(h) * wide_mask(m_ref, at, width)
            top = u.astype(BF16)
            high[at, :width] = top
            low[at, :width] = (u - top.astype(F32)).astype(BF16)
            return carry

        each_chunk(clips * EARLY.clip_rows, activate)
        for c in range(clips):
            rows = slice(c * EARLY.clip_rows, (c + 1) * EARLY.clip_rows)
            pooled = nn(pool_ref[...], high[rows, :width]) + nn(pool_ref[...], low[rows, :width])
            out = slice(c * LATE.clip_rows, (c + 1) * LATE.clip_rows)
            a_ref[out, at_column : at_column + width] = pooled.astype(BF16)
        at_column += width
    unpack_points(pack, me_ref[0], piece_refs, 0, raw, ws, wt_ref)
    y_ref[...] = nt(a_ref[...], wt_ref[DIRECT : DIRECT + REDUCED, :])
    tile[...] = jnp.zeros_like(tile)
    own = jnp.sum(mc_ref[...], axis=0, keepdims=True)
    mean, spread = local_moments(y_ref, mc_ref, clips * LATE.clip_rows, own[:, 0:1])
    put_row(tile, 0, mean)
    put_row(tile, 4, spread)
    send_tile(pay_ref, tile)


def local_backward(y_ref, dz_of, m_ref, mean, rstd, scale, shift, dh_ref, out_ref, rows):
    width = y_ref.shape[1]

    def body(r, carry):
        at = pl.ds(r, CHUNK)
        masking = wide_mask(m_ref, at, width)
        xhat = (y_ref[at, :] - mean) * rstd
        h = scale * xhat + shift
        gate = jax.nn.sigmoid(h)
        if out_ref is not None:
            out_ref[at, :width] = (h * gate * masking).astype(out_ref.dtype)
        dh = dz_of(at) * masking * gate * (1.0 + h * (1.0 - gate))
        dh_ref[at, :] = dh
        return carry[0] + fold8(dh * xhat), carry[1] + fold8(dh)

    blank = jnp.zeros((8, width), F32)
    first, second = each_chunk(rows, body, (blank, blank))
    return jnp.sum(first, axis=0, keepdims=True), jnp.sum(second, axis=0, keepdims=True)


def cut_kernel(me_ref, x_ref, *o_refs):
    size = o_refs[0].shape[0]
    for k, o_ref in enumerate(o_refs):
        o_ref[...] = x_ref[pl.ds(pl.multiple_of((me_ref[0] ^ k) * size, 16), size), :]


def join_kernel(me_ref, *refs):
    *x_refs, o_ref = refs
    for k, x_ref in enumerate(x_refs):
        o_ref[me_ref[0] ^ k] = x_ref[...]


def late_outputs_kernel(
    clips, groups, me_ref, g_ref, counts_ref, aff_ref, yd_ref, yw_ref, ys_ref, yp_ref, mc_ref, *refs
):
    up_refs, o_refs = refs[:groups], refs[groups : 2 * groups]
    dd_ref, dw_ref, ds_ref, dp_ref, pay_ref, st_ref, shares, up, out, tile = refs[2 * groups :]
    me = me_ref[0]
    means, rstds = combine_moments(g_ref[...], counts_ref[:, 3:4, :], 0, 8, 8)
    st_ref[0:8, :] = means
    st_ref[8:16, :] = rstds
    st = st_ref[...]
    tile[...] = jnp.zeros_like(tile)
    for k, ref in enumerate(up_refs):
        shares[me ^ k] = ref[...].astype(F32)
    at = 0
    for unit, y_ref, dh_ref in zip(
        OUTER, (yd_ref, yw_ref, ys_ref, yp_ref), (dd_ref, dw_ref, ds_ref, dp_ref)
    ):
        mean, rstd = outer_stats(st, unit)
        scale, shift = affine_of(aff_ref, 1, unit)
        width = TILE_ROW[unit][1]
        own = width // groups
        for s in range(groups):
            up[:, s * own : (s + 1) * own] = shares[s, :, at : at + own]
        first, second = local_backward(
            y_ref, lambda rows: up[rows, :width], m_ref=mc_ref, mean=mean, rstd=rstd, scale=scale,
            shift=shift, dh_ref=dh_ref, out_ref=out, rows=clips * LATE.clip_rows,
        )
        for s in range(groups):
            shares[s, :, at : at + own] = out[:, s * own : (s + 1) * own]
        at += own
        put_row(tile, TILE_ROW[unit][0], first)
        put_row(tile, 8 + TILE_ROW[unit][0], second)
    for k, ref in enumerate(o_refs):
        ref[...] = shares[me ^ k].astype(BF16)
    send_tile(pay_ref, tile)


def finish_rows(dh, y, masking, mean, rstd, scale, scale_sum, shift_sum, count):
    xhat = (y - mean) * rstd
    return scale * rstd * (dh - (shift_sum + xhat * scale_sum) / count) * masking


def finish_kernel(
    geo, clips, g_ref, st_ref, str_ref, aff_ref, dw_ref, ds_ref, yw_ref, ys_ref, m_ref,
    gw_ref, gs_ref, sums_ref
):
    rows = clips * geo.clip_rows
    sums_ref[...] = jnp.sum(g_ref[...], axis=0)
    sums, st = sums_ref[...], st_ref[...]
    count = str_ref[2:3, 0:1]
    for unit, d_ref, y_ref, o_ref in (("w", dw_ref, yw_ref, gw_ref), ("s", ds_ref, ys_ref, gs_ref)):
        first, width = TILE_ROW[unit]
        mean, rstd = outer_stats(st, unit)
        scale, _ = affine_of(aff_ref, geo.block, unit)
        scale_sum, shift_sum = row(sums, first, width), row(sums, 8 + first, width)

        def finish(r, carry):
            at = pl.ds(r, CHUNK)
            dy = finish_rows(
                d_ref[at, :], y_ref[at, :], wide_mask(m_ref, at, width), mean, rstd, scale, scale_sum,
                shift_sum, count,
            )
            o_ref[at, :] = dy.astype(BF16)
            return carry

        each_chunk(rows, finish)


def inner_backward_kernel(
    geo, clips, pack, str_ref, aff_ref, gw_ref, gs_ref, yr_ref, kw_ref, ks_ref, m_ref,
    dh_ref, pay_ref, pad_w, pad_s, kt_w, kt_s, dz, tile
):
    rows = clips * geo.clip_rows
    size = geo.frame_rows
    st_r = str_ref[...]
    for width, g_ref, pad in ((WIDE, gw_ref, pad_w), (SPREAD, gs_ref, pad_s)):
        masks = edge_masks(geo, width)
        for c in range(clips):
            base = c * geo.padded_rows
            clear_edges(geo, pad, c)

            def store(j, placed):
                at = slice(base + size, base + size + geo.clip_rows)
                pad[at, width * j : width * (j + 1)] = placed.astype(BF16)

            value = g_ref[c * geo.clip_rows : (c + 1) * geo.clip_rows, :].astype(F32)
            gather_cells(geo, value, masks, -1, store)
    for k_ref, kt, own, width, depth in (
        (kw_ref, kt_w, pack.wide, WIDE, NARROW), (ks_ref, kt_s, pack.spread, SPREAD, SQUEEZE)
    ):
        for t in range(3):
            whole = whole_kernel(k_ref, t, own)
            for j in range(9):
                kt[t, width * j : width * (j + 1), :] = whole[:, depth * j : depth * (j + 1)]
    for pad, kt, depth, start in ((pad_w, kt_w, NARROW, 0), (pad_s, kt_s, SQUEEZE, NARROW)):
        for c in range(clips):
            base = c * geo.padded_rows
            total = None
            for t in range(3):
                at = base + size * (2 - t)
                term = nn(pad[at : at + geo.clip_rows, :], kt[t])
                total = term if total is None else total + term
            dz[c * geo.clip_rows : (c + 1) * geo.clip_rows, start : start + depth] = total
    scale, shift = affine_of(aff_ref, geo.block, "r")
    first, second = local_backward(
        yr_ref, lambda at: dz[at, :], m_ref=m_ref, mean=row(st_r, 0, REDUCED),
        rstd=row(st_r, 4, REDUCED), scale=scale, shift=shift, dh_ref=dh_ref, out_ref=None, rows=rows,
    )
    tile[...] = jnp.zeros_like(tile)
    put_row(tile, 0, first)
    put_row(tile, 4, second)
    send_tile(pay_ref, tile)


def kernel_grad_kernel(
    geo, clips, pack, halves, me_ref, gw_ref, gs_ref, bn_ref, bs_ref, *refs
):
    send_ref, grad_w, grad_s = refs[-3:]
    keep_refs = refs[-4:-3] if halves else ()
    for source, target in zip(refs[:-4], (*keep_refs, send_ref)):
        target[:, pack.kernels : pack.kernels + source.shape[1], :] = source[...]
    size = geo.frame_rows
    for g_ref, b_ref, grad in ((gw_ref, bn_ref, grad_w), (gs_ref, bs_ref, grad_s)):
        for t in range(3):
            total = None
            for c in range(clips):
                at = c * geo.padded_rows + size * t
                term = tn(
                    g_ref[c * geo.clip_rows : (c + 1) * geo.clip_rows, :],
                    b_ref[at : at + geo.clip_rows, :],
                )
                total = term if total is None else total + term
            grad[t] = total
    me = me_ref[0]
    for k in range(pack.groups):
        target, place = ((*keep_refs, send_ref)[k % 2], k // 2) if halves else (send_ref, me ^ k)
        for at, own, wide, t, u, _ in pack.kernel_tiles():
            source = grad_w if wide else grad_s
            first = pl.multiple_of((me ^ k) * own, 8)
            part = source[t, pl.ds(first, own), 128 * u : 128 * u + 128]
            target[place, at : at + own, :] = part.astype(BF16)


def point_grad_kernel(pack, me_ref, gy_ref, a_ref, keep_ref, send_ref, whole, shares):
    whole[...] = tn(gy_ref[...], a_ref[...])
    for s in range(pack.groups):
        for at, begin, own in pack.point_parts():
            shares[s, at : at + own, : pack.features] = whole[begin + s * own : begin + (s + 1) * own, :]
    for k in range(pack.groups):
        target = (keep_ref, send_ref)[k % 2]
        for at, u, width in pack.point_blocks(0):
            target[k // 2, at : at + pack.point, :] = shares[
                me_ref[0] ^ k, : pack.point, 128 * u : 128 * u + 128
            ].astype(BF16)


def halve_kernel(keep_ref, got_ref, even_ref, odd_ref):
    for q in range(keep_ref.shape[0]):
        target = (even_ref, odd_ref)[q % 2]
        target[q // 2] = (keep_ref[q].astype(F32) + got_ref[q].astype(F32)).astype(BF16)


def add_kernel(keep_ref, got_ref, o_ref):
    o_ref[...] = (keep_ref[0].astype(F32) + got_ref[0].astype(F32)).astype(BF16)


def scatter_halves_kernel(mb_ref, x_ref, even_ref, odd_ref, held):
    held[...] = x_ref[...].astype(F32)
    size = even_ref.shape[1]
    for k in range(2 * even_ref.shape[0]):
        first = pl.multiple_of((mb_ref[0] ^ k) * size, 8)
        (even_ref, odd_ref)[k % 2][k // 2] = held[pl.ds(first, size), :].astype(BF16)


def total_kernel(*refs):
    *x_refs, o_ref = refs
    at = 0
    for x_ref in x_refs:
        total = x_ref[0].astype(F32)
        for k in range(1, x_ref.shape[0]):
            total = total + x_ref[k].astype(F32)
        size = x_ref.shape[1]
        o_ref[:, at : at + size, :] = jnp.broadcast_to(
            total.astype(BF16)[None], (o_ref.shape[0],) + total.shape
        )
        at += size


def read_kernels(pack, rows, w_ref, s_ref, turned):
    for at, own, wide, t, u, width in pack.kernel_tiles():
        target, columns = (w_ref, 9 * NARROW) if wide else (turned, 9 * SQUEEZE)
        start = columns * t + 128 * u
        target[:, start : start + width] = rows[at : at + own, :width].astype(F32)
    s_ref[...] = jnp.transpose(turned[...])


def read_points(pack, start, rows, o_refs):
    for at, u, width in pack.point_blocks(start):
        block = rows[at : at + pack.point, :].astype(F32)
        for (first, _, own), o_ref in zip(pack.point_parts(), o_refs):
            o_ref[:, 128 * u : 128 * u + width] = block[first : first + own, :width]


def late_gradients_kernel(pack, batches, mb_ref, *refs):
    x_refs = refs[:batches]
    w_ref, s_ref, held, turned = refs[batches:]
    for k, x_ref in enumerate(x_refs):
        held[mb_ref[0] ^ k] = x_ref[...]
    read_kernels(pack, held[...].reshape(-1, 128), w_ref, s_ref, turned)


def early_gradients_kernel(pack, late_pack, size, x_ref, late_ref, w_ref, s_ref, *refs):
    *o_refs, wide, turned = refs
    rows = x_ref[:, :size, :].reshape(-1, 128)
    read_kernels(pack, rows, wide, s_ref, turned)
    read_points(late_pack, pack.kernels, rows, o_refs[len(o_refs) // 2 :])
    read_points(pack, 0, x_ref[:, size:, :].reshape(-1, 128), o_refs[: len(o_refs) // 2])

    def join(g, carry):
        parts = []
        for r in range(4):
            at = pl.ds(4 * g + r, 1)
            parts.append(jnp.concatenate([wide[at, :], late_ref[at, :]], axis=0))
        first = pl.multiple_of(4 * WIDE_COLUMNS * g, 128)
        w_ref[:, pl.ds(first, 4 * WIDE_COLUMNS)] = jnp.concatenate(parts, axis=1)
        return carry

    lax.fori_loop(0, pack.wide // 4, join, 0)


def point_gradients(
    geo, clips, g_ref, sums_ref, st_ref, str_ref, aff_ref, dr_ref, dd_ref, dp_ref, yr_ref, yd_ref,
    yp_ref, m_ref, gy_ref, sumr_ref, held
):
    rows = clips * geo.clip_rows
    sumr_ref[...] = jnp.sum(g_ref[...], axis=0)
    sums, sums_r, st, st_r = sums_ref[...], sumr_ref[...], st_ref[...], str_ref[...]
    count = st_r[2:3, 0:1]
    scale_d, _ = affine_of(aff_ref, geo.block, "d")
    scale_r, _ = affine_of(aff_ref, geo.block, "r")
    scale_p, _ = affine_of(aff_ref, geo.block, "p")
    mean_d, rstd_d = outer_stats(st, "d")
    mean_p, rstd_p = outer_stats(st, "p")
    mean_r, rstd_r = row(st_r, 0, REDUCED), row(st_r, 4, REDUCED)

    def pair(unit):
        first, width = TILE_ROW[unit]
        return row(sums, first, width), row(sums, 8 + first, width)

    pair_d, pair_p = pair("d"), pair("p")
    pair_r = (row(sums_r, 0, REDUCED), row(sums_r, 4, REDUCED))

    def finish(r, carry):
        at = pl.ds(r, CHUNK)
        gy_ref[at, :DIRECT] = finish_rows(
            dd_ref[at, :], yd_ref[at, :], wide_mask(m_ref, at, DIRECT), mean_d, rstd_d, scale_d, *pair_d, count
        ).astype(BF16)
        gy_ref[at, DIRECT : DIRECT + REDUCED] = finish_rows(
            dr_ref[at, :], yr_ref[at, :], wide_mask(m_ref, at, REDUCED), mean_r, rstd_r, scale_r, *pair_r, count
        ).astype(BF16)
        held[at, :] = finish_rows(
            dp_ref[at, :], yp_ref[at, :], m_ref[at, :], mean_p, rstd_p, scale_p, *pair_p, count
        )
        return carry

    each_chunk(rows, finish)
    masks = edge_masks(geo, PROJECT)
    for c in range(clips):
        at = slice(c * geo.clip_rows, (c + 1) * geo.clip_rows)
        gy_ref[at, DIRECT + REDUCED :] = mean_cells(geo, held[at, :], masks).astype(BF16)


def late_input_kernel(
    clips, g_ref, sums_ref, st_ref, str_ref, aff_ref, dr_ref, dd_ref, dp_ref, yr_ref, yd_ref, yp_ref,
    mc_ref, wt_ref, spread_ref, est_ref, ed_ref, ew_ref, es_ref, ep_ref, m_ref,
    gy_ref, hd_ref, hw_ref, hs_ref, hp_ref, pay_ref, sumr_ref, held, grad, wide, tile
):
    point_gradients(
        LATE, clips, g_ref, sums_ref, st_ref, str_ref, aff_ref, dr_ref, dd_ref, dp_ref, yr_ref,
        yd_ref, yp_ref, mc_ref, gy_ref, sumr_ref, held,
    )
    grad[...] = nn(gy_ref[...], wt_ref[...]).astype(BF16)
    st = est_ref[...]
    tile[...] = jnp.zeros_like(tile)
    column = 0
    for unit, y_ref, dh_ref in zip(
        OUTER, (ed_ref, ew_ref, es_ref, ep_ref), (hd_ref, hw_ref, hs_ref, hp_ref)
    ):
        width = TILE_ROW[unit][1]
        for c in range(clips):
            wide[c * EARLY.clip_rows : (c + 1) * EARLY.clip_rows, :width] = nn(
                spread_ref[...],
                grad[c * LATE.clip_rows : (c + 1) * LATE.clip_rows, column : column + width],
            )
        column += width
        mean, rstd = outer_stats(st, unit)
        scale, shift = affine_of(aff_ref, 0, unit)
        sums = local_backward(
            y_ref, lambda at: wide[at, :width], m_ref=m_ref, mean=mean, rstd=rstd, scale=scale,
            shift=shift, dh_ref=dh_ref, out_ref=None, rows=clips * EARLY.clip_rows,
        )
        put_row(tile, TILE_ROW[unit][0], sums[0])
        put_row(tile, 8 + TILE_ROW[unit][0], sums[1])
    send_tile(pay_ref, tile)


def early_input_kernel(
    pack, clips, me_ref, g_ref, sums_ref, st_ref, str_ref, aff_ref, dr_ref, dd_ref, dp_ref, yr_ref,
    yd_ref, yp_ref, m_ref, wt_ref, gy_ref, *refs
):
    x_refs = refs[: pack.groups]
    sumr_ref, held, turned = refs[pack.groups :]
    point_gradients(
        EARLY, clips, g_ref, sums_ref, st_ref, str_ref, aff_ref, dr_ref, dd_ref, dp_ref, yr_ref,
        yd_ref, yp_ref, m_ref, gy_ref, sumr_ref, held,
    )
    depth = turned.shape[1]
    rows = clips * EARLY.clip_rows
    for j in range(0, rows, 128):
        size = min(128, rows - j)
        grad = jnp.transpose(nn(gy_ref[j : j + size, :], wt_ref[...]) * wide_mask(m_ref, slice(j, j + size), wt_ref.shape[1]))
        for s in range(pack.groups):
            turned[s, :, j : j + size] = grad[s * depth : (s + 1) * depth, :].astype(BF16)
    for k, x_ref in enumerate(x_refs):
        x_ref[...] = turned[me_ref[0] ^ k]


def feature_kernel(pack, me_ref, *refs):
    *x_refs, o_ref, held = refs
    for k, x_ref in enumerate(x_refs):
        held[me_ref[0] ^ k] = x_ref[...]
    width = held.shape[2]
    for s in range(pack.groups):
        o_ref[:, s * width : (s + 1) * width] = held[s].astype(F32)


def pool_matrix():
    matrix = np.zeros((LATE.clip_rows, EARLY.clip_rows), np.float32)
    for f in range(EARLY.frames):
        for h in range(EARLY.height):
            for w in range(EARLY.width):
                cell = (f // 2) * LATE.frame_rows + (h // 2) * LATE.pitch + w // 2
                matrix[cell, (f * EARLY.height + h) * EARLY.width + w] = 0.125
    return matrix


def pad_late(field):
    padded = jnp.pad(field, ((0, 0), (0, 0), (0, 0), (0, LATE.pitch - LATE.width), (0, 0)))
    return padded.reshape(-1, field.shape[4])


def shards(
    clip_features, visible, direct_early, narrow_early, squeeze_early, project_early, direct_late,
    narrow_late, squeeze_late, project_late, wide_kernels, spread_kernels, direct_norm, narrow_norm,
    wide_norm, squeeze_norm, spread_norm, project_norm, upstream_direct, upstream_wide,
    upstream_spread, upstream_project,
):
    groups = lax.axis_size("ch")
    batches = lax.axis_size("batch")
    devices = groups * batches
    me = lax.axis_index("ch")
    me_ref = jnp.reshape(me, (1,)).astype(jnp.int32)
    held_clips = visible.shape[0]
    clips = held_clips // groups
    rows = clips * EARLY.clip_rows
    late_rows = clips * LATE.clip_rows
    depth = clip_features.shape[0]
    features = depth * groups
    pack = Packing(groups, features)
    late_pack = Packing(groups, CONCAT)

    def exchange(payload):
        return lax.all_to_all(payload, BOTH, 0, 0)

    def swap(value, bit):
        return lax.ppermute(value, "ch", [(i, i ^ bit) for i in range(groups)])

    class Shares:
        def __init__(self, own):
            self.pieces, self.bit = {0: own}, groups // 2
            self.step()

        def step(self):
            for k in list(self.pieces):
                self.pieces[k | self.bit] = swap(self.pieces[k], self.bit)
            self.bit //= 2

        def all(self, *behind):
            if behind:
                last = max(self.pieces)
                self.pieces[last] = ordered(self.pieces[last], *behind)
            while self.bit:
                self.step()
            return [self.pieces[k] for k in range(groups)]

    early_parts = (direct_early, narrow_early, squeeze_early, project_early)
    late_parts = (direct_late, narrow_late, squeeze_late, project_late)
    norms = (direct_norm, narrow_norm, squeeze_norm, wide_norm, spread_norm, project_norm)
    norm_rows = jnp.concatenate(norms, axis=2).reshape(4, -1)
    norm_space = padded16(4 * -(-norm_rows.shape[1] // 128))
    pieces, early_points = call(
        lambda *refs: prepare_kernel(pack, *refs),
        [((groups, depth, rows), BF16), ((pack.points + norm_space, 128), BF16)],
        [clip_features, norm_rows] + [part.T for part in early_parts],
        [((pack.point_rows, pack.point_tiles * 128), F32), ((norm_space, 128), F32)],
        us=2.5,
    )
    arrived = lax.all_to_all(pieces, "ch", 0, 0)
    point_shares = Shares(early_points).all()
    flat_rows = wide_kernels.shape[1] // 128
    halves = call(split_kernel, [((flat_rows, 128), BF16)] * 2, [wide_kernels, pieces], us=4.8, idle=1)
    spread_rows = jnp.transpose(
        spread_kernels.reshape(2, SPREAD_COLUMNS, spread_kernels.shape[3]), (0, 2, 1)
    )

    def packed(use, block, behind):
        return call(
            lambda *refs: pack_kernel(use, *refs),
            [((use.kernels, 128), BF16)],
            [halves[block].reshape(-1, WIDE_COLUMNS), spread_rows[block]] + list(behind),
            us=2.5,
            idle=len(behind),
        )[0]

    early_shares = Shares(ordered(packed(pack, 0, ()), point_shares[-1], arrived)).all()
    own_visible = lax.dynamic_slice_in_dim(visible, me * clips, clips, 0)
    fine = own_visible.astype(F32).reshape(rows, 1)
    mask = jnp.broadcast_to(fine, (rows, 128))
    cells = own_visible.reshape(clips, 2, 2, 6, 2, 6, 2).max(axis=(2, 4, 6)).astype(F32)
    coarse = jnp.broadcast_to(pad_late(cells[..., None]), (late_rows, 128))

    upstream = (upstream_direct, upstream_wide, upstream_spread, upstream_project)
    up_rows = pad_late(jnp.concatenate(upstream, axis=4))
    up_pieces = call(
        cut_kernel, [((late_rows, up_rows.shape[1]), BF16)] * groups, [me_ref, up_rows], us=1
    )
    up_pieces = [up_pieces[0]] + [swap(up_pieces[k], k) for k in range(1, groups)]

    pool = jnp.asarray(pool_matrix(), BF16)
    spread_back = jnp.asarray(pool_matrix().T, BF16)

    act, wt, affine, yr, pay = call(
        lambda *refs: early_first_kernel(pack, *refs),
        [
            ((rows, features), BF16), ((POINT, features), BF16), ((4, SLOTS), F32),
            ((rows, REDUCED), F32), ((devices, 8, 128), F32),
        ],
        [me_ref, arrived] + point_shares + [mask, coarse],
        [
            ((features, rows), F32), ((groups, pack.point_rows, pack.point_tiles * 128), F32),
            ((POINT, features), F32), ((groups, norm_space, 128), F32), ((8, 128), F32),
        ],
        us=8.6,
    )
    (late_points_own,) = call(
        lambda *refs: pack_late_kernel(late_pack, *refs),
        [((late_pack.points, 128), BF16)],
        [part.T for part in late_parts] + [act],
        [((late_pack.point_rows, late_pack.point_tiles * 128), F32)],
        us=1.5,
        idle=1,
    )
    late_own = packed(pack, 1, (act,))
    counts = exchange(pay)
    late_point_shares = Shares(ordered(late_points_own, counts)).all()
    late_shares = Shares(ordered(late_own, late_point_shares[groups // 2]))
    yd, yp, tile = call(
        lambda *refs: other_points_kernel(EARLY, clips, *refs),
        [((rows, DIRECT), F32), ((rows, PROJECT), F32), ((16, 128), F32)],
        [act, wt, mask],
        us=12,
    )

    def second(geo, count_row, g, y, masking, pieces, other, behind=()):
        own = clips * geo.clip_rows
        padded = clips * geo.padded_rows
        return call(
            lambda *refs: second_kernel(geo, clips, pack, count_row, *refs),
            [
                ((padded, 128 * WIDE_TILES), BF16), ((padded, 128 * SPREAD_TILES), BF16),
                ((own, WIDE), F32), ((own, SPREAD), F32),
                ((3, groups, pack.wide_rows, 128 * WIDE_TILES), BF16),
                ((3, groups, pack.spread_rows, 128 * SPREAD_TILES), BF16),
                ((devices, 16, 128), F32), ((8, 128), F32),
            ],
            [me_ref, g, counts, affine, y, masking, other] + pieces + list(behind),
            [((own, REDUCED), F32), ((16, 128), F32)],
            idle=len(behind),
            us=25 if geo is EARLY else 9,
        )

    bn, bs, yw, ys, kw, ks, pay, st_r = second(
        EARLY, 2, counts, yr, mask, early_shares, tile, (late_own,)
    )
    g = exchange(pay)
    late_act, late_wt, lyr, pay, st = call(
        lambda *refs: pool_kernel(late_pack, clips, *refs),
        [
            ((late_rows, CONCAT), BF16), ((POINT, CONCAT), BF16), ((late_rows, REDUCED), F32),
            ((devices, 8, 128), F32), ((16, 128), F32),
        ],
        [me_ref, g, counts, affine, yd, yw, ys, yp, mask, pool, coarse] + late_point_shares,
        [
            ((rows, 384), BF16), ((rows, 384), BF16),
            ((groups, late_pack.point_rows, late_pack.point_tiles * 128), F32),
            ((POINT, CONCAT), F32), ((8, 128), F32),
        ],
        us=15,
    )
    g = exchange(pay)
    lyd, lyp, tile = call(
        lambda *refs: other_points_kernel(LATE, clips, *refs),
        [((late_rows, DIRECT), F32), ((late_rows, PROJECT), F32), ((16, 128), F32)],
        [late_act, late_wt, coarse],
        us=3.7,
    )
    late_shares = late_shares.all(g)
    lbn, lbs, lyw, lys, lkw, lks, pay, lst_r = second(LATE, 3, g, lyr, coarse, late_shares, tile)
    g = exchange(pay)
    widths = [TILE_ROW[unit][1] for unit in OUTER]
    res = call(
        lambda *refs: late_outputs_kernel(clips, groups, *refs),
        [(up_pieces[0].shape, BF16)] * groups
        + [((late_rows, w), F32) for w in widths]
        + [((devices, 16, 128), F32), ((16, 128), F32)],
        [me_ref, g, counts, affine, lyd, lyw, lys, lyp, coarse] + up_pieces,
        [
            ((groups,) + up_pieces[0].shape, F32), ((late_rows, WIDE), F32), ((late_rows, WIDE), F32),
            ((16, 128), F32),
        ],
        us=4,
    )
    outs, (hd, hw, hs, hp), (pay, lst) = res[:groups], res[groups : groups + 4], res[groups + 4 :]
    g = exchange(pay)

    outs = [outs[0]] + [swap(outs[k], k) for k in range(1, groups)]

    def finish(geo, g, st, st_r, hw, hs, yw, ys, masking, behind=()):
        own = clips * geo.clip_rows
        return call(
            lambda *refs: finish_kernel(geo, clips, *refs),
            [((own, WIDE), BF16), ((own, SPREAD), BF16), ((16, 128), F32)],
            [g, st, st_r, affine, hw, hs, yw, ys, masking] + list(behind),
            idle=len(behind),
            us=7 if geo is EARLY else 2.5,
        )

    def inner(geo, st_r, gw, gs, yr, kw, ks, masking, behind=()):
        own = clips * geo.clip_rows
        padded = clips * geo.padded_rows
        return call(
            lambda *refs: inner_backward_kernel(geo, clips, pack, *refs),
            [((own, REDUCED), F32), ((devices, 8, 128), F32)],
            [st_r, affine, gw, gs, yr, kw, ks, masking] + list(behind),
            [
                ((padded, 9 * WIDE), BF16), ((padded, 9 * SPREAD), BF16),
                ((3, 9 * WIDE, NARROW), BF16), ((3, 9 * SPREAD, SQUEEZE), BF16),
                ((own, REDUCED), F32), ((8, 128), F32),
            ],
            idle=len(behind),
            us=16 if geo is EARLY else 5.6,
        )

    unit = 16 * batches

    def kernel_grads(geo, size, gw, gs, bn, bs, halves, others=()):
        outs = [(groups // 2, size, 128)] * 2 if halves else [(groups, size, 128)]
        return call(
            lambda *refs: kernel_grad_kernel(geo, clips, pack, halves, *refs),
            [(shape, BF16) for shape in outs],
            [me_ref, gw, gs, bn, bs] + list(others),
            [((3, WIDE, 128 * WIDE_TILES), F32), ((3, SPREAD, 128 * SPREAD_TILES), F32)],
            us=10 if geo is EARLY else 5,
        )

    def point_grads(use, size, gy, act, behind=()):
        return call(
            lambda *refs: point_grad_kernel(use, *refs),
            [((groups // 2, size, 128), BF16)] * 2,
            [me_ref, gy, act] + list(behind),
            [((POINT, use.features), F32), ((groups, use.point_rows, use.point_tiles * 128), F32)],
            us=4.5,
            idle=len(behind),
        )

    class Reduction:
        def __init__(self, keep, send):
            self.keep, self.bit = keep, 1
            self.got = swap(send, 1)

        def halve(self, *behind):
            while 2 * self.bit < groups:
                shape = (self.keep.shape[0] // 2,) + self.keep.shape[1:]
                self.keep, send = call(
                    halve_kernel, [(shape, BF16)] * 2, [self.keep, self.got] + list(behind),
                    idle=len(behind),
                    us=2.5,
                )
                self.bit *= 2
                self.got = swap(send, self.bit)
            return self.keep

        def add(self, *behind):
            return call(
                add_kernel, [(self.keep.shape[1:], BF16)], [self.keep, self.got] + list(behind),
                idle=len(behind),
                us=2,
            )[0]

    mb_ref = jnp.reshape(lax.axis_index("batch"), (1,)).astype(jnp.int32)

    def batch_swap(value, bit):
        return lax.ppermute(value, "batch", [(i, i ^ bit) for i in range(batches)])

    def whole_units(size):
        return -(-size // unit) * unit

    gw, gs, late_sums = finish(LATE, g, lst, lst_r, hw, hs, lyw, lys, coarse)
    hr, pay = inner(LATE, lst_r, gw, gs, lyr, lkw, lks, coarse)
    g = exchange(pay)
    (late_kernels,) = kernel_grads(
        LATE, whole_units(pack.kernels), gw, gs, lbn, lbs, False
    )
    late_share = lax.psum_scatter(late_kernels, "ch", scatter_dimension=0)
    (out_arrived,) = call(
        join_kernel,
        [((groups,) + outs[0].shape, BF16)],
        [me_ref] + outs,
        us=1,
    )
    gy, ed, ew, es, ep, pay, late_sums_r = call(
        lambda *refs: late_input_kernel(clips, *refs),
        [((late_rows, POINT), BF16)]
        + [((rows, w), F32) for w in widths]
        + [((devices, 16, 128), F32), ((8, 128), F32)],
        [g, late_sums, lst, lst_r, affine, hr, hd, hp, lyr, lyd, lyp, coarse, late_wt, spread_back,
         st, yd, yw, ys, yp, mask, late_kernels, out_arrived],
        [((late_rows, PROJECT), F32), ((late_rows, CONCAT), BF16), ((rows, WIDE), F32), ((16, 128), F32)],
        idle=2,
        us=15,
    )
    g = exchange(pay)
    late_points = point_grads(late_pack, late_pack.points, gy, late_act)
    gw, gs, sums = finish(EARLY, g, st, st_r, ew, es, yw, ys, mask, late_points[1:])
    early_size = whole_units(pack.kernels + late_pack.points)
    halves = kernel_grads(EARLY, early_size, gw, gs, bn, bs, True, late_points)
    early_sum = Reduction(*halves)

    class BatchHalves(Reduction):
        def __init__(self, keep, send):
            self.keep, self.bit = keep, 1
            self.got = batch_swap(send, 1)

        def step(self, *behind):
            shape = (self.keep.shape[0] // 2,) + self.keep.shape[1:]
            self.keep, send = call(
                halve_kernel, [(shape, BF16)] * 2, [self.keep, self.got] + list(behind),
                idle=len(behind), us=1.5,
            )
            self.bit *= 2
            self.got = batch_swap(send, self.bit)
            return self.keep

        def spread(self, *behind):
            own = self.add(*behind)
            self.pieces, self.bit = {0: own}, batches // 2
            return own

        def double(self):
            got = {k | self.bit: batch_swap(self.pieces[k], self.bit) for k in self.pieces}
            self.pieces.update(got)
            self.bit //= 2
            return list(got.values())

    late_piece = late_share.shape[0] // batches
    late_halves = call(
        scatter_halves_kernel,
        [((batches // 2, late_piece, 128), BF16)] * 2,
        [mb_ref, late_share, halves[1]],
        [(late_share.shape, F32)],
        us=3,
        idle=1,
    )
    late_sum = BatchHalves(*late_halves)
    kept = early_sum.halve(late_halves[1])
    hr, pay = inner(EARLY, st_r, gw, gs, yr, kw, ks, mask, behind=(kept,))
    g = exchange(pay)
    late_kept = late_sum.step(hr)
    own = early_sum.add(late_kept)
    parts = lax.all_to_all(own.reshape(batches, -1, 128), "batch", 0, 0)
    late_kept = own
    while 2 * late_sum.bit < batches:
        late_kept = late_sum.step(own)
    gy, *x_parts, sums_r = call(
        lambda *refs: early_input_kernel(pack, clips, *refs),
        [((rows, POINT), BF16)] + [((depth, rows), BF16)] * groups + [((8, 128), F32)],
        [me_ref, g, sums, st, st_r, affine, hr, ed, ep, yr, yd, yp, mask, wt, late_kept],
        [((rows, PROJECT), F32), ((groups, depth, rows), BF16)],
        idle=1,
        us=8.5,
    )
    x_parts = [x_parts[0]] + [swap(x_parts[k], k) for k in range(1, groups)]
    late_own = late_sum.spread(gy)
    point_halves = point_grads(pack, whole_units(pack.points), gy, act, (late_own,))
    point_sum = Reduction(*point_halves)
    kept = point_sum.halve()
    got = late_sum.double()
    point_own = point_sum.add(parts, *got)
    point_parts = lax.all_to_all(point_own.reshape(batches, -1, 128), "batch", 0, 0)
    (feature_grad,) = call(
        lambda *refs: feature_kernel(pack, *refs),
        [((depth, groups * rows), F32)],
        [me_ref] + x_parts + [point_own],
        [((groups, depth, rows), BF16)],
        idle=1,
        us=2,
    )
    while late_sum.bit > 1:
        got = late_sum.double()
    kernels_size, points_size = parts.shape[1], point_parts.shape[1]
    (parts,) = call(
        total_kernel,
        [((batches, kernels_size + points_size, 128), BF16)],
        [parts, point_parts, feature_grad] + got,
        us=2,
        idle=1 + len(got),
    )
    early_total = lax.all_to_all(parts, "batch", 0, 0)
    while late_sum.bit:
        late_sum.double()
    late_pieces = [late_sum.pieces[k] for k in range(batches)]
    late_wide, late_spread = call(
        lambda *refs: late_gradients_kernel(pack, batches, *refs),
        [((pack.wide, WIDE_COLUMNS), F32), ((SPREAD_COLUMNS, pack.spread), F32)],
        [mb_ref] + late_pieces,
        [((batches, late_piece, 128), BF16), ((pack.spread, SPREAD_COLUMNS), F32)],
        us=4,
    )
    out_arrived = out_arrived.reshape(
        held_clips, LATE.frames, LATE.height, LATE.pitch, -1
    )[:, :, :, : LATE.width]
    outputs, at = [], 0
    for part in upstream:
        outputs.append(out_arrived[..., at : at + part.shape[4]])
        at += part.shape[4]

    wide_grad, early_spread, *point_outs = call(
        lambda *refs: early_gradients_kernel(pack, late_pack, kernels_size, *refs),
        [(wide_kernels.shape, F32), ((SPREAD_COLUMNS, pack.spread), F32)]
        + [(part.shape[::-1], F32) for part in early_parts + late_parts],
        [early_total, late_wide],
        [((pack.wide, WIDE_COLUMNS), F32), ((pack.spread, SPREAD_COLUMNS), F32)],
        us=8,
    )
    point_outs = [part.T for part in point_outs]
    spread_grad = jnp.stack(
        [part.reshape(spread_kernels.shape[1:]) for part in (early_spread, late_spread)]
    )

    def outer_pair(tile, unit):
        first, width = TILE_ROW[unit]
        return jnp.stack([tile[k : k + 3].reshape(-1)[:width] for k in (first, first + 8)])

    def inner_pair(tile, low, high):
        return jnp.stack([tile[k : k + 2].reshape(-1)[low:high] for k in (0, 4)])

    def own_part(early_pair, late_pair):
        both = jnp.stack([early_pair, late_pair])
        size = both.shape[2] // groups
        return lax.dynamic_slice_in_dim(both, me * size, size, 2)

    norm_grads = [
        own_part(outer_pair(sums, "d"), outer_pair(late_sums, "d")),
        own_part(inner_pair(sums_r, 0, NARROW), inner_pair(late_sums_r, 0, NARROW)),
        own_part(outer_pair(sums, "w"), outer_pair(late_sums, "w")),
        own_part(inner_pair(sums_r, NARROW, REDUCED), inner_pair(late_sums_r, NARROW, REDUCED)),
        own_part(outer_pair(sums, "s"), outer_pair(late_sums, "s")),
        own_part(outer_pair(sums, "p"), outer_pair(late_sums, "p")),
    ]
    return tuple(outputs) + (feature_grad,) + tuple(point_outs) + (
        wide_grad, spread_grad,
    ) + tuple(norm_grads)


def solution(mesh):
    columns = P(None, "ch")
    norm = P(None, None, "ch")
    clips = P("batch", None, None, None, "ch")
    kernels = P(None, None, None, "ch")
    return jax.shard_map(
        shards,
        mesh=mesh,
        in_specs=(P("ch", "batch"), P("batch", None, None, None)) + (columns,) * 9 + (kernels,)
        + (norm,) * 6 + (clips,) * 4,
        out_specs=(clips,) * 4 + (P("ch", "batch"),) + (columns,) * 9 + (kernels,) + (norm,) * 6,
        check_vma=False,
    )
```

```python
import jax
import jax.numpy as jnp
import numpy as np
from jax import lax
from jax.experimental import pallas as pl
from jax.experimental.pallas import tpu as pltpu
from jax.sharding import PartitionSpec as P

F32 = jnp.float32
BF16 = jnp.bfloat16
EPSILON = 0.001
FLOPS_A_US = 1.1e9
BOTH = ("batch", "ch")
DIRECT, NARROW, WIDE, SQUEEZE, SPREAD, PROJECT = 256, 160, 320, 32, 128, 128
REDUCED = NARROW + SQUEEZE
POINT = DIRECT + REDUCED + PROJECT
CONCAT = DIRECT + WIDE + SPREAD + PROJECT
WIDE_COLUMNS = 27 * NARROW
SPREAD_COLUMNS = 27 * SQUEEZE
POINT_WIDTHS = (DIRECT, NARROW, SQUEEZE, PROJECT)
SLOT = {"d": (0, DIRECT), "r": (256, REDUCED), "w": (512, WIDE), "s": (896, SPREAD), "p": (1024, PROJECT)}
SLOTS = 1152
NORM_ORDER = ((0, DIRECT), (256, NARROW), (256 + NARROW, SQUEEZE), (512, WIDE), (896, SPREAD), (1024, PROJECT))
TILE_ROW = {"d": (0, DIRECT), "w": (2, WIDE), "s": (5, SPREAD), "p": (6, PROJECT)}
OUTER = ("d", "w", "s", "p")
SUMS = {
    "w": ((0, 0), (0, 320), WIDE), "s": ((0, 640), (0, 768), SPREAD), "p": ((0, 896), (1, 896), PROJECT),
    "d": ((1, 384), (1, 640), DIRECT), "r": ((1, 0), (1, 192), REDUCED),
}
CHUNK = 96


class Geometry:
    def __init__(self, frames, height, width, pitch, block):
        self.frames, self.height, self.width, self.pitch = frames, height, width, pitch
        self.block = block
        self.frame_rows = height * pitch
        self.clip_rows = frames * self.frame_rows
        self.padded_rows = (frames + 2) * self.frame_rows
        self.dense = pitch == width


EARLY = Geometry(4, 12, 12, 12, 0)
LATE = Geometry(2, 6, 6, 8, 1)


def nt(a, b):
    return lax.dot_general(a, b, (((1,), (1,)), ((), ())), preferred_element_type=F32)


def nn(a, b):
    return lax.dot_general(a, b, (((1,), (0,)), ((), ())), preferred_element_type=F32)


def tn(a, b):
    return lax.dot_general(a, b, (((0,), (0,)), ((), ())), preferred_element_type=F32)


def call(kernel, outs, ins, scratch=(), us=0, idle=0):
    moved = sum(int(np.prod(s)) * jnp.dtype(d).itemsize for s, d in outs)
    moved += sum(int(np.prod(x.shape)) * x.dtype.itemsize for x in ins[: len(ins) - idle])

    def spec(k, x):
        if k >= len(ins) - idle:
            return pl.BlockSpec(memory_space=pl.ANY)
        return pl.BlockSpec(memory_space=pltpu.SMEM if x.ndim == 1 else pltpu.VMEM)

    def body(*refs):
        kept = len(ins) - idle
        kernel(*refs[:kept], *refs[len(ins) :])

    return pl.pallas_call(
        body,
        out_shape=[jax.ShapeDtypeStruct(s, d) for s, d in outs],
        in_specs=[spec(k, x) for k, x in enumerate(ins)],
        out_specs=[pl.BlockSpec(memory_space=pltpu.VMEM)] * len(outs),
        scratch_shapes=[pltpu.VMEM(s, d) for s, d in scratch],
        compiler_params=pltpu.CompilerParams(vmem_limit_bytes=56 * 2**20),
        cost_estimate=pl.CostEstimate(
            flops=int(us * FLOPS_A_US) or 10 * moved, bytes_accessed=moved, transcendentals=0
        ),
    )(*ins)


def ordered(value, *behind):
    anywhere = pl.BlockSpec(memory_space=pl.ANY)
    return pl.pallas_call(
        lambda *refs: None,
        out_shape=jax.ShapeDtypeStruct(value.shape, value.dtype),
        in_specs=[anywhere] * (1 + len(behind)),
        out_specs=anywhere,
        input_output_aliases={0: 0},
    )(value, *behind)


def each_chunk(rows, body, init=0, chunk=CHUNK):
    return lax.fori_loop(
        0, rows // chunk, lambda i, carry: body(pl.multiple_of(i * chunk, chunk), carry), init
    )


def wide_mask(m_ref, at, width):
    part = m_ref[at, :]
    if width <= 128:
        return part[:, :width]
    return jnp.concatenate([part] * -(-width // 128), axis=1)[:, :width]


def row(tile, first, width):
    pieces = [
        tile[first + i : first + i + 1, : min(128, width - 128 * i)] for i in range(-(-width // 128))
    ]
    return pieces[0] if len(pieces) == 1 else jnp.concatenate(pieces, axis=1)


def put_row(ref, first, vector):
    width = vector.shape[1]
    for i in range(-(-width // 128)):
        part = vector[:, 128 * i : min(128 * (i + 1), width)]
        ref[first + i : first + i + 1, : part.shape[1]] = part


def put_sums(tiles, unit, sums):
    for (which, start), vector in zip(SUMS[unit][:2], sums):
        at = 0
        while at < vector.shape[1]:
            r, lane = divmod(start + at, 128)
            size = min(128 - lane, vector.shape[1] - at)
            tiles[which][r : r + 1, lane : lane + size] = vector[:, at : at + size]
            at += size


def get_sums(tiles, unit):
    sums = []
    for which, start in SUMS[unit][:2]:
        pieces, at = [], 0
        while at < SUMS[unit][2]:
            r, lane = divmod(start + at, 128)
            size = min(128 - lane, SUMS[unit][2] - at)
            pieces.append(tiles[which][r : r + 1, lane : lane + size])
            at += size
        sums.append(pieces[0] if len(pieces) == 1 else jnp.concatenate(pieces, axis=1))
    return sums


def affine_of(aff_ref, block, unit):
    start, width = SLOT[unit]
    return (
        aff_ref[2 * block : 2 * block + 1, start : start + width],
        aff_ref[2 * block + 1 : 2 * block + 2, start : start + width],
    )


def fold8(value):
    total = value[0:8]
    for i in range(1, value.shape[0] // 8):
        total = total + value[8 * i : 8 * i + 8]
    return total


def local_moments(y_ref, m_ref, rows, count):
    width = y_ref.shape[1]

    def first(r, acc):
        at = pl.ds(r, CHUNK)
        return acc + fold8(y_ref[at, :] * wide_mask(m_ref, at, width))

    total = each_chunk(rows, first, jnp.zeros((8, width), F32))
    mean = jnp.sum(total, axis=0, keepdims=True) / count

    def second(r, acc):
        at = pl.ds(r, CHUNK)
        centred = (y_ref[at, :] - mean) * wide_mask(m_ref, at, width)
        return acc + fold8(centred * centred)

    spread = each_chunk(rows, second, jnp.zeros((8, width), F32))
    return mean, jnp.sum(spread, axis=0, keepdims=True)


def combine_moments(payload, counts, first, second, size):
    means = payload[:, first : first + size, :]
    total = jnp.sum(counts, axis=0)
    mean = jnp.sum(means * counts, axis=0) / total
    offset = means - mean[None]
    spread = jnp.sum(payload[:, second : second + size, :] + counts * offset * offset, axis=0)
    return mean, lax.rsqrt(spread / total + EPSILON)


def send_tile(pay_ref, tile_ref):
    pay_ref[...] = jnp.broadcast_to(tile_ref[...][None], pay_ref.shape)


def shifted(value, offset):
    if offset == 0:
        return value
    return pltpu.roll(value, (-offset) % value.shape[0], 0)


def cell_index(geo, shape):
    r = lax.broadcasted_iota(jnp.int32, shape, 0).astype(F32)
    line = jnp.floor((r + 0.5) * (1.0 / geo.pitch))
    column = r - geo.pitch * line
    frame = jnp.floor((line + 0.5) * (1.0 / geo.height))
    return line - geo.height * frame, column


def edge_masks(geo, width):
    line, column = cell_index(geo, (geo.clip_rows, width))
    return (
        {e: (line + e > -0.5) & (line + e < geo.height - 0.5) for e in (-1, 1)},
        {e: (column + e > -0.5) & (column + e < geo.width - 0.5) for e in (-1, 1)},
    )


def gather_cells(geo, value, masks, sign, store):
    lines, columns = masks
    for b, dw in enumerate((-1, 0, 1)):
        moved = shifted(value, sign * dw)
        if dw and geo.dense:
            moved = jnp.where(columns[sign * dw], moved, 0.0)
        for a, dh in enumerate((-1, 0, 1)):
            placed = shifted(moved, sign * dh * geo.pitch)
            if dh:
                placed = jnp.where(lines[sign * dh], placed, 0.0)
            store(3 * a + b, placed)


def frame_shift(geo, value, offset):
    if offset == 0:
        return value
    size = geo.frame_rows
    blank = jnp.zeros((size, value.shape[1]), value.dtype)
    if offset > 0:
        return jnp.concatenate([value[size:], blank], axis=0)
    return jnp.concatenate([blank, value[:-size]], axis=0)


def mean_cells(geo, value, masks):
    lines, columns = masks
    total = value
    for e in (-1, 1):
        moved = shifted(value, e)
        total = total + (jnp.where(columns[e], moved, 0.0) if geo.dense else moved)
    again = total
    for e in (-1, 1):
        again = again + jnp.where(lines[e], shifted(total, e * geo.pitch), 0.0)
    return (again + frame_shift(geo, again, 1) + frame_shift(geo, again, -1)) / 27.0


def clear_edges(geo, ref, clip):
    base = clip * geo.padded_rows
    size = geo.frame_rows
    blank = jnp.zeros((size, ref.shape[1]), ref.dtype)
    ref[base : base + size, :] = blank
    ref[base + geo.padded_rows - size : base + geo.padded_rows, :] = blank


def padded16(size):
    return -(-size // 16) * 16


class Packing:
    def __init__(self, groups, features):
        self.groups = groups
        self.wide, self.spread, self.point = WIDE // groups, SPREAD // groups, POINT // groups
        self.wide_rows = padded16(self.wide)
        self.spread_rows = padded16(self.spread)
        self.point_rows = padded16(self.point)
        self.kernels = 3 * WIDE_TILES * self.wide_rows + 3 * SPREAD_TILES * self.spread_rows
        self.features = features
        self.point_tiles = -(-features // 128)
        self.points = self.point_tiles * self.point_rows

    def kernel_tiles(self):
        at = 0
        for own, size, tiles, columns, wide in (
            (self.wide, self.wide_rows, WIDE_TILES, 9 * NARROW, True),
            (self.spread, self.spread_rows, SPREAD_TILES, 9 * SQUEEZE, False),
        ):
            for t in range(3):
                for u in range(tiles):
                    yield at, own, wide, t, u, min(128, columns - 128 * u)
                    at += size

    def point_blocks(self, start):
        for u in range(self.point_tiles):
            yield start + u * self.point_rows, u, min(128, self.features - 128 * u)

    def point_parts(self):
        at = start = 0
        for width in POINT_WIDTHS:
            own = width // self.groups
            yield at, start, own
            at += own
            start += width


WIDE_TILES = -(-9 * NARROW // 128)
SPREAD_TILES = -(-9 * SQUEEZE // 128)


def fit_tile(value):
    width = value.shape[1]
    if width == 128:
        return value
    return jnp.concatenate([value, jnp.zeros((value.shape[0], 128 - width), value.dtype)], axis=1)


def pack_points(pack, part_refs, o_ref, start, scratch):
    for (at, _, own), ref in zip(pack.point_parts(), part_refs):
        scratch[at : at + own, : pack.features] = ref[...].astype(F32)
    for at, u, width in pack.point_blocks(start):
        o_ref[at : at + pack.point, :] = fit_tile(
            scratch[: pack.point, 128 * u : 128 * u + width].astype(BF16)
        )


def unpack_points(pack, me, piece_refs, start, raw, scratch, wt_ref):
    for k, ref in enumerate(piece_refs):
        for at, u, width in pack.point_blocks(start):
            raw[me ^ k, : pack.point, 128 * u : 128 * u + width] = ref[at : at + pack.point, :width].astype(F32)
    for s in range(pack.groups):
        for at, begin, own in pack.point_parts():
            scratch[begin + s * own : begin + (s + 1) * own, :] = raw[s, at : at + own, : pack.features]
    wt_ref[...] = scratch[...].astype(BF16)


def unpack_kernels(pack, me, piece_refs, kw_ref, ks_ref):
    for k, ref in enumerate(piece_refs):
        for at, own, wide, t, u, _ in pack.kernel_tiles():
            target = kw_ref if wide else ks_ref
            size = target.shape[2]
            target[t, me ^ k, :, 128 * u : 128 * u + 128] = ref[at : at + size, :]


def whole_kernel(ref, t, own):
    if own == ref.shape[2]:
        return ref[t].reshape(ref.shape[1] * own, ref.shape[3])
    parts = [ref[t, s].astype(F32)[:own] for s in range(ref.shape[1])]
    return jnp.concatenate(parts, axis=0).astype(BF16)


def prepare_kernel(pack, x_ref, norm_ref, p0, p1, p2, p3, o_ref, b_ref, scratch, rows):
    width = o_ref.shape[2]
    for s in range(pack.groups):
        o_ref[s] = x_ref[:, s * width : (s + 1) * width]
    pack_points(pack, (p0, p1, p2, p3), b_ref, 0, scratch)
    rows[...] = jnp.zeros_like(rows)
    for u in range(-(-norm_ref.shape[1] // 128)):
        part = norm_ref[:, 128 * u : 128 * (u + 1)].astype(F32)
        rows[4 * u : 4 * u + 4, : part.shape[1]] = part
    b_ref[pack.points :, :] = rows[...].astype(BF16)


def split_kernel(x_ref, a_ref, b_ref):
    tiles = x_ref.shape[1] // 128

    def move(first, count):
        value = x_ref[:, pl.ds(128 * first, 128 * count)].astype(F32)
        for r, ref in ((0, a_ref), (1, b_ref)):
            parts = [value[r : r + 1, 128 * j : 128 * (j + 1)] for j in range(count)]
            ref[pl.ds(first, count), :] = jnp.concatenate(parts, axis=0).astype(BF16)

    def step(i, carry):
        move(pl.multiple_of(16 * i, 16), 16)
        return carry

    lax.fori_loop(0, tiles // 16, step, 0)
    if tiles % 16:
        move(tiles // 16 * 16, tiles % 16)


def pack_kernel(pack, w_ref, s_ref, o_ref):
    for at, own, wide, t, u, width in pack.kernel_tiles():
        source, columns = (w_ref, 9 * NARROW) if wide else (s_ref, 9 * SQUEEZE)
        start = columns * t + 128 * u
        o_ref[at : at + own, :] = fit_tile(source[:, start : start + width])


def pack_late_kernel(pack, p0, p1, p2, p3, o_ref, scratch):
    pack_points(pack, (p0, p1, p2, p3), o_ref, 0, scratch)


def early_first_kernel(
    pack, me_ref, x_ref, *refs
):
    groups = pack.groups
    piece_refs = refs[:groups]
    m_ref, mc_ref, a_ref, wt_ref, aff_ref, y_ref, pay_ref, xs, raw, ws, norm_raw, tile = refs[groups:]
    me = me_ref[0]
    depth, rows = x_ref.shape[1], x_ref.shape[2]
    for s in range(groups):
        xs[s * depth : (s + 1) * depth, :] = x_ref[s].astype(F32)
    for j in range(0, rows, 128):
        size = min(128, rows - j)
        turned = jnp.transpose(xs[:, j : j + size])
        a_ref[j : j + size, :] = (turned * wide_mask(m_ref, slice(j, j + size), turned.shape[1])).astype(BF16)
    unpack_points(pack, me, piece_refs, 0, raw, ws, wt_ref)
    for k, ref in enumerate(piece_refs):
        norm_raw[me ^ k] = ref[pack.points :, :].astype(F32)
    at = 0
    for slot, whole in NORM_ORDER:
        own = whole // groups
        for s in range(groups):
            left, u = at % 128, at // 128
            first = min(own, 128 - left)
            to = slot + s * own
            aff_ref[:, to : to + first] = norm_raw[s, 4 * u : 4 * u + 4, left : left + first]
            if first < own:
                aff_ref[:, to + first : to + own] = norm_raw[s, 4 * u + 4 : 4 * u + 8, : own - first]
        at += own
    y_ref[...] = nt(a_ref[...], wt_ref[DIRECT : DIRECT + REDUCED, :])
    tile[...] = jnp.zeros_like(tile)
    count = jnp.sum(m_ref[...], axis=0, keepdims=True)
    coarse = jnp.sum(mc_ref[...], axis=0, keepdims=True)
    mean, spread = local_moments(y_ref, m_ref, rows, count[:, 0:1])
    put_row(tile, 0, mean)
    put_row(tile, 2, count)
    put_row(tile, 3, coarse)
    put_row(tile, 4, spread)
    send_tile(pay_ref, tile)


def other_points_kernel(geo, clips, a_ref, wt_ref, m_ref, yd_ref, yp_ref, tile):
    yd_ref[...] = nt(a_ref[...], wt_ref[:DIRECT, :])
    projected = nt(a_ref[...], wt_ref[DIRECT + REDUCED :, :])
    masks = edge_masks(geo, PROJECT)
    for c in range(clips):
        rows = slice(c * geo.clip_rows, (c + 1) * geo.clip_rows)
        yp_ref[rows, :] = mean_cells(geo, projected[rows], masks)
    tile[...] = jnp.zeros_like(tile)
    count = jnp.sum(m_ref[...], axis=0, keepdims=True)[:, 0:1]
    for unit, ref in (("d", yd_ref), ("p", yp_ref)):
        mean, spread = local_moments(ref, m_ref, clips * geo.clip_rows, count)
        put_row(tile, TILE_ROW[unit][0], mean)
        put_row(tile, 8 + TILE_ROW[unit][0], spread)


def second_kernel(
    geo, clips, pack, count_row, me_ref, g_ref, counts_ref, aff_ref, y_ref, m_ref, pd_ref, *refs
):
    piece_refs = refs[: pack.groups]
    (bn_ref, bs_ref, yw_ref, ys_ref, kw_ref, ks_ref, pay_ref, st_ref, us, tile) = refs[pack.groups :]
    unpack_kernels(pack, me_ref[0], piece_refs, kw_ref, ks_ref)
    rows = clips * geo.clip_rows
    counts = counts_ref[:, count_row : count_row + 1, :]
    means, rstds = combine_moments(g_ref[...], counts, 0, 4, 2)
    st_ref[...] = jnp.zeros_like(st_ref)
    st_ref[0:2, :] = means
    st_ref[2:3, :] = jnp.sum(counts, axis=0)
    st_ref[4:6, :] = rstds
    mean, rstd = row(means, 0, REDUCED), row(rstds, 0, REDUCED)
    scale, shift = affine_of(aff_ref, geo.block, "r")

    def activate(r, carry):
        at = pl.ds(r, CHUNK)
        h = scale * ((y_ref[at, :] - mean) * rstd) + shift
        us[at, :] = h * jax.nn.sigmoid(h) * wide_mask(m_ref, at, REDUCED)
        return carry

    each_chunk(rows, activate)
    masks = edge_masks(geo, REDUCED)
    size = geo.frame_rows
    for c in range(clips):
        base = c * geo.padded_rows
        clear_edges(geo, bn_ref, c)
        clear_edges(geo, bs_ref, c)
        inside = slice(base + size, base + size + geo.clip_rows)
        for ref, used in ((bn_ref, 9 * NARROW), (bs_ref, 9 * SQUEEZE)):
            ref[inside, used:] = jnp.zeros((geo.clip_rows, ref.shape[1] - used), BF16)

        def store(j, placed):
            at = slice(base + size, base + size + geo.clip_rows)
            bn_ref[at, NARROW * j : NARROW * (j + 1)] = placed[:, :NARROW].astype(BF16)
            bs_ref[at, SQUEEZE * j : SQUEEZE * (j + 1)] = placed[:, NARROW:].astype(BF16)

        gather_cells(geo, us[c * geo.clip_rows : (c + 1) * geo.clip_rows, :], masks, 1, store)
    for c in range(clips):
        base = c * geo.padded_rows
        out = slice(c * geo.clip_rows, (c + 1) * geo.clip_rows)
        for b_ref, k_ref, o_ref, own in (
            (bn_ref, kw_ref, yw_ref, pack.wide), (bs_ref, ks_ref, ys_ref, pack.spread)
        ):
            total = None
            for t in range(3):
                term = nt(
                    b_ref[base + size * t : base + size * t + geo.clip_rows, :],
                    whole_kernel(k_ref, t, own),
                )
                total = term if total is None else total + term
            o_ref[out, :] = total
    tile[...] = pd_ref[...]
    own = jnp.sum(m_ref[...], axis=0, keepdims=True)[:, 0:1]
    for unit, ref in (("w", yw_ref), ("s", ys_ref)):
        mean, spread = local_moments(ref, m_ref, rows, own)
        put_row(tile, TILE_ROW[unit][0], mean)
        put_row(tile, 8 + TILE_ROW[unit][0], spread)
    send_tile(pay_ref, tile)


def outer_stats(st, unit):
    first, width = TILE_ROW[unit]
    return row(st, first, width), row(st, 8 + first, width)


def pool_kernel(
    pack, clips, me_ref, g_ref, counts_ref, aff_ref, yd_ref, yw_ref, ys_ref, yp_ref, m_ref, pool_ref,
    mc_ref, *refs
):
    piece_refs = refs[: pack.groups]
    a_ref, wt_ref, y_ref, pay_ref, st_ref, high, low, raw, ws, tile = refs[pack.groups :]
    means, rstds = combine_moments(g_ref[...], counts_ref[:, 2:3, :], 0, 8, 8)
    st_ref[0:8, :] = means
    st_ref[8:16, :] = rstds
    st = st_ref[...]
    at_column = 0
    for unit, ref in zip(OUTER, (yd_ref, yw_ref, ys_ref, yp_ref)):
        width = TILE_ROW[unit][1]
        mean, rstd = outer_stats(st, unit)
        scale, shift = affine_of(aff_ref, 0, unit)

        def activate(r, carry):
            at = pl.ds(r, CHUNK)
            h = scale * ((ref[at, :] - mean) * rstd) + shift
            u = h * jax.nn.sigmoid(h) * wide_mask(m_ref, at, width)
            top = u.astype(BF16)
            high[at, :width] = top
            low[at, :width] = (u - top.astype(F32)).astype(BF16)
            return carry

        each_chunk(clips * EARLY.clip_rows, activate)
        for c in range(clips):
            rows = slice(c * EARLY.clip_rows, (c + 1) * EARLY.clip_rows)
            pooled = nn(pool_ref[...], high[rows, :width]) + nn(pool_ref[...], low[rows, :width])
            out = slice(c * LATE.clip_rows, (c + 1) * LATE.clip_rows)
            a_ref[out, at_column : at_column + width] = pooled.astype(BF16)
        at_column += width
    unpack_points(pack, me_ref[0], piece_refs, 0, raw, ws, wt_ref)
    y_ref[...] = nt(a_ref[...], wt_ref[DIRECT : DIRECT + REDUCED, :])
    tile[...] = jnp.zeros_like(tile)
    own = jnp.sum(mc_ref[...], axis=0, keepdims=True)
    mean, spread = local_moments(y_ref, mc_ref, clips * LATE.clip_rows, own[:, 0:1])
    put_row(tile, 0, mean)
    put_row(tile, 4, spread)
    send_tile(pay_ref, tile)


def local_backward(y_ref, dz_of, m_ref, mean, rstd, scale, shift, dh_ref, out_ref, rows):
    width = y_ref.shape[1]

    def body(r, carry):
        at = pl.ds(r, CHUNK)
        masking = wide_mask(m_ref, at, width)
        xhat = (y_ref[at, :] - mean) * rstd
        h = scale * xhat + shift
        gate = jax.nn.sigmoid(h)
        if out_ref is not None:
            out_ref[at, :width] = (h * gate * masking).astype(out_ref.dtype)
        dh = dz_of(at) * masking * gate * (1.0 + h * (1.0 - gate))
        dh_ref[at, :] = dh
        return carry[0] + fold8(dh * xhat), carry[1] + fold8(dh)

    blank = jnp.zeros((8, width), F32)
    first, second = each_chunk(rows, body, (blank, blank))
    return jnp.sum(first, axis=0, keepdims=True), jnp.sum(second, axis=0, keepdims=True)


def cut_kernel(me_ref, x_ref, *o_refs):
    size = o_refs[0].shape[0]
    for k, o_ref in enumerate(o_refs):
        o_ref[...] = x_ref[pl.ds(pl.multiple_of((me_ref[0] ^ k) * size, 16), size), :]


def join_kernel(me_ref, *refs):
    *x_refs, o_ref = refs
    for k, x_ref in enumerate(x_refs):
        o_ref[me_ref[0] ^ k] = x_ref[...]


def late_outputs_kernel(
    clips, groups, me_ref, g_ref, counts_ref, aff_ref, yd_ref, yw_ref, ys_ref, yp_ref, mc_ref, *refs
):
    up_refs, o_refs = refs[:groups], refs[groups : 2 * groups]
    dd_ref, dw_ref, ds_ref, dp_ref, pay_ref, rest_ref, st_ref, shares, up, out, tile = refs[2 * groups :]
    me = me_ref[0]
    means, rstds = combine_moments(g_ref[...], counts_ref[:, 3:4, :], 0, 8, 8)
    st_ref[0:8, :] = means
    st_ref[8:16, :] = rstds
    st = st_ref[...]
    tile[...] = jnp.zeros_like(tile)
    rest_ref[...] = jnp.zeros_like(rest_ref)
    for k, ref in enumerate(up_refs):
        shares[me ^ k] = ref[...].astype(F32)
    at = 0
    for unit, y_ref, dh_ref in zip(
        OUTER, (yd_ref, yw_ref, ys_ref, yp_ref), (dd_ref, dw_ref, ds_ref, dp_ref)
    ):
        mean, rstd = outer_stats(st, unit)
        scale, shift = affine_of(aff_ref, 1, unit)
        width = TILE_ROW[unit][1]
        own = width // groups
        for s in range(groups):
            up[:, s * own : (s + 1) * own] = shares[s, :, at : at + own]
        sums = local_backward(
            y_ref, lambda rows: up[rows, :width], m_ref=mc_ref, mean=mean, rstd=rstd, scale=scale,
            shift=shift, dh_ref=dh_ref, out_ref=out, rows=clips * LATE.clip_rows,
        )
        for s in range(groups):
            shares[s, :, at : at + own] = out[:, s * own : (s + 1) * own]
        at += own
        put_sums((tile, rest_ref), unit, sums)
    for k, ref in enumerate(o_refs):
        ref[...] = shares[me ^ k].astype(BF16)
    send_tile(pay_ref, tile)


def finish_rows(dh, y, masking, mean, rstd, scale, scale_sum, shift_sum, count):
    xhat = (y - mean) * rstd
    return scale * rstd * (dh - (shift_sum + xhat * scale_sum) / count) * masking


def finish_kernel(
    geo, clips, g_ref, st_ref, str_ref, aff_ref, dw_ref, ds_ref, yw_ref, ys_ref, m_ref,
    gw_ref, gs_ref, sums_ref
):
    rows = clips * geo.clip_rows
    sums_ref[...] = jnp.sum(g_ref[...], axis=0)
    sums, st = sums_ref[...], st_ref[...]
    count = str_ref[2:3, 0:1]
    for unit, d_ref, y_ref, o_ref in (("w", dw_ref, yw_ref, gw_ref), ("s", ds_ref, ys_ref, gs_ref)):
        first, width = TILE_ROW[unit]
        mean, rstd = outer_stats(st, unit)
        scale, _ = affine_of(aff_ref, geo.block, unit)
        scale_sum, shift_sum = get_sums((sums,), unit)

        def finish(r, carry):
            at = pl.ds(r, CHUNK)
            dy = finish_rows(
                d_ref[at, :], y_ref[at, :], wide_mask(m_ref, at, width), mean, rstd, scale, scale_sum,
                shift_sum, count,
            )
            o_ref[at, :] = dy.astype(BF16)
            return carry

        each_chunk(rows, finish)


def inner_backward_kernel(
    geo, clips, pack, str_ref, aff_ref, gw_ref, gs_ref, yr_ref, kw_ref, ks_ref, m_ref, rest_ref,
    dh_ref, pay_ref, pad_w, pad_s, kt_w, kt_s, dz, tile
):
    rows = clips * geo.clip_rows
    size = geo.frame_rows
    st_r = str_ref[...]
    for width, g_ref, pad in ((WIDE, gw_ref, pad_w), (SPREAD, gs_ref, pad_s)):
        masks = edge_masks(geo, width)
        for c in range(clips):
            base = c * geo.padded_rows
            clear_edges(geo, pad, c)

            def store(j, placed):
                at = slice(base + size, base + size + geo.clip_rows)
                pad[at, width * j : width * (j + 1)] = placed.astype(BF16)

            value = g_ref[c * geo.clip_rows : (c + 1) * geo.clip_rows, :].astype(F32)
            gather_cells(geo, value, masks, -1, store)
    for k_ref, kt, own, width, depth in (
        (kw_ref, kt_w, pack.wide, WIDE, NARROW), (ks_ref, kt_s, pack.spread, SPREAD, SQUEEZE)
    ):
        for t in range(3):
            whole = whole_kernel(k_ref, t, own)
            for j in range(9):
                kt[t, width * j : width * (j + 1), :] = whole[:, depth * j : depth * (j + 1)]
    for pad, kt, depth, start in ((pad_w, kt_w, NARROW, 0), (pad_s, kt_s, SQUEEZE, NARROW)):
        for c in range(clips):
            base = c * geo.padded_rows
            total = None
            for t in range(3):
                at = base + size * (2 - t)
                term = nn(pad[at : at + geo.clip_rows, :], kt[t])
                total = term if total is None else total + term
            dz[c * geo.clip_rows : (c + 1) * geo.clip_rows, start : start + depth] = total
    scale, shift = affine_of(aff_ref, geo.block, "r")
    sums = local_backward(
        yr_ref, lambda at: dz[at, :], m_ref=m_ref, mean=row(st_r, 0, REDUCED),
        rstd=row(st_r, 4, REDUCED), scale=scale, shift=shift, dh_ref=dh_ref, out_ref=None, rows=rows,
    )
    tile[...] = rest_ref[...]
    put_sums((None, tile), "r", sums)
    send_tile(pay_ref, tile)


def kernel_grad_kernel(
    geo, clips, pack, halves, me_ref, gw_ref, gs_ref, bn_ref, bs_ref, *refs
):
    send_ref, grad_w, grad_s = refs[-3:]
    keep_refs = refs[-4:-3] if halves else ()
    for source, target in zip(refs[:-4], (*keep_refs, send_ref)):
        target[:, pack.kernels : pack.kernels + source.shape[1], :] = source[...]
    size = geo.frame_rows
    for g_ref, b_ref, grad in ((gw_ref, bn_ref, grad_w), (gs_ref, bs_ref, grad_s)):
        for t in range(3):
            total = None
            for c in range(clips):
                at = c * geo.padded_rows + size * t
                term = tn(
                    g_ref[c * geo.clip_rows : (c + 1) * geo.clip_rows, :],
                    b_ref[at : at + geo.clip_rows, :],
                )
                total = term if total is None else total + term
            grad[t] = total
    me = me_ref[0]
    for k in range(pack.groups):
        target, place = ((*keep_refs, send_ref)[k % 2], k // 2) if halves else (send_ref, me ^ k)
        for at, own, wide, t, u, _ in pack.kernel_tiles():
            source = grad_w if wide else grad_s
            first = pl.multiple_of((me ^ k) * own, 8)
            part = source[t, pl.ds(first, own), 128 * u : 128 * u + 128]
            target[place, at : at + own, :] = part.astype(BF16)


def point_grad_kernel(pack, me_ref, gy_ref, a_ref, keep_ref, send_ref, whole, shares):
    whole[...] = tn(gy_ref[...], a_ref[...])
    for s in range(pack.groups):
        for at, begin, own in pack.point_parts():
            shares[s, at : at + own, : pack.features] = whole[begin + s * own : begin + (s + 1) * own, :]
    for k in range(pack.groups):
        target = (keep_ref, send_ref)[k % 2]
        for at, u, width in pack.point_blocks(0):
            target[k // 2, at : at + pack.point, :] = shares[
                me_ref[0] ^ k, : pack.point, 128 * u : 128 * u + 128
            ].astype(BF16)


def halve_kernel(keep_ref, got_ref, even_ref, odd_ref):
    for q in range(keep_ref.shape[0]):
        target = (even_ref, odd_ref)[q % 2]
        target[q // 2] = (keep_ref[q].astype(F32) + got_ref[q].astype(F32)).astype(BF16)


def add_kernel(keep_ref, got_ref, o_ref):
    o_ref[...] = (keep_ref[0].astype(F32) + got_ref[0].astype(F32)).astype(BF16)


def scatter_halves_kernel(mb_ref, x_ref, even_ref, odd_ref, held):
    held[...] = x_ref[...].astype(F32)
    size = even_ref.shape[1]
    for k in range(2 * even_ref.shape[0]):
        first = pl.multiple_of((mb_ref[0] ^ k) * size, 8)
        (even_ref, odd_ref)[k % 2][k // 2] = held[pl.ds(first, size), :].astype(BF16)


def total_kernel(*refs):
    *x_refs, o_ref = refs
    at = 0
    for x_ref in x_refs:
        total = x_ref[0].astype(F32)
        for k in range(1, x_ref.shape[0]):
            total = total + x_ref[k].astype(F32)
        size = x_ref.shape[1]
        o_ref[:, at : at + size, :] = jnp.broadcast_to(
            total.astype(BF16)[None], (o_ref.shape[0],) + total.shape
        )
        at += size


def read_kernels(pack, rows, w_ref, s_ref, turned):
    for at, own, wide, t, u, width in pack.kernel_tiles():
        target, columns = (w_ref, 9 * NARROW) if wide else (turned, 9 * SQUEEZE)
        start = columns * t + 128 * u
        target[:, start : start + width] = rows[at : at + own, :width].astype(F32)
    s_ref[...] = jnp.transpose(turned[...])


def read_points(pack, start, rows, o_refs):
    for at, u, width in pack.point_blocks(start):
        block = rows[at : at + pack.point, :].astype(F32)
        for (first, _, own), o_ref in zip(pack.point_parts(), o_refs):
            o_ref[:, 128 * u : 128 * u + width] = block[first : first + own, :width]


def late_gradients_kernel(pack, batches, mb_ref, *refs):
    x_refs = refs[:batches]
    w_ref, s_ref, held, turned = refs[batches:]
    for k, x_ref in enumerate(x_refs):
        held[mb_ref[0] ^ k] = x_ref[...]
    read_kernels(pack, held[...].reshape(-1, 128), w_ref, s_ref, turned)


def early_gradients_kernel(pack, late_pack, size, x_ref, late_ref, w_ref, s_ref, *refs):
    *o_refs, wide, turned = refs
    rows = x_ref[:, :size, :].reshape(-1, 128)
    read_kernels(pack, rows, wide, s_ref, turned)
    read_points(late_pack, pack.kernels, rows, o_refs[len(o_refs) // 2 :])
    read_points(pack, 0, x_ref[:, size:, :].reshape(-1, 128), o_refs[: len(o_refs) // 2])

    def join(g, carry):
        parts = []
        for r in range(4):
            at = pl.ds(4 * g + r, 1)
            parts.append(jnp.concatenate([wide[at, :], late_ref[at, :]], axis=0))
        first = pl.multiple_of(4 * WIDE_COLUMNS * g, 128)
        w_ref[:, pl.ds(first, 4 * WIDE_COLUMNS)] = jnp.concatenate(parts, axis=1)
        return carry

    lax.fori_loop(0, pack.wide // 4, join, 0)


def point_gradients(
    geo, clips, g_ref, sums_ref, st_ref, str_ref, aff_ref, dr_ref, dd_ref, dp_ref, yr_ref, yd_ref,
    yp_ref, m_ref, gy_ref, sumr_ref, held
):
    rows = clips * geo.clip_rows
    sumr_ref[...] = jnp.sum(g_ref[...], axis=0)
    sums, sums_r, st, st_r = sums_ref[...], sumr_ref[...], st_ref[...], str_ref[...]
    count = st_r[2:3, 0:1]
    scale_d, _ = affine_of(aff_ref, geo.block, "d")
    scale_r, _ = affine_of(aff_ref, geo.block, "r")
    scale_p, _ = affine_of(aff_ref, geo.block, "p")
    mean_d, rstd_d = outer_stats(st, "d")
    mean_p, rstd_p = outer_stats(st, "p")
    mean_r, rstd_r = row(st_r, 0, REDUCED), row(st_r, 4, REDUCED)

    pair_d, pair_p, pair_r = (get_sums((sums, sums_r), unit) for unit in "dpr")

    def finish(r, carry):
        at = pl.ds(r, CHUNK)
        gy_ref[at, :DIRECT] = finish_rows(
            dd_ref[at, :], yd_ref[at, :], wide_mask(m_ref, at, DIRECT), mean_d, rstd_d, scale_d, *pair_d, count
        ).astype(BF16)
        gy_ref[at, DIRECT : DIRECT + REDUCED] = finish_rows(
            dr_ref[at, :], yr_ref[at, :], wide_mask(m_ref, at, REDUCED), mean_r, rstd_r, scale_r, *pair_r, count
        ).astype(BF16)
        held[at, :] = finish_rows(
            dp_ref[at, :], yp_ref[at, :], m_ref[at, :], mean_p, rstd_p, scale_p, *pair_p, count
        )
        return carry

    each_chunk(rows, finish)
    masks = edge_masks(geo, PROJECT)
    for c in range(clips):
        at = slice(c * geo.clip_rows, (c + 1) * geo.clip_rows)
        gy_ref[at, DIRECT + REDUCED :] = mean_cells(geo, held[at, :], masks).astype(BF16)


def late_input_kernel(
    clips, g_ref, sums_ref, st_ref, str_ref, aff_ref, dr_ref, dd_ref, dp_ref, yr_ref, yd_ref, yp_ref,
    mc_ref, wt_ref, spread_ref, est_ref, ed_ref, ew_ref, es_ref, ep_ref, m_ref,
    gy_ref, hd_ref, hw_ref, hs_ref, hp_ref, pay_ref, rest_ref, sumr_ref, held, grad, wide, tile
):
    point_gradients(
        LATE, clips, g_ref, sums_ref, st_ref, str_ref, aff_ref, dr_ref, dd_ref, dp_ref, yr_ref,
        yd_ref, yp_ref, mc_ref, gy_ref, sumr_ref, held,
    )
    grad[...] = nn(gy_ref[...], wt_ref[...]).astype(BF16)
    st = est_ref[...]
    tile[...] = jnp.zeros_like(tile)
    rest_ref[...] = jnp.zeros_like(rest_ref)
    column = 0
    for unit, y_ref, dh_ref in zip(
        OUTER, (ed_ref, ew_ref, es_ref, ep_ref), (hd_ref, hw_ref, hs_ref, hp_ref)
    ):
        width = TILE_ROW[unit][1]
        for c in range(clips):
            wide[c * EARLY.clip_rows : (c + 1) * EARLY.clip_rows, :width] = nn(
                spread_ref[...],
                grad[c * LATE.clip_rows : (c + 1) * LATE.clip_rows, column : column + width],
            )
        column += width
        mean, rstd = outer_stats(st, unit)
        scale, shift = affine_of(aff_ref, 0, unit)
        sums = local_backward(
            y_ref, lambda at: wide[at, :width], m_ref=m_ref, mean=mean, rstd=rstd, scale=scale,
            shift=shift, dh_ref=dh_ref, out_ref=None, rows=clips * EARLY.clip_rows,
        )
        put_sums((tile, rest_ref), unit, sums)
    send_tile(pay_ref, tile)


def early_input_kernel(
    pack, clips, me_ref, g_ref, sums_ref, st_ref, str_ref, aff_ref, dr_ref, dd_ref, dp_ref, yr_ref,
    yd_ref, yp_ref, m_ref, wt_ref, gy_ref, *refs
):
    x_refs = refs[: pack.groups]
    sumr_ref, held, turned = refs[pack.groups :]
    point_gradients(
        EARLY, clips, g_ref, sums_ref, st_ref, str_ref, aff_ref, dr_ref, dd_ref, dp_ref, yr_ref,
        yd_ref, yp_ref, m_ref, gy_ref, sumr_ref, held,
    )
    depth = turned.shape[1]
    rows = clips * EARLY.clip_rows
    for j in range(0, rows, 128):
        size = min(128, rows - j)
        grad = jnp.transpose(nn(gy_ref[j : j + size, :], wt_ref[...]) * wide_mask(m_ref, slice(j, j + size), wt_ref.shape[1]))
        for s in range(pack.groups):
            turned[s, :, j : j + size] = grad[s * depth : (s + 1) * depth, :].astype(BF16)
    for k, x_ref in enumerate(x_refs):
        x_ref[...] = turned[me_ref[0] ^ k]


def feature_kernel(pack, me_ref, *refs):
    *x_refs, o_ref, held = refs
    for k, x_ref in enumerate(x_refs):
        held[me_ref[0] ^ k] = x_ref[...]
    width = held.shape[2]
    for s in range(pack.groups):
        o_ref[:, s * width : (s + 1) * width] = held[s].astype(F32)


def pool_matrix():
    matrix = np.zeros((LATE.clip_rows, EARLY.clip_rows), np.float32)
    for f in range(EARLY.frames):
        for h in range(EARLY.height):
            for w in range(EARLY.width):
                cell = (f // 2) * LATE.frame_rows + (h // 2) * LATE.pitch + w // 2
                matrix[cell, (f * EARLY.height + h) * EARLY.width + w] = 0.125
    return matrix


def pad_late(field):
    padded = jnp.pad(field, ((0, 0), (0, 0), (0, 0), (0, LATE.pitch - LATE.width), (0, 0)))
    return padded.reshape(-1, field.shape[4])


def shards(
    clip_features, visible, direct_early, narrow_early, squeeze_early, project_early, direct_late,
    narrow_late, squeeze_late, project_late, wide_kernels, spread_kernels, direct_norm, narrow_norm,
    wide_norm, squeeze_norm, spread_norm, project_norm, upstream_direct, upstream_wide,
    upstream_spread, upstream_project,
):
    groups = lax.axis_size("ch")
    batches = lax.axis_size("batch")
    devices = groups * batches
    me = lax.axis_index("ch")
    me_ref = jnp.reshape(me, (1,)).astype(jnp.int32)
    held_clips = visible.shape[0]
    clips = held_clips // groups
    rows = clips * EARLY.clip_rows
    late_rows = clips * LATE.clip_rows
    depth = clip_features.shape[0]
    features = depth * groups
    pack = Packing(groups, features)
    late_pack = Packing(groups, CONCAT)

    def exchange(payload):
        return lax.all_to_all(payload, BOTH, 0, 0)

    def swap(value, bit):
        return lax.ppermute(value, "ch", [(i, i ^ bit) for i in range(groups)])

    class Shares:
        def __init__(self, own):
            self.pieces, self.bit = {0: own}, groups // 2
            self.step()

        def step(self):
            for k in list(self.pieces):
                self.pieces[k | self.bit] = swap(self.pieces[k], self.bit)
            self.bit //= 2

        def all(self, *behind):
            if behind:
                last = max(self.pieces)
                self.pieces[last] = ordered(self.pieces[last], *behind)
            while self.bit:
                self.step()
            return [self.pieces[k] for k in range(groups)]

    early_parts = (direct_early, narrow_early, squeeze_early, project_early)
    late_parts = (direct_late, narrow_late, squeeze_late, project_late)
    norms = (direct_norm, narrow_norm, squeeze_norm, wide_norm, spread_norm, project_norm)
    norm_rows = jnp.concatenate(norms, axis=2).reshape(4, -1)
    norm_space = padded16(4 * -(-norm_rows.shape[1] // 128))
    pieces, early_points = call(
        lambda *refs: prepare_kernel(pack, *refs),
        [((groups, depth, rows), BF16), ((pack.points + norm_space, 128), BF16)],
        [clip_features, norm_rows] + [part.T for part in early_parts],
        [((pack.point_rows, pack.point_tiles * 128), F32), ((norm_space, 128), F32)],
        us=2.5,
    )
    arrived = lax.all_to_all(pieces, "ch", 0, 0)
    point_shares = Shares(early_points).all()
    flat_rows = wide_kernels.shape[1] // 128
    halves = call(split_kernel, [((flat_rows, 128), BF16)] * 2, [wide_kernels, pieces], us=4.8, idle=1)
    spread_rows = jnp.transpose(
        spread_kernels.reshape(2, SPREAD_COLUMNS, spread_kernels.shape[3]), (0, 2, 1)
    )

    def packed(use, block, behind):
        return call(
            lambda *refs: pack_kernel(use, *refs),
            [((use.kernels, 128), BF16)],
            [halves[block].reshape(-1, WIDE_COLUMNS), spread_rows[block]] + list(behind),
            us=2.5,
            idle=len(behind),
        )[0]

    early_shares = Shares(ordered(packed(pack, 0, ()), point_shares[-1], arrived))
    own_visible = lax.dynamic_slice_in_dim(visible, me * clips, clips, 0)
    fine = own_visible.astype(F32).reshape(rows, 1)
    mask = jnp.broadcast_to(fine, (rows, 128))
    cells = own_visible.reshape(clips, 2, 2, 6, 2, 6, 2).max(axis=(2, 4, 6)).astype(F32)
    coarse = jnp.broadcast_to(pad_late(cells[..., None]), (late_rows, 128))

    upstream = (upstream_direct, upstream_wide, upstream_spread, upstream_project)
    up_rows = pad_late(jnp.concatenate(upstream, axis=4))
    up_pieces = call(
        cut_kernel, [((late_rows, up_rows.shape[1]), BF16)] * groups, [me_ref, up_rows], us=1
    )
    up_pieces = [up_pieces[0]] + [swap(up_pieces[k], k) for k in range(1, groups)]

    pool = jnp.asarray(pool_matrix(), BF16)
    spread_back = jnp.asarray(pool_matrix().T, BF16)

    act, wt, affine, yr, pay = call(
        lambda *refs: early_first_kernel(pack, *refs),
        [
            ((rows, features), BF16), ((POINT, features), BF16), ((4, SLOTS), F32),
            ((rows, REDUCED), F32), ((devices, 8, 128), F32),
        ],
        [me_ref, arrived] + point_shares + [mask, coarse],
        [
            ((features, rows), F32), ((groups, pack.point_rows, pack.point_tiles * 128), F32),
            ((POINT, features), F32), ((groups, norm_space, 128), F32), ((8, 128), F32),
        ],
        us=8.6,
    )
    (late_points_own,) = call(
        lambda *refs: pack_late_kernel(late_pack, *refs),
        [((late_pack.points, 128), BF16)],
        [part.T for part in late_parts] + [act],
        [((late_pack.point_rows, late_pack.point_tiles * 128), F32)],
        us=1.5,
        idle=1,
    )
    late_own = packed(pack, 1, (act,))
    counts = exchange(pay)
    late_point_shares = Shares(ordered(late_points_own, counts)).all()
    late_shares = Shares(ordered(late_own, late_point_shares[groups // 2]))
    yd, yp, tile = call(
        lambda *refs: other_points_kernel(EARLY, clips, *refs),
        [((rows, DIRECT), F32), ((rows, PROJECT), F32), ((16, 128), F32)],
        [act, wt, mask],
        us=12,
    )

    def second(geo, count_row, g, y, masking, pieces, other, behind=()):
        own = clips * geo.clip_rows
        padded = clips * geo.padded_rows
        return call(
            lambda *refs: second_kernel(geo, clips, pack, count_row, *refs),
            [
                ((padded, 128 * WIDE_TILES), BF16), ((padded, 128 * SPREAD_TILES), BF16),
                ((own, WIDE), F32), ((own, SPREAD), F32),
                ((3, groups, pack.wide_rows, 128 * WIDE_TILES), BF16),
                ((3, groups, pack.spread_rows, 128 * SPREAD_TILES), BF16),
                ((devices, 16, 128), F32), ((8, 128), F32),
            ],
            [me_ref, g, counts, affine, y, masking, other] + pieces + list(behind),
            [((own, REDUCED), F32), ((16, 128), F32)],
            idle=len(behind),
            us=25 if geo is EARLY else 9,
        )

    early_shares = early_shares.all(counts)
    bn, bs, yw, ys, kw, ks, pay, st_r = second(
        EARLY, 2, counts, yr, mask, early_shares, tile, (late_own,)
    )
    g = exchange(pay)
    late_act, late_wt, lyr, pay, st = call(
        lambda *refs: pool_kernel(late_pack, clips, *refs),
        [
            ((late_rows, CONCAT), BF16), ((POINT, CONCAT), BF16), ((late_rows, REDUCED), F32),
            ((devices, 8, 128), F32), ((16, 128), F32),
        ],
        [me_ref, g, counts, affine, yd, yw, ys, yp, mask, pool, coarse] + late_point_shares,
        [
            ((rows, 384), BF16), ((rows, 384), BF16),
            ((groups, late_pack.point_rows, late_pack.point_tiles * 128), F32),
            ((POINT, CONCAT), F32), ((8, 128), F32),
        ],
        us=15,
    )
    g = exchange(pay)
    lyd, lyp, tile = call(
        lambda *refs: other_points_kernel(LATE, clips, *refs),
        [((late_rows, DIRECT), F32), ((late_rows, PROJECT), F32), ((16, 128), F32)],
        [late_act, late_wt, coarse],
        us=3.7,
    )
    late_shares = late_shares.all(g)
    lbn, lbs, lyw, lys, lkw, lks, pay, lst_r = second(LATE, 3, g, lyr, coarse, late_shares, tile)
    g = exchange(pay)
    widths = [TILE_ROW[unit][1] for unit in OUTER]
    res = call(
        lambda *refs: late_outputs_kernel(clips, groups, *refs),
        [(up_pieces[0].shape, BF16)] * groups
        + [((late_rows, w), F32) for w in widths]
        + [((devices, 8, 128), F32), ((8, 128), F32), ((16, 128), F32)],
        [me_ref, g, counts, affine, lyd, lyw, lys, lyp, coarse] + up_pieces,
        [
            ((groups,) + up_pieces[0].shape, F32), ((late_rows, WIDE), F32), ((late_rows, WIDE), F32),
            ((8, 128), F32),
        ],
        us=4,
    )
    outs, (hd, hw, hs, hp), (pay, rest, lst) = res[:groups], res[groups : groups + 4], res[groups + 4 :]
    g = exchange(pay)

    outs = [outs[0]] + [swap(outs[k], k) for k in range(1, groups)]

    def finish(geo, g, st, st_r, hw, hs, yw, ys, masking, behind=()):
        own = clips * geo.clip_rows
        return call(
            lambda *refs: finish_kernel(geo, clips, *refs),
            [((own, WIDE), BF16), ((own, SPREAD), BF16), ((8, 128), F32)],
            [g, st, st_r, affine, hw, hs, yw, ys, masking] + list(behind),
            idle=len(behind),
            us=7 if geo is EARLY else 2.5,
        )

    def inner(geo, st_r, gw, gs, yr, kw, ks, masking, rest, behind=()):
        own = clips * geo.clip_rows
        padded = clips * geo.padded_rows
        return call(
            lambda *refs: inner_backward_kernel(geo, clips, pack, *refs),
            [((own, REDUCED), F32), ((devices, 8, 128), F32)],
            [st_r, affine, gw, gs, yr, kw, ks, masking, rest] + list(behind),
            [
                ((padded, 9 * WIDE), BF16), ((padded, 9 * SPREAD), BF16),
                ((3, 9 * WIDE, NARROW), BF16), ((3, 9 * SPREAD, SQUEEZE), BF16),
                ((own, REDUCED), F32), ((8, 128), F32),
            ],
            idle=len(behind),
            us=16 if geo is EARLY else 5.6,
        )

    unit = 16 * batches

    def kernel_grads(geo, size, gw, gs, bn, bs, halves, others=()):
        outs = [(groups // 2, size, 128)] * 2 if halves else [(groups, size, 128)]
        return call(
            lambda *refs: kernel_grad_kernel(geo, clips, pack, halves, *refs),
            [(shape, BF16) for shape in outs],
            [me_ref, gw, gs, bn, bs] + list(others),
            [((3, WIDE, 128 * WIDE_TILES), F32), ((3, SPREAD, 128 * SPREAD_TILES), F32)],
            us=10 if geo is EARLY else 5,
        )

    def point_grads(use, size, gy, act, behind=()):
        return call(
            lambda *refs: point_grad_kernel(use, *refs),
            [((groups // 2, size, 128), BF16)] * 2,
            [me_ref, gy, act] + list(behind),
            [((POINT, use.features), F32), ((groups, use.point_rows, use.point_tiles * 128), F32)],
            us=4.5,
            idle=len(behind),
        )

    class Reduction:
        def __init__(self, keep, send):
            self.keep, self.bit = keep, 1
            self.got = swap(send, 1)

        def halve(self, *behind):
            while 2 * self.bit < groups:
                shape = (self.keep.shape[0] // 2,) + self.keep.shape[1:]
                self.keep, send = call(
                    halve_kernel, [(shape, BF16)] * 2, [self.keep, self.got] + list(behind),
                    idle=len(behind),
                    us=2.5,
                )
                self.bit *= 2
                self.got = swap(send, self.bit)
            return self.keep

        def add(self, *behind):
            return call(
                add_kernel, [(self.keep.shape[1:], BF16)], [self.keep, self.got] + list(behind),
                idle=len(behind),
                us=2,
            )[0]

    mb_ref = jnp.reshape(lax.axis_index("batch"), (1,)).astype(jnp.int32)

    def batch_swap(value, bit):
        return lax.ppermute(value, "batch", [(i, i ^ bit) for i in range(batches)])

    def whole_units(size):
        return -(-size // unit) * unit

    gw, gs, late_sums = finish(LATE, g, lst, lst_r, hw, hs, lyw, lys, coarse)
    hr, pay = inner(LATE, lst_r, gw, gs, lyr, lkw, lks, coarse, rest)
    g = exchange(pay)
    (late_kernels,) = kernel_grads(
        LATE, whole_units(pack.kernels), gw, gs, lbn, lbs, False
    )
    late_share = lax.psum_scatter(ordered(late_kernels, g), "ch", scatter_dimension=0)
    gy, ed, ew, es, ep, pay, rest, late_sums_r = call(
        lambda *refs: late_input_kernel(clips, *refs),
        [((late_rows, POINT), BF16)]
        + [((rows, w), F32) for w in widths]
        + [((devices, 8, 128), F32), ((8, 128), F32), ((8, 128), F32)],
        [g, late_sums, lst, lst_r, affine, hr, hd, hp, lyr, lyd, lyp, coarse, late_wt, spread_back,
         st, yd, yw, ys, yp, mask, late_kernels],
        [((late_rows, PROJECT), F32), ((late_rows, CONCAT), BF16), ((rows, WIDE), F32), ((8, 128), F32)],
        idle=1,
        us=15,
    )
    g = exchange(pay)
    (out_arrived,) = call(
        join_kernel,
        [((groups,) + outs[0].shape, BF16)],
        [me_ref] + outs + [gy],
        us=1,
        idle=1,
    )
    late_points = point_grads(late_pack, late_pack.points, gy, late_act)
    gw, gs, sums = finish(
        EARLY, g, st, st_r, ew, es, yw, ys, mask, (late_points[1], out_arrived)
    )
    early_size = whole_units(pack.kernels + late_pack.points)
    halves = kernel_grads(EARLY, early_size, gw, gs, bn, bs, True, late_points)
    early_sum = Reduction(*halves)

    class BatchHalves(Reduction):
        def __init__(self, keep, send):
            self.keep, self.bit = keep, 1
            self.got = batch_swap(send, 1)

        def step(self, *behind):
            shape = (self.keep.shape[0] // 2,) + self.keep.shape[1:]
            self.keep, send = call(
                halve_kernel, [(shape, BF16)] * 2, [self.keep, self.got] + list(behind),
                idle=len(behind), us=1.5,
            )
            self.bit *= 2
            self.got = batch_swap(send, self.bit)
            return self.keep

        def spread(self, *behind):
            own = self.add(*behind)
            self.pieces, self.bit = {0: own}, batches // 2
            return own

        def double(self):
            got = {k | self.bit: batch_swap(self.pieces[k], self.bit) for k in self.pieces}
            self.pieces.update(got)
            self.bit //= 2
            return list(got.values())

    late_piece = late_share.shape[0] // batches
    late_halves = call(
        scatter_halves_kernel,
        [((batches // 2, late_piece, 128), BF16)] * 2,
        [mb_ref, late_share, halves[1]],
        [(late_share.shape, F32)],
        us=3,
        idle=1,
    )
    late_sum = BatchHalves(*late_halves)
    kept = early_sum.halve(late_halves[1])
    hr, pay = inner(EARLY, st_r, gw, gs, yr, kw, ks, mask, rest, behind=(kept,))
    g = exchange(pay)
    late_kept = late_sum.step(hr)
    own = early_sum.add(late_kept)
    parts = lax.all_to_all(own.reshape(batches, -1, 128), "batch", 0, 0)
    late_kept = own
    while 2 * late_sum.bit < batches:
        late_kept = late_sum.step(own)
    gy, *x_parts, sums_r = call(
        lambda *refs: early_input_kernel(pack, clips, *refs),
        [((rows, POINT), BF16)] + [((depth, rows), BF16)] * groups + [((8, 128), F32)],
        [me_ref, g, sums, st, st_r, affine, hr, ed, ep, yr, yd, yp, mask, wt, late_kept],
        [((rows, PROJECT), F32), ((groups, depth, rows), BF16)],
        idle=1,
        us=8.5,
    )
    x_parts = [x_parts[0]] + [swap(x_parts[k], k) for k in range(1, groups)]
    late_own = late_sum.spread(gy)
    point_halves = point_grads(pack, whole_units(pack.points), gy, act, (late_own,))
    point_sum = Reduction(*point_halves)
    kept = point_sum.halve()
    got = late_sum.double()
    point_own = point_sum.add(parts)
    point_parts = lax.all_to_all(point_own.reshape(batches, -1, 128), "batch", 0, 0)
    (feature_grad,) = call(
        lambda *refs: feature_kernel(pack, *refs),
        [((depth, groups * rows), F32)],
        [me_ref] + x_parts + [point_own],
        [((groups, depth, rows), BF16)],
        idle=1,
        us=2,
    )
    while late_sum.bit > 1:
        got = late_sum.double()
    kernels_size, points_size = parts.shape[1], point_parts.shape[1]
    (parts,) = call(
        total_kernel,
        [((batches, kernels_size + points_size, 128), BF16)],
        [parts, point_parts, feature_grad] + got,
        us=2,
        idle=1 + len(got),
    )
    early_total = lax.all_to_all(parts, "batch", 0, 0)
    while late_sum.bit:
        late_sum.double()
    late_pieces = [late_sum.pieces[k] for k in range(batches)]
    late_wide, late_spread = call(
        lambda *refs: late_gradients_kernel(pack, batches, *refs),
        [((pack.wide, WIDE_COLUMNS), F32), ((SPREAD_COLUMNS, pack.spread), F32)],
        [mb_ref] + late_pieces,
        [((batches, late_piece, 128), BF16), ((pack.spread, SPREAD_COLUMNS), F32)],
        us=4,
    )
    out_arrived = out_arrived.reshape(
        held_clips, LATE.frames, LATE.height, LATE.pitch, -1
    )[:, :, :, : LATE.width]
    outputs, at = [], 0
    for part in upstream:
        outputs.append(out_arrived[..., at : at + part.shape[4]])
        at += part.shape[4]

    wide_grad, early_spread, *point_outs = call(
        lambda *refs: early_gradients_kernel(pack, late_pack, kernels_size, *refs),
        [(wide_kernels.shape, F32), ((SPREAD_COLUMNS, pack.spread), F32)]
        + [(part.shape[::-1], F32) for part in early_parts + late_parts],
        [early_total, late_wide],
        [((pack.wide, WIDE_COLUMNS), F32), ((pack.spread, SPREAD_COLUMNS), F32)],
        us=8,
    )
    point_outs = [part.T for part in point_outs]
    spread_grad = jnp.stack(
        [part.reshape(spread_kernels.shape[1:]) for part in (early_spread, late_spread)]
    )

    def sum_pair(tiles, unit, low=0, high=None):
        first, second, width = SUMS[unit]
        flat = [tile.reshape(-1) for tile in tiles]
        high = width if high is None else high
        return jnp.stack([flat[t][at + low : at + high] for t, at in (first, second)])

    def own_part(early_pair, late_pair):
        both = jnp.stack([early_pair, late_pair])
        size = both.shape[2] // groups
        return lax.dynamic_slice_in_dim(both, me * size, size, 2)

    early_tiles, late_tiles = (sums, sums_r), (late_sums, late_sums_r)
    norm_grads = [
        own_part(*(sum_pair(tiles, *part) for tiles in (early_tiles, late_tiles)))
        for part in (
            ("d",), ("r", 0, NARROW), ("w",), ("r", NARROW, REDUCED), ("s",), ("p",),
        )
    ]
    return tuple(outputs) + (feature_grad,) + tuple(point_outs) + (
        wide_grad, spread_grad,
    ) + tuple(norm_grads)


def solution(mesh):
    columns = P(None, "ch")
    norm = P(None, None, "ch")
    clips = P("batch", None, None, None, "ch")
    kernels = P(None, None, None, "ch")
    return jax.shard_map(
        shards,
        mesh=mesh,
        in_specs=(P("ch", "batch"), P("batch", None, None, None)) + (columns,) * 9 + (kernels,)
        + (norm,) * 6 + (clips,) * 4,
        out_specs=(clips,) * 4 + (P("ch", "batch"),) + (columns,) * 9 + (kernels,) + (norm,) * 6,
        check_vma=False,
    )
```

```python
import jax
import jax.numpy as jnp
import numpy as np
from jax import lax
from jax.experimental import pallas as pl
from jax.experimental.pallas import tpu as pltpu
from jax.sharding import PartitionSpec as P

F32 = jnp.float32
BF16 = jnp.bfloat16
EPSILON = 0.001
FLOPS_A_US = 1.1e9
BOTH = ("batch", "ch")
DIRECT, NARROW, WIDE, SQUEEZE, SPREAD, PROJECT = 256, 160, 320, 32, 128, 128
REDUCED = NARROW + SQUEEZE
POINT = DIRECT + REDUCED + PROJECT
CONCAT = DIRECT + WIDE + SPREAD + PROJECT
WIDE_COLUMNS = 27 * NARROW
SPREAD_COLUMNS = 27 * SQUEEZE
POINT_WIDTHS = (DIRECT, NARROW, SQUEEZE, PROJECT)
SLOT = {"d": (0, DIRECT), "r": (256, REDUCED), "w": (512, WIDE), "s": (896, SPREAD), "p": (1024, PROJECT)}
SLOTS = 1152
NORM_ORDER = ((0, DIRECT), (256, NARROW), (256 + NARROW, SQUEEZE), (512, WIDE), (896, SPREAD), (1024, PROJECT))
TILE_ROW = {"d": (0, DIRECT), "w": (2, WIDE), "s": (5, SPREAD), "p": (6, PROJECT)}
OUTER = ("d", "w", "s", "p")
SUMS = {
    "w": ((0, 0), (0, 320), WIDE), "s": ((0, 640), (0, 768), SPREAD), "p": ((0, 896), (1, 896), PROJECT),
    "d": ((1, 384), (1, 640), DIRECT), "r": ((1, 0), (1, 192), REDUCED),
}
CHUNK = 96


class Geometry:
    def __init__(self, frames, height, width, pitch, block):
        self.frames, self.height, self.width, self.pitch = frames, height, width, pitch
        self.block = block
        self.frame_rows = height * pitch
        self.clip_rows = frames * self.frame_rows
        self.padded_rows = (frames + 2) * self.frame_rows
        self.dense = pitch == width


EARLY = Geometry(4, 12, 12, 12, 0)
LATE = Geometry(2, 6, 6, 8, 1)


def nt(a, b):
    return lax.dot_general(a, b, (((1,), (1,)), ((), ())), preferred_element_type=F32)


def nn(a, b):
    return lax.dot_general(a, b, (((1,), (0,)), ((), ())), preferred_element_type=F32)


def tn(a, b):
    return lax.dot_general(a, b, (((0,), (0,)), ((), ())), preferred_element_type=F32)


def call(kernel, outs, ins, scratch=(), us=0, idle=0):
    moved = sum(int(np.prod(s)) * jnp.dtype(d).itemsize for s, d in outs)
    moved += sum(int(np.prod(x.shape)) * x.dtype.itemsize for x in ins[: len(ins) - idle])

    def spec(k, x):
        if k >= len(ins) - idle:
            return pl.BlockSpec(memory_space=pl.ANY)
        return pl.BlockSpec(memory_space=pltpu.SMEM if x.ndim == 1 else pltpu.VMEM)

    def body(*refs):
        kept = len(ins) - idle
        kernel(*refs[:kept], *refs[len(ins) :])

    return pl.pallas_call(
        body,
        out_shape=[jax.ShapeDtypeStruct(s, d) for s, d in outs],
        in_specs=[spec(k, x) for k, x in enumerate(ins)],
        out_specs=[pl.BlockSpec(memory_space=pltpu.VMEM)] * len(outs),
        scratch_shapes=[pltpu.VMEM(s, d) for s, d in scratch],
        compiler_params=pltpu.CompilerParams(vmem_limit_bytes=56 * 2**20),
        cost_estimate=pl.CostEstimate(
            flops=int(us * FLOPS_A_US) or 10 * moved, bytes_accessed=moved, transcendentals=0
        ),
    )(*ins)


def ordered(value, *behind):
    anywhere = pl.BlockSpec(memory_space=pl.ANY)
    return pl.pallas_call(
        lambda *refs: None,
        out_shape=jax.ShapeDtypeStruct(value.shape, value.dtype),
        in_specs=[anywhere] * (1 + len(behind)),
        out_specs=anywhere,
        input_output_aliases={0: 0},
    )(value, *behind)


def each_chunk(rows, body, init=0, chunk=CHUNK):
    return lax.fori_loop(
        0, rows // chunk, lambda i, carry: body(pl.multiple_of(i * chunk, chunk), carry), init
    )


def wide_mask(m_ref, at, width):
    part = m_ref[at, :]
    if width <= 128:
        return part[:, :width]
    return jnp.concatenate([part] * -(-width // 128), axis=1)[:, :width]


def row(tile, first, width):
    pieces = [
        tile[first + i : first + i + 1, : min(128, width - 128 * i)] for i in range(-(-width // 128))
    ]
    return pieces[0] if len(pieces) == 1 else jnp.concatenate(pieces, axis=1)


def put_row(ref, first, vector):
    width = vector.shape[1]
    for i in range(-(-width // 128)):
        part = vector[:, 128 * i : min(128 * (i + 1), width)]
        ref[first + i : first + i + 1, : part.shape[1]] = part


def put_sums(tiles, unit, sums):
    for (which, start), vector in zip(SUMS[unit][:2], sums):
        at = 0
        while at < vector.shape[1]:
            r, lane = divmod(start + at, 128)
            size = min(128 - lane, vector.shape[1] - at)
            tiles[which][r : r + 1, lane : lane + size] = vector[:, at : at + size]
            at += size


def get_sums(tiles, unit):
    sums = []
    for which, start in SUMS[unit][:2]:
        pieces, at = [], 0
        while at < SUMS[unit][2]:
            r, lane = divmod(start + at, 128)
            size = min(128 - lane, SUMS[unit][2] - at)
            pieces.append(tiles[which][r : r + 1, lane : lane + size])
            at += size
        sums.append(pieces[0] if len(pieces) == 1 else jnp.concatenate(pieces, axis=1))
    return sums


def affine_of(aff_ref, block, unit):
    start, width = SLOT[unit]
    return (
        aff_ref[2 * block : 2 * block + 1, start : start + width],
        aff_ref[2 * block + 1 : 2 * block + 2, start : start + width],
    )


def fold8(value):
    total = value[0:8]
    for i in range(1, value.shape[0] // 8):
        total = total + value[8 * i : 8 * i + 8]
    return total


def local_moments(y_ref, m_ref, rows, count):
    width = y_ref.shape[1]

    def first(r, acc):
        at = pl.ds(r, CHUNK)
        return acc + fold8(y_ref[at, :] * wide_mask(m_ref, at, width))

    total = each_chunk(rows, first, jnp.zeros((8, width), F32))
    mean = jnp.sum(total, axis=0, keepdims=True) / count

    def second(r, acc):
        at = pl.ds(r, CHUNK)
        centred = (y_ref[at, :] - mean) * wide_mask(m_ref, at, width)
        return acc + fold8(centred * centred)

    spread = each_chunk(rows, second, jnp.zeros((8, width), F32))
    return mean, jnp.sum(spread, axis=0, keepdims=True)


def combine_moments(payload, counts, first, second, size):
    means = payload[:, first : first + size, :]
    total = jnp.sum(counts, axis=0)
    mean = jnp.sum(means * counts, axis=0) / total
    offset = means - mean[None]
    spread = jnp.sum(payload[:, second : second + size, :] + counts * offset * offset, axis=0)
    return mean, lax.rsqrt(spread / total + EPSILON)


def send_tile(pay_ref, tile_ref):
    pay_ref[...] = jnp.broadcast_to(tile_ref[...][None], pay_ref.shape)


def shifted(value, offset):
    if offset == 0:
        return value
    return pltpu.roll(value, (-offset) % value.shape[0], 0)


def cell_index(geo, shape):
    r = lax.broadcasted_iota(jnp.int32, shape, 0).astype(F32)
    line = jnp.floor((r + 0.5) * (1.0 / geo.pitch))
    column = r - geo.pitch * line
    frame = jnp.floor((line + 0.5) * (1.0 / geo.height))
    return line - geo.height * frame, column


def edge_masks(geo, width):
    line, column = cell_index(geo, (geo.clip_rows, width))
    return (
        {e: (line + e > -0.5) & (line + e < geo.height - 0.5) for e in (-1, 1)},
        {e: (column + e > -0.5) & (column + e < geo.width - 0.5) for e in (-1, 1)},
    )


def gather_cells(geo, value, masks, sign, store):
    lines, columns = masks
    for b, dw in enumerate((-1, 0, 1)):
        moved = shifted(value, sign * dw)
        if dw and geo.dense:
            moved = jnp.where(columns[sign * dw], moved, 0.0)
        for a, dh in enumerate((-1, 0, 1)):
            placed = shifted(moved, sign * dh * geo.pitch)
            if dh:
                placed = jnp.where(lines[sign * dh], placed, 0.0)
            store(3 * a + b, placed)


def frame_shift(geo, value, offset):
    if offset == 0:
        return value
    size = geo.frame_rows
    blank = jnp.zeros((size, value.shape[1]), value.dtype)
    if offset > 0:
        return jnp.concatenate([value[size:], blank], axis=0)
    return jnp.concatenate([blank, value[:-size]], axis=0)


def mean_cells(geo, value, masks):
    lines, columns = masks
    total = value
    for e in (-1, 1):
        moved = shifted(value, e)
        total = total + (jnp.where(columns[e], moved, 0.0) if geo.dense else moved)
    again = total
    for e in (-1, 1):
        again = again + jnp.where(lines[e], shifted(total, e * geo.pitch), 0.0)
    return (again + frame_shift(geo, again, 1) + frame_shift(geo, again, -1)) / 27.0


def clear_edges(geo, ref, clip):
    base = clip * geo.padded_rows
    size = geo.frame_rows
    blank = jnp.zeros((size, ref.shape[1]), ref.dtype)
    ref[base : base + size, :] = blank
    ref[base + geo.padded_rows - size : base + geo.padded_rows, :] = blank


def padded16(size):
    return -(-size // 16) * 16


class Packing:
    def __init__(self, groups, features):
        self.groups = groups
        self.wide, self.spread, self.point = WIDE // groups, SPREAD // groups, POINT // groups
        self.wide_rows = padded16(self.wide)
        self.spread_rows = padded16(self.spread)
        self.point_rows = padded16(self.point)
        self.kernels = 3 * WIDE_TILES * self.wide_rows + 3 * SPREAD_TILES * self.spread_rows
        self.features = features
        self.point_tiles = -(-features // 128)
        self.points = self.point_tiles * self.point_rows

    def kernel_tiles(self):
        at = 0
        for own, size, tiles, columns, wide in (
            (self.wide, self.wide_rows, WIDE_TILES, 9 * NARROW, True),
            (self.spread, self.spread_rows, SPREAD_TILES, 9 * SQUEEZE, False),
        ):
            for t in range(3):
                for u in range(tiles):
                    yield at, own, wide, t, u, min(128, columns - 128 * u)
                    at += size

    def point_blocks(self, start):
        for u in range(self.point_tiles):
            yield start + u * self.point_rows, u, min(128, self.features - 128 * u)

    def point_parts(self):
        at = start = 0
        for width in POINT_WIDTHS:
            own = width // self.groups
            yield at, start, own
            at += own
            start += width


WIDE_TILES = -(-9 * NARROW // 128)
SPREAD_TILES = -(-9 * SQUEEZE // 128)


def fit_tile(value):
    width = value.shape[1]
    if width == 128:
        return value
    return jnp.concatenate([value, jnp.zeros((value.shape[0], 128 - width), value.dtype)], axis=1)


def pack_points(pack, part_refs, o_ref, start, scratch):
    for (at, _, own), ref in zip(pack.point_parts(), part_refs):
        scratch[at : at + own, : pack.features] = ref[...].astype(F32)
    for at, u, width in pack.point_blocks(start):
        o_ref[at : at + pack.point, :] = fit_tile(
            scratch[: pack.point, 128 * u : 128 * u + width].astype(BF16)
        )


def unpack_points(pack, me, piece_refs, start, raw, scratch, wt_ref):
    for k, ref in enumerate(piece_refs):
        for at, u, width in pack.point_blocks(start):
            raw[me ^ k, : pack.point, 128 * u : 128 * u + width] = ref[at : at + pack.point, :width].astype(F32)
    for s in range(pack.groups):
        for at, begin, own in pack.point_parts():
            scratch[begin + s * own : begin + (s + 1) * own, :] = raw[s, at : at + own, : pack.features]
    wt_ref[...] = scratch[...].astype(BF16)


def unpack_kernels(pack, me, piece_refs, kw_ref, ks_ref):
    for k, ref in enumerate(piece_refs):
        for at, own, wide, t, u, _ in pack.kernel_tiles():
            target = kw_ref if wide else ks_ref
            size = target.shape[2]
            target[t, me ^ k, :, 128 * u : 128 * u + 128] = ref[at : at + size, :]


def whole_kernel(ref, t, own):
    if own == ref.shape[2]:
        return ref[t].reshape(ref.shape[1] * own, ref.shape[3])
    parts = [ref[t, s].astype(F32)[:own] for s in range(ref.shape[1])]
    return jnp.concatenate(parts, axis=0).astype(BF16)


def prepare_kernel(pack, x_ref, norm_ref, p0, p1, p2, p3, o_ref, b_ref, scratch, rows):
    width = o_ref.shape[2]
    for s in range(pack.groups):
        o_ref[s] = x_ref[:, s * width : (s + 1) * width]
    pack_points(pack, (p0, p1, p2, p3), b_ref, 0, scratch)
    rows[...] = jnp.zeros_like(rows)
    for u in range(-(-norm_ref.shape[1] // 128)):
        part = norm_ref[:, 128 * u : 128 * (u + 1)].astype(F32)
        rows[4 * u : 4 * u + 4, : part.shape[1]] = part
    b_ref[pack.points :, :] = rows[...].astype(BF16)


def split_kernel(x_ref, a_ref, b_ref):
    tiles = x_ref.shape[1] // 128

    def move(first, count):
        value = x_ref[:, pl.ds(128 * first, 128 * count)].astype(F32)
        for r, ref in ((0, a_ref), (1, b_ref)):
            parts = [value[r : r + 1, 128 * j : 128 * (j + 1)] for j in range(count)]
            ref[pl.ds(first, count), :] = jnp.concatenate(parts, axis=0).astype(BF16)

    def step(i, carry):
        move(pl.multiple_of(16 * i, 16), 16)
        return carry

    lax.fori_loop(0, tiles // 16, step, 0)
    if tiles % 16:
        move(tiles // 16 * 16, tiles % 16)


def pack_kernel(pack, w_ref, s_ref, o_ref):
    for at, own, wide, t, u, width in pack.kernel_tiles():
        source, columns = (w_ref, 9 * NARROW) if wide else (s_ref, 9 * SQUEEZE)
        start = columns * t + 128 * u
        o_ref[at : at + own, :] = fit_tile(source[:, start : start + width])


def pack_late_kernel(pack, p0, p1, p2, p3, o_ref, scratch):
    pack_points(pack, (p0, p1, p2, p3), o_ref, 0, scratch)


def early_first_kernel(
    pack, me_ref, x_ref, *refs
):
    groups = pack.groups
    piece_refs = refs[:groups]
    m_ref, mc_ref, a_ref, wt_ref, aff_ref, y_ref, pay_ref, xs, raw, ws, norm_raw, tile = refs[groups:]
    me = me_ref[0]
    depth, rows = x_ref.shape[1], x_ref.shape[2]
    for s in range(groups):
        xs[s * depth : (s + 1) * depth, :] = x_ref[s].astype(F32)
    for j in range(0, rows, 128):
        size = min(128, rows - j)
        turned = jnp.transpose(xs[:, j : j + size])
        a_ref[j : j + size, :] = (turned * wide_mask(m_ref, slice(j, j + size), turned.shape[1])).astype(BF16)
    unpack_points(pack, me, piece_refs, 0, raw, ws, wt_ref)
    for k, ref in enumerate(piece_refs):
        norm_raw[me ^ k] = ref[pack.points :, :].astype(F32)
    at = 0
    for slot, whole in NORM_ORDER:
        own = whole // groups
        for s in range(groups):
            left, u = at % 128, at // 128
            first = min(own, 128 - left)
            to = slot + s * own
            aff_ref[:, to : to + first] = norm_raw[s, 4 * u : 4 * u + 4, left : left + first]
            if first < own:
                aff_ref[:, to + first : to + own] = norm_raw[s, 4 * u + 4 : 4 * u + 8, : own - first]
        at += own
    y_ref[...] = nt(a_ref[...], wt_ref[DIRECT : DIRECT + REDUCED, :])
    tile[...] = jnp.zeros_like(tile)
    count = jnp.sum(m_ref[...], axis=0, keepdims=True)
    coarse = jnp.sum(mc_ref[...], axis=0, keepdims=True)
    mean, spread = local_moments(y_ref, m_ref, rows, count[:, 0:1])
    put_row(tile, 0, mean)
    put_row(tile, 2, count)
    put_row(tile, 3, coarse)
    put_row(tile, 4, spread)
    send_tile(pay_ref, tile)


def other_points_kernel(geo, clips, a_ref, wt_ref, m_ref, yd_ref, yp_ref, tile):
    yd_ref[...] = nt(a_ref[...], wt_ref[:DIRECT, :])
    projected = nt(a_ref[...], wt_ref[DIRECT + REDUCED :, :])
    masks = edge_masks(geo, PROJECT)
    for c in range(clips):
        rows = slice(c * geo.clip_rows, (c + 1) * geo.clip_rows)
        yp_ref[rows, :] = mean_cells(geo, projected[rows], masks)
    tile[...] = jnp.zeros_like(tile)
    count = jnp.sum(m_ref[...], axis=0, keepdims=True)[:, 0:1]
    for unit, ref in (("d", yd_ref), ("p", yp_ref)):
        mean, spread = local_moments(ref, m_ref, clips * geo.clip_rows, count)
        put_row(tile, TILE_ROW[unit][0], mean)
        put_row(tile, 8 + TILE_ROW[unit][0], spread)


def second_kernel(
    geo, clips, pack, count_row, me_ref, g_ref, counts_ref, aff_ref, y_ref, m_ref, pd_ref, *refs
):
    piece_refs = refs[: pack.groups]
    (bn_ref, bs_ref, yw_ref, ys_ref, kw_ref, ks_ref, pay_ref, st_ref, us, tile) = refs[pack.groups :]
    unpack_kernels(pack, me_ref[0], piece_refs, kw_ref, ks_ref)
    rows = clips * geo.clip_rows
    counts = counts_ref[:, count_row : count_row + 1, :]
    means, rstds = combine_moments(g_ref[...], counts, 0, 4, 2)
    st_ref[...] = jnp.zeros_like(st_ref)
    st_ref[0:2, :] = means
    st_ref[2:3, :] = jnp.sum(counts, axis=0)
    st_ref[4:6, :] = rstds
    mean, rstd = row(means, 0, REDUCED), row(rstds, 0, REDUCED)
    scale, shift = affine_of(aff_ref, geo.block, "r")

    def activate(r, carry):
        at = pl.ds(r, CHUNK)
        h = scale * ((y_ref[at, :] - mean) * rstd) + shift
        us[at, :] = h * jax.nn.sigmoid(h) * wide_mask(m_ref, at, REDUCED)
        return carry

    each_chunk(rows, activate)
    masks = edge_masks(geo, REDUCED)
    size = geo.frame_rows
    for c in range(clips):
        base = c * geo.padded_rows
        clear_edges(geo, bn_ref, c)
        clear_edges(geo, bs_ref, c)
        inside = slice(base + size, base + size + geo.clip_rows)
        for ref, used in ((bn_ref, 9 * NARROW), (bs_ref, 9 * SQUEEZE)):
            ref[inside, used:] = jnp.zeros((geo.clip_rows, ref.shape[1] - used), BF16)

        def store(j, placed):
            at = slice(base + size, base + size + geo.clip_rows)
            bn_ref[at, NARROW * j : NARROW * (j + 1)] = placed[:, :NARROW].astype(BF16)
            bs_ref[at, SQUEEZE * j : SQUEEZE * (j + 1)] = placed[:, NARROW:].astype(BF16)

        gather_cells(geo, us[c * geo.clip_rows : (c + 1) * geo.clip_rows, :], masks, 1, store)
    for c in range(clips):
        base = c * geo.padded_rows
        out = slice(c * geo.clip_rows, (c + 1) * geo.clip_rows)
        for b_ref, k_ref, o_ref, own in (
            (bn_ref, kw_ref, yw_ref, pack.wide), (bs_ref, ks_ref, ys_ref, pack.spread)
        ):
            total = None
            for t in range(3):
                term = nt(
                    b_ref[base + size * t : base + size * t + geo.clip_rows, :],
                    whole_kernel(k_ref, t, own),
                )
                total = term if total is None else total + term
            o_ref[out, :] = total
    tile[...] = pd_ref[...]
    own = jnp.sum(m_ref[...], axis=0, keepdims=True)[:, 0:1]
    for unit, ref in (("w", yw_ref), ("s", ys_ref)):
        mean, spread = local_moments(ref, m_ref, rows, own)
        put_row(tile, TILE_ROW[unit][0], mean)
        put_row(tile, 8 + TILE_ROW[unit][0], spread)
    send_tile(pay_ref, tile)


def outer_stats(st, unit):
    first, width = TILE_ROW[unit]
    return row(st, first, width), row(st, 8 + first, width)


def pool_kernel(
    pack, clips, me_ref, g_ref, counts_ref, aff_ref, yd_ref, yw_ref, ys_ref, yp_ref, m_ref, pool_ref,
    mc_ref, *refs
):
    piece_refs = refs[: pack.groups]
    a_ref, wt_ref, y_ref, pay_ref, st_ref, high, low, raw, ws, tile = refs[pack.groups :]
    means, rstds = combine_moments(g_ref[...], counts_ref[:, 2:3, :], 0, 8, 8)
    st_ref[0:8, :] = means
    st_ref[8:16, :] = rstds
    st = st_ref[...]
    at_column = 0
    for unit, ref in zip(OUTER, (yd_ref, yw_ref, ys_ref, yp_ref)):
        width = TILE_ROW[unit][1]
        mean, rstd = outer_stats(st, unit)
        scale, shift = affine_of(aff_ref, 0, unit)

        def activate(r, carry):
            at = pl.ds(r, CHUNK)
            h = scale * ((ref[at, :] - mean) * rstd) + shift
            u = h * jax.nn.sigmoid(h) * wide_mask(m_ref, at, width)
            top = u.astype(BF16)
            high[at, :width] = top
            low[at, :width] = (u - top.astype(F32)).astype(BF16)
            return carry

        each_chunk(clips * EARLY.clip_rows, activate)
        for c in range(clips):
            rows = slice(c * EARLY.clip_rows, (c + 1) * EARLY.clip_rows)
            pooled = nn(pool_ref[...], high[rows, :width]) + nn(pool_ref[...], low[rows, :width])
            out = slice(c * LATE.clip_rows, (c + 1) * LATE.clip_rows)
            a_ref[out, at_column : at_column + width] = pooled.astype(BF16)
        at_column += width
    unpack_points(pack, me_ref[0], piece_refs, 0, raw, ws, wt_ref)
    y_ref[...] = nt(a_ref[...], wt_ref[DIRECT : DIRECT + REDUCED, :])
    tile[...] = jnp.zeros_like(tile)
    own = jnp.sum(mc_ref[...], axis=0, keepdims=True)
    mean, spread = local_moments(y_ref, mc_ref, clips * LATE.clip_rows, own[:, 0:1])
    put_row(tile, 0, mean)
    put_row(tile, 4, spread)
    send_tile(pay_ref, tile)


def local_backward(y_ref, dz_of, m_ref, mean, rstd, scale, shift, dh_ref, out_ref, rows):
    width = y_ref.shape[1]

    def body(r, carry):
        at = pl.ds(r, CHUNK)
        masking = wide_mask(m_ref, at, width)
        xhat = (y_ref[at, :] - mean) * rstd
        h = scale * xhat + shift
        gate = jax.nn.sigmoid(h)
        if out_ref is not None:
            out_ref[at, :width] = (h * gate * masking).astype(out_ref.dtype)
        dh = dz_of(at) * masking * gate * (1.0 + h * (1.0 - gate))
        dh_ref[at, :] = dh
        return carry[0] + fold8(dh * xhat), carry[1] + fold8(dh)

    blank = jnp.zeros((8, width), F32)
    first, second = each_chunk(rows, body, (blank, blank))
    return jnp.sum(first, axis=0, keepdims=True), jnp.sum(second, axis=0, keepdims=True)


def cut_kernel(me_ref, x_ref, *o_refs):
    size = o_refs[0].shape[0]
    for k, o_ref in enumerate(o_refs):
        o_ref[...] = x_ref[pl.ds(pl.multiple_of((me_ref[0] ^ k) * size, 16), size), :]


def join_kernel(me_ref, *refs):
    *x_refs, o_ref = refs
    for k, x_ref in enumerate(x_refs):
        o_ref[me_ref[0] ^ k] = x_ref[...]


def late_outputs_kernel(
    clips, groups, me_ref, g_ref, counts_ref, aff_ref, yd_ref, yw_ref, ys_ref, yp_ref, mc_ref, *refs
):
    up_refs, o_refs = refs[:groups], refs[groups : 2 * groups]
    dd_ref, dw_ref, ds_ref, dp_ref, pay_ref, rest_ref, st_ref, shares, up, out, tile = refs[2 * groups :]
    me = me_ref[0]
    means, rstds = combine_moments(g_ref[...], counts_ref[:, 3:4, :], 0, 8, 8)
    st_ref[0:8, :] = means
    st_ref[8:16, :] = rstds
    st = st_ref[...]
    tile[...] = jnp.zeros_like(tile)
    rest_ref[...] = jnp.zeros_like(rest_ref)
    for k, ref in enumerate(up_refs):
        shares[me ^ k] = ref[...].astype(F32)
    at = 0
    for unit, y_ref, dh_ref in zip(
        OUTER, (yd_ref, yw_ref, ys_ref, yp_ref), (dd_ref, dw_ref, ds_ref, dp_ref)
    ):
        mean, rstd = outer_stats(st, unit)
        scale, shift = affine_of(aff_ref, 1, unit)
        width = TILE_ROW[unit][1]
        own = width // groups
        for s in range(groups):
            up[:, s * own : (s + 1) * own] = shares[s, :, at : at + own]
        sums = local_backward(
            y_ref, lambda rows: up[rows, :width], m_ref=mc_ref, mean=mean, rstd=rstd, scale=scale,
            shift=shift, dh_ref=dh_ref, out_ref=out, rows=clips * LATE.clip_rows,
        )
        for s in range(groups):
            shares[s, :, at : at + own] = out[:, s * own : (s + 1) * own]
        at += own
        put_sums((tile, rest_ref), unit, sums)
    for k, ref in enumerate(o_refs):
        ref[...] = shares[me ^ k].astype(BF16)
    send_tile(pay_ref, tile)


def finish_rows(dh, y, masking, mean, rstd, scale, scale_sum, shift_sum, count):
    xhat = (y - mean) * rstd
    return scale * rstd * (dh - (shift_sum + xhat * scale_sum) / count) * masking


def finish_kernel(
    geo, clips, g_ref, st_ref, str_ref, aff_ref, dw_ref, ds_ref, yw_ref, ys_ref, m_ref,
    gw_ref, gs_ref, sums_ref
):
    rows = clips * geo.clip_rows
    sums_ref[...] = jnp.sum(g_ref[...], axis=0)
    sums, st = sums_ref[...], st_ref[...]
    count = str_ref[2:3, 0:1]
    for unit, d_ref, y_ref, o_ref in (("w", dw_ref, yw_ref, gw_ref), ("s", ds_ref, ys_ref, gs_ref)):
        first, width = TILE_ROW[unit]
        mean, rstd = outer_stats(st, unit)
        scale, _ = affine_of(aff_ref, geo.block, unit)
        scale_sum, shift_sum = get_sums((sums,), unit)

        def finish(r, carry):
            at = pl.ds(r, CHUNK)
            dy = finish_rows(
                d_ref[at, :], y_ref[at, :], wide_mask(m_ref, at, width), mean, rstd, scale, scale_sum,
                shift_sum, count,
            )
            o_ref[at, :] = dy.astype(BF16)
            return carry

        each_chunk(rows, finish)


def inner_backward_kernel(
    geo, clips, pack, str_ref, aff_ref, gw_ref, gs_ref, yr_ref, kw_ref, ks_ref, m_ref, rest_ref,
    dh_ref, pay_ref, pad_w, pad_s, kt_w, kt_s, dz, tile
):
    rows = clips * geo.clip_rows
    size = geo.frame_rows
    st_r = str_ref[...]
    for width, g_ref, pad in ((WIDE, gw_ref, pad_w), (SPREAD, gs_ref, pad_s)):
        masks = edge_masks(geo, width)
        for c in range(clips):
            base = c * geo.padded_rows
            clear_edges(geo, pad, c)

            def store(j, placed):
                at = slice(base + size, base + size + geo.clip_rows)
                pad[at, width * j : width * (j + 1)] = placed.astype(BF16)

            value = g_ref[c * geo.clip_rows : (c + 1) * geo.clip_rows, :].astype(F32)
            gather_cells(geo, value, masks, -1, store)
    for k_ref, kt, own, width, depth in (
        (kw_ref, kt_w, pack.wide, WIDE, NARROW), (ks_ref, kt_s, pack.spread, SPREAD, SQUEEZE)
    ):
        for t in range(3):
            whole = whole_kernel(k_ref, t, own)
            for j in range(9):
                kt[t, width * j : width * (j + 1), :] = whole[:, depth * j : depth * (j + 1)]
    for pad, kt, depth, start in ((pad_w, kt_w, NARROW, 0), (pad_s, kt_s, SQUEEZE, NARROW)):
        for c in range(clips):
            base = c * geo.padded_rows
            total = None
            for t in range(3):
                at = base + size * (2 - t)
                term = nn(pad[at : at + geo.clip_rows, :], kt[t])
                total = term if total is None else total + term
            dz[c * geo.clip_rows : (c + 1) * geo.clip_rows, start : start + depth] = total
    scale, shift = affine_of(aff_ref, geo.block, "r")
    sums = local_backward(
        yr_ref, lambda at: dz[at, :], m_ref=m_ref, mean=row(st_r, 0, REDUCED),
        rstd=row(st_r, 4, REDUCED), scale=scale, shift=shift, dh_ref=dh_ref, out_ref=None, rows=rows,
    )
    tile[...] = rest_ref[...]
    put_sums((None, tile), "r", sums)
    send_tile(pay_ref, tile)


def kernel_grad_kernel(
    geo, clips, pack, halves, me_ref, gw_ref, gs_ref, bn_ref, bs_ref, *refs
):
    send_ref, grad_w, grad_s = refs[-3:]
    keep_refs = refs[-4:-3] if halves else ()
    for source, target in zip(refs[:-4], (*keep_refs, send_ref)):
        target[:, pack.kernels : pack.kernels + source.shape[1], :] = source[...]
    size = geo.frame_rows
    for g_ref, b_ref, grad in ((gw_ref, bn_ref, grad_w), (gs_ref, bs_ref, grad_s)):
        for t in range(3):
            total = None
            for c in range(clips):
                at = c * geo.padded_rows + size * t
                term = tn(
                    g_ref[c * geo.clip_rows : (c + 1) * geo.clip_rows, :],
                    b_ref[at : at + geo.clip_rows, :],
                )
                total = term if total is None else total + term
            grad[t] = total
    me = me_ref[0]
    for k in range(pack.groups):
        target, place = ((*keep_refs, send_ref)[k % 2], k // 2) if halves else (send_ref, me ^ k)
        for at, own, wide, t, u, _ in pack.kernel_tiles():
            source = grad_w if wide else grad_s
            first = pl.multiple_of((me ^ k) * own, 8)
            part = source[t, pl.ds(first, own), 128 * u : 128 * u + 128]
            target[place, at : at + own, :] = part.astype(BF16)


def point_grad_kernel(pack, me_ref, gy_ref, a_ref, keep_ref, send_ref, whole, shares):
    whole[...] = tn(gy_ref[...], a_ref[...])
    for s in range(pack.groups):
        for at, begin, own in pack.point_parts():
            shares[s, at : at + own, : pack.features] = whole[begin + s * own : begin + (s + 1) * own, :]
    for k in range(pack.groups):
        target = (keep_ref, send_ref)[k % 2]
        for at, u, width in pack.point_blocks(0):
            target[k // 2, at : at + pack.point, :] = shares[
                me_ref[0] ^ k, : pack.point, 128 * u : 128 * u + 128
            ].astype(BF16)


def halve_kernel(keep_ref, got_ref, even_ref, odd_ref):
    for q in range(keep_ref.shape[0]):
        target = (even_ref, odd_ref)[q % 2]
        target[q // 2] = (keep_ref[q].astype(F32) + got_ref[q].astype(F32)).astype(BF16)


def add_kernel(keep_ref, got_ref, o_ref):
    o_ref[...] = (keep_ref[0].astype(F32) + got_ref[0].astype(F32)).astype(BF16)


def scatter_halves_kernel(mb_ref, x_ref, even_ref, odd_ref, held):
    held[...] = x_ref[...].astype(F32)
    size = even_ref.shape[1]
    for k in range(2 * even_ref.shape[0]):
        first = pl.multiple_of((mb_ref[0] ^ k) * size, 8)
        (even_ref, odd_ref)[k % 2][k // 2] = held[pl.ds(first, size), :].astype(BF16)


def total_kernel(*refs):
    *x_refs, o_ref = refs
    at = 0
    for x_ref in x_refs:
        total = x_ref[0].astype(F32)
        for k in range(1, x_ref.shape[0]):
            total = total + x_ref[k].astype(F32)
        size = x_ref.shape[1]
        o_ref[:, at : at + size, :] = jnp.broadcast_to(
            total.astype(BF16)[None], (o_ref.shape[0],) + total.shape
        )
        at += size


def read_kernels(pack, rows, w_ref, s_ref, turned):
    for at, own, wide, t, u, width in pack.kernel_tiles():
        target, columns = (w_ref, 9 * NARROW) if wide else (turned, 9 * SQUEEZE)
        start = columns * t + 128 * u
        target[:, start : start + width] = rows[at : at + own, :width].astype(F32)
    s_ref[...] = jnp.transpose(turned[...])


def read_points(pack, start, rows, o_refs):
    for at, u, width in pack.point_blocks(start):
        block = rows[at : at + pack.point, :].astype(F32)
        for (first, _, own), o_ref in zip(pack.point_parts(), o_refs):
            o_ref[:, 128 * u : 128 * u + width] = block[first : first + own, :width]


def late_gradients_kernel(pack, batches, mb_ref, *refs):
    x_refs = refs[:batches]
    w_ref, s_ref, held, turned = refs[batches:]
    for k, x_ref in enumerate(x_refs):
        held[mb_ref[0] ^ k] = x_ref[...]
    read_kernels(pack, held[...].reshape(-1, 128), w_ref, s_ref, turned)


def early_gradients_kernel(pack, late_pack, size, x_ref, late_ref, w_ref, s_ref, *refs):
    *o_refs, wide, turned = refs
    rows = x_ref[:, :size, :].reshape(-1, 128)
    read_kernels(pack, rows, wide, s_ref, turned)
    read_points(late_pack, pack.kernels, rows, o_refs[len(o_refs) // 2 :])
    read_points(pack, 0, x_ref[:, size:, :].reshape(-1, 128), o_refs[: len(o_refs) // 2])

    def join(g, carry):
        parts = []
        for r in range(4):
            at = pl.ds(4 * g + r, 1)
            parts.append(jnp.concatenate([wide[at, :], late_ref[at, :]], axis=0))
        first = pl.multiple_of(4 * WIDE_COLUMNS * g, 128)
        w_ref[:, pl.ds(first, 4 * WIDE_COLUMNS)] = jnp.concatenate(parts, axis=1)
        return carry

    lax.fori_loop(0, pack.wide // 4, join, 0, unroll=5)


def point_gradients(
    geo, clips, g_ref, sums_ref, st_ref, str_ref, aff_ref, dr_ref, dd_ref, dp_ref, yr_ref, yd_ref,
    yp_ref, m_ref, gy_ref, sumr_ref, held
):
    rows = clips * geo.clip_rows
    sumr_ref[...] = jnp.sum(g_ref[...], axis=0)
    sums, sums_r, st, st_r = sums_ref[...], sumr_ref[...], st_ref[...], str_ref[...]
    count = st_r[2:3, 0:1]
    scale_d, _ = affine_of(aff_ref, geo.block, "d")
    scale_r, _ = affine_of(aff_ref, geo.block, "r")
    scale_p, _ = affine_of(aff_ref, geo.block, "p")
    mean_d, rstd_d = outer_stats(st, "d")
    mean_p, rstd_p = outer_stats(st, "p")
    mean_r, rstd_r = row(st_r, 0, REDUCED), row(st_r, 4, REDUCED)

    pair_d, pair_p, pair_r = (get_sums((sums, sums_r), unit) for unit in "dpr")

    def finish(r, carry):
        at = pl.ds(r, CHUNK)
        gy_ref[at, :DIRECT] = finish_rows(
            dd_ref[at, :], yd_ref[at, :], wide_mask(m_ref, at, DIRECT), mean_d, rstd_d, scale_d, *pair_d, count
        ).astype(BF16)
        gy_ref[at, DIRECT : DIRECT + REDUCED] = finish_rows(
            dr_ref[at, :], yr_ref[at, :], wide_mask(m_ref, at, REDUCED), mean_r, rstd_r, scale_r, *pair_r, count
        ).astype(BF16)
        held[at, :] = finish_rows(
            dp_ref[at, :], yp_ref[at, :], m_ref[at, :], mean_p, rstd_p, scale_p, *pair_p, count
        )
        return carry

    each_chunk(rows, finish)
    masks = edge_masks(geo, PROJECT)
    for c in range(clips):
        at = slice(c * geo.clip_rows, (c + 1) * geo.clip_rows)
        gy_ref[at, DIRECT + REDUCED :] = mean_cells(geo, held[at, :], masks).astype(BF16)


def late_input_kernel(
    clips, g_ref, sums_ref, st_ref, str_ref, aff_ref, dr_ref, dd_ref, dp_ref, yr_ref, yd_ref, yp_ref,
    mc_ref, wt_ref, spread_ref, est_ref, ed_ref, ew_ref, es_ref, ep_ref, m_ref,
    gy_ref, hd_ref, hw_ref, hs_ref, hp_ref, pay_ref, rest_ref, sumr_ref, held, grad, wide, tile
):
    point_gradients(
        LATE, clips, g_ref, sums_ref, st_ref, str_ref, aff_ref, dr_ref, dd_ref, dp_ref, yr_ref,
        yd_ref, yp_ref, mc_ref, gy_ref, sumr_ref, held,
    )
    grad[...] = nn(gy_ref[...], wt_ref[...]).astype(BF16)
    st = est_ref[...]
    tile[...] = jnp.zeros_like(tile)
    rest_ref[...] = jnp.zeros_like(rest_ref)
    column = 0
    for unit, y_ref, dh_ref in zip(
        OUTER, (ed_ref, ew_ref, es_ref, ep_ref), (hd_ref, hw_ref, hs_ref, hp_ref)
    ):
        width = TILE_ROW[unit][1]
        for c in range(clips):
            wide[c * EARLY.clip_rows : (c + 1) * EARLY.clip_rows, :width] = nn(
                spread_ref[...],
                grad[c * LATE.clip_rows : (c + 1) * LATE.clip_rows, column : column + width],
            )
        column += width
        mean, rstd = outer_stats(st, unit)
        scale, shift = affine_of(aff_ref, 0, unit)
        sums = local_backward(
            y_ref, lambda at: wide[at, :width], m_ref=m_ref, mean=mean, rstd=rstd, scale=scale,
            shift=shift, dh_ref=dh_ref, out_ref=None, rows=clips * EARLY.clip_rows,
        )
        put_sums((tile, rest_ref), unit, sums)
    send_tile(pay_ref, tile)


def early_input_kernel(
    pack, clips, me_ref, g_ref, sums_ref, st_ref, str_ref, aff_ref, dr_ref, dd_ref, dp_ref, yr_ref,
    yd_ref, yp_ref, m_ref, wt_ref, gy_ref, *refs
):
    x_refs = refs[: pack.groups]
    sumr_ref, held, turned = refs[pack.groups :]
    point_gradients(
        EARLY, clips, g_ref, sums_ref, st_ref, str_ref, aff_ref, dr_ref, dd_ref, dp_ref, yr_ref,
        yd_ref, yp_ref, m_ref, gy_ref, sumr_ref, held,
    )
    depth = turned.shape[1]
    rows = clips * EARLY.clip_rows
    for j in range(0, rows, 128):
        size = min(128, rows - j)
        grad = jnp.transpose(nn(gy_ref[j : j + size, :], wt_ref[...]) * wide_mask(m_ref, slice(j, j + size), wt_ref.shape[1]))
        for s in range(pack.groups):
            turned[s, :, j : j + size] = grad[s * depth : (s + 1) * depth, :].astype(BF16)
    for k, x_ref in enumerate(x_refs):
        x_ref[...] = turned[me_ref[0] ^ k]


def feature_kernel(pack, me_ref, *refs):
    *x_refs, o_ref, held = refs
    for k, x_ref in enumerate(x_refs):
        held[me_ref[0] ^ k] = x_ref[...]
    width = held.shape[2]
    for s in range(pack.groups):
        o_ref[:, s * width : (s + 1) * width] = held[s].astype(F32)


def pool_matrix():
    matrix = np.zeros((LATE.clip_rows, EARLY.clip_rows), np.float32)
    for f in range(EARLY.frames):
        for h in range(EARLY.height):
            for w in range(EARLY.width):
                cell = (f // 2) * LATE.frame_rows + (h // 2) * LATE.pitch + w // 2
                matrix[cell, (f * EARLY.height + h) * EARLY.width + w] = 0.125
    return matrix


def pad_late(field):
    padded = jnp.pad(field, ((0, 0), (0, 0), (0, 0), (0, LATE.pitch - LATE.width), (0, 0)))
    return padded.reshape(-1, field.shape[4])


def shards(
    clip_features, visible, direct_early, narrow_early, squeeze_early, project_early, direct_late,
    narrow_late, squeeze_late, project_late, wide_kernels, spread_kernels, direct_norm, narrow_norm,
    wide_norm, squeeze_norm, spread_norm, project_norm, upstream_direct, upstream_wide,
    upstream_spread, upstream_project,
):
    groups = lax.axis_size("ch")
    batches = lax.axis_size("batch")
    devices = groups * batches
    me = lax.axis_index("ch")
    me_ref = jnp.reshape(me, (1,)).astype(jnp.int32)
    held_clips = visible.shape[0]
    clips = held_clips // groups
    rows = clips * EARLY.clip_rows
    late_rows = clips * LATE.clip_rows
    depth = clip_features.shape[0]
    features = depth * groups
    pack = Packing(groups, features)
    late_pack = Packing(groups, CONCAT)

    def exchange(payload):
        return lax.all_to_all(payload, BOTH, 0, 0)

    def swap(value, bit):
        return lax.ppermute(value, "ch", [(i, i ^ bit) for i in range(groups)])

    class Shares:
        def __init__(self, own):
            self.pieces, self.bit = {0: own}, groups // 2
            self.step()

        def step(self):
            for k in list(self.pieces):
                self.pieces[k | self.bit] = swap(self.pieces[k], self.bit)
            self.bit //= 2

        def all(self, *behind):
            if behind:
                last = max(self.pieces)
                self.pieces[last] = ordered(self.pieces[last], *behind)
            while self.bit:
                self.step()
            return [self.pieces[k] for k in range(groups)]

    early_parts = (direct_early, narrow_early, squeeze_early, project_early)
    late_parts = (direct_late, narrow_late, squeeze_late, project_late)
    norms = (direct_norm, narrow_norm, squeeze_norm, wide_norm, spread_norm, project_norm)
    norm_rows = jnp.concatenate(norms, axis=2).reshape(4, -1)
    norm_space = padded16(4 * -(-norm_rows.shape[1] // 128))
    pieces, early_points = call(
        lambda *refs: prepare_kernel(pack, *refs),
        [((groups, depth, rows), BF16), ((pack.points + norm_space, 128), BF16)],
        [clip_features, norm_rows] + [part.T for part in early_parts],
        [((pack.point_rows, pack.point_tiles * 128), F32), ((norm_space, 128), F32)],
        us=2.5,
    )
    arrived = lax.all_to_all(pieces, "ch", 0, 0)
    point_shares = Shares(early_points).all()
    flat_rows = wide_kernels.shape[1] // 128
    halves = call(split_kernel, [((flat_rows, 128), BF16)] * 2, [wide_kernels, pieces], us=4.8, idle=1)
    spread_rows = jnp.transpose(
        spread_kernels.reshape(2, SPREAD_COLUMNS, spread_kernels.shape[3]), (0, 2, 1)
    )

    def packed(use, block, behind):
        return call(
            lambda *refs: pack_kernel(use, *refs),
            [((use.kernels, 128), BF16)],
            [halves[block].reshape(-1, WIDE_COLUMNS), spread_rows[block]] + list(behind),
            us=2.5,
            idle=len(behind),
        )[0]

    early_shares = Shares(ordered(packed(pack, 0, ()), point_shares[-1], arrived))
    own_visible = lax.dynamic_slice_in_dim(visible, me * clips, clips, 0)
    fine = own_visible.astype(F32).reshape(rows, 1)
    mask = jnp.broadcast_to(fine, (rows, 128))
    cells = own_visible.reshape(clips, 2, 2, 6, 2, 6, 2).max(axis=(2, 4, 6)).astype(F32)
    coarse = jnp.broadcast_to(pad_late(cells[..., None]), (late_rows, 128))

    upstream = (upstream_direct, upstream_wide, upstream_spread, upstream_project)
    up_rows = pad_late(jnp.concatenate(upstream, axis=4))
    up_pieces = call(
        cut_kernel, [((late_rows, up_rows.shape[1]), BF16)] * groups, [me_ref, up_rows], us=1
    )
    up_pieces = [up_pieces[0]] + [swap(up_pieces[k], k) for k in range(1, groups)]

    pool = jnp.asarray(pool_matrix(), BF16)
    spread_back = jnp.asarray(pool_matrix().T, BF16)

    act, wt, affine, yr, pay = call(
        lambda *refs: early_first_kernel(pack, *refs),
        [
            ((rows, features), BF16), ((POINT, features), BF16), ((4, SLOTS), F32),
            ((rows, REDUCED), F32), ((devices, 8, 128), F32),
        ],
        [me_ref, arrived] + point_shares + [mask, coarse],
        [
            ((features, rows), F32), ((groups, pack.point_rows, pack.point_tiles * 128), F32),
            ((POINT, features), F32), ((groups, norm_space, 128), F32), ((8, 128), F32),
        ],
        us=8.6,
    )
    (late_points_own,) = call(
        lambda *refs: pack_late_kernel(late_pack, *refs),
        [((late_pack.points, 128), BF16)],
        [part.T for part in late_parts] + [act],
        [((late_pack.point_rows, late_pack.point_tiles * 128), F32)],
        us=1.5,
        idle=1,
    )
    late_own = packed(pack, 1, (act,))
    counts = exchange(pay)
    late_point_shares = Shares(ordered(late_points_own, counts)).all()
    late_shares = Shares(ordered(late_own, late_point_shares[groups // 2]))
    yd, yp, tile = call(
        lambda *refs: other_points_kernel(EARLY, clips, *refs),
        [((rows, DIRECT), F32), ((rows, PROJECT), F32), ((16, 128), F32)],
        [act, wt, mask],
        us=12,
    )

    def second(geo, count_row, g, y, masking, pieces, other, behind=()):
        own = clips * geo.clip_rows
        padded = clips * geo.padded_rows
        return call(
            lambda *refs: second_kernel(geo, clips, pack, count_row, *refs),
            [
                ((padded, 128 * WIDE_TILES), BF16), ((padded, 128 * SPREAD_TILES), BF16),
                ((own, WIDE), F32), ((own, SPREAD), F32),
                ((3, groups, pack.wide_rows, 128 * WIDE_TILES), BF16),
                ((3, groups, pack.spread_rows, 128 * SPREAD_TILES), BF16),
                ((devices, 16, 128), F32), ((8, 128), F32),
            ],
            [me_ref, g, counts, affine, y, masking, other] + pieces + list(behind),
            [((own, REDUCED), F32), ((16, 128), F32)],
            idle=len(behind),
            us=25 if geo is EARLY else 9,
        )

    early_shares = early_shares.all(counts)
    bn, bs, yw, ys, kw, ks, pay, st_r = second(
        EARLY, 2, counts, yr, mask, early_shares, tile, (late_own,)
    )
    g = exchange(pay)
    late_act, late_wt, lyr, pay, st = call(
        lambda *refs: pool_kernel(late_pack, clips, *refs),
        [
            ((late_rows, CONCAT), BF16), ((POINT, CONCAT), BF16), ((late_rows, REDUCED), F32),
            ((devices, 8, 128), F32), ((16, 128), F32),
        ],
        [me_ref, g, counts, affine, yd, yw, ys, yp, mask, pool, coarse] + late_point_shares,
        [
            ((rows, 384), BF16), ((rows, 384), BF16),
            ((groups, late_pack.point_rows, late_pack.point_tiles * 128), F32),
            ((POINT, CONCAT), F32), ((8, 128), F32),
        ],
        us=15,
    )
    g = exchange(pay)
    lyd, lyp, tile = call(
        lambda *refs: other_points_kernel(LATE, clips, *refs),
        [((late_rows, DIRECT), F32), ((late_rows, PROJECT), F32), ((16, 128), F32)],
        [late_act, late_wt, coarse],
        us=3.7,
    )
    late_shares = late_shares.all(g)
    lbn, lbs, lyw, lys, lkw, lks, pay, lst_r = second(LATE, 3, g, lyr, coarse, late_shares, tile)
    g = exchange(pay)
    widths = [TILE_ROW[unit][1] for unit in OUTER]
    res = call(
        lambda *refs: late_outputs_kernel(clips, groups, *refs),
        [(up_pieces[0].shape, BF16)] * groups
        + [((late_rows, w), F32) for w in widths]
        + [((devices, 8, 128), F32), ((8, 128), F32), ((16, 128), F32)],
        [me_ref, g, counts, affine, lyd, lyw, lys, lyp, coarse] + up_pieces,
        [
            ((groups,) + up_pieces[0].shape, F32), ((late_rows, WIDE), F32), ((late_rows, WIDE), F32),
            ((8, 128), F32),
        ],
        us=4,
    )
    outs, (hd, hw, hs, hp), (pay, rest, lst) = res[:groups], res[groups : groups + 4], res[groups + 4 :]
    g = exchange(pay)

    outs = [outs[0]] + [swap(outs[k], k) for k in range(1, groups)]

    def finish(geo, g, st, st_r, hw, hs, yw, ys, masking, behind=()):
        own = clips * geo.clip_rows
        return call(
            lambda *refs: finish_kernel(geo, clips, *refs),
            [((own, WIDE), BF16), ((own, SPREAD), BF16), ((8, 128), F32)],
            [g, st, st_r, affine, hw, hs, yw, ys, masking] + list(behind),
            idle=len(behind),
            us=7 if geo is EARLY else 2.5,
        )

    def inner(geo, st_r, gw, gs, yr, kw, ks, masking, rest, behind=()):
        own = clips * geo.clip_rows
        padded = clips * geo.padded_rows
        return call(
            lambda *refs: inner_backward_kernel(geo, clips, pack, *refs),
            [((own, REDUCED), F32), ((devices, 8, 128), F32)],
            [st_r, affine, gw, gs, yr, kw, ks, masking, rest] + list(behind),
            [
                ((padded, 9 * WIDE), BF16), ((padded, 9 * SPREAD), BF16),
                ((3, 9 * WIDE, NARROW), BF16), ((3, 9 * SPREAD, SQUEEZE), BF16),
                ((own, REDUCED), F32), ((8, 128), F32),
            ],
            idle=len(behind),
            us=16 if geo is EARLY else 5.6,
        )

    unit = 16 * batches

    def kernel_grads(geo, size, gw, gs, bn, bs, halves, others=()):
        outs = [(groups // 2, size, 128)] * 2 if halves else [(groups, size, 128)]
        return call(
            lambda *refs: kernel_grad_kernel(geo, clips, pack, halves, *refs),
            [(shape, BF16) for shape in outs],
            [me_ref, gw, gs, bn, bs] + list(others),
            [((3, WIDE, 128 * WIDE_TILES), F32), ((3, SPREAD, 128 * SPREAD_TILES), F32)],
            us=10 if geo is EARLY else 5,
        )

    def point_grads(use, size, gy, act, behind=()):
        return call(
            lambda *refs: point_grad_kernel(use, *refs),
            [((groups // 2, size, 128), BF16)] * 2,
            [me_ref, gy, act] + list(behind),
            [((POINT, use.features), F32), ((groups, use.point_rows, use.point_tiles * 128), F32)],
            us=4.5,
            idle=len(behind),
        )

    class Reduction:
        def __init__(self, keep, send):
            self.keep, self.bit = keep, 1
            self.got = swap(send, 1)

        def halve(self, *behind):
            while 2 * self.bit < groups:
                shape = (self.keep.shape[0] // 2,) + self.keep.shape[1:]
                self.keep, send = call(
                    halve_kernel, [(shape, BF16)] * 2, [self.keep, self.got] + list(behind),
                    idle=len(behind),
                    us=2.5,
                )
                self.bit *= 2
                self.got = swap(send, self.bit)
            return self.keep

        def add(self, *behind):
            return call(
                add_kernel, [(self.keep.shape[1:], BF16)], [self.keep, self.got] + list(behind),
                idle=len(behind),
                us=2,
            )[0]

    mb_ref = jnp.reshape(lax.axis_index("batch"), (1,)).astype(jnp.int32)

    def batch_swap(value, bit):
        return lax.ppermute(value, "batch", [(i, i ^ bit) for i in range(batches)])

    def whole_units(size):
        return -(-size // unit) * unit

    gw, gs, late_sums = finish(LATE, g, lst, lst_r, hw, hs, lyw, lys, coarse)
    hr, pay = inner(LATE, lst_r, gw, gs, lyr, lkw, lks, coarse, rest)
    g = exchange(pay)
    (late_kernels,) = kernel_grads(
        LATE, whole_units(pack.kernels), gw, gs, lbn, lbs, False
    )
    late_share = lax.psum_scatter(ordered(late_kernels, g), "ch", scatter_dimension=0)
    gy, ed, ew, es, ep, pay, rest, late_sums_r = call(
        lambda *refs: late_input_kernel(clips, *refs),
        [((late_rows, POINT), BF16)]
        + [((rows, w), F32) for w in widths]
        + [((devices, 8, 128), F32), ((8, 128), F32), ((8, 128), F32)],
        [g, late_sums, lst, lst_r, affine, hr, hd, hp, lyr, lyd, lyp, coarse, late_wt, spread_back,
         st, yd, yw, ys, yp, mask, late_kernels],
        [((late_rows, PROJECT), F32), ((late_rows, CONCAT), BF16), ((rows, WIDE), F32), ((8, 128), F32)],
        idle=1,
        us=15,
    )
    g = exchange(pay)
    (out_arrived,) = call(
        join_kernel,
        [((groups,) + outs[0].shape, BF16)],
        [me_ref] + outs + [gy],
        us=1,
        idle=1,
    )
    late_points = point_grads(late_pack, late_pack.points, gy, late_act)
    gw, gs, sums = finish(
        EARLY, g, st, st_r, ew, es, yw, ys, mask, (late_points[1], out_arrived)
    )
    early_size = whole_units(pack.kernels + late_pack.points)
    halves = kernel_grads(EARLY, early_size, gw, gs, bn, bs, True, late_points)
    early_sum = Reduction(*halves)

    class BatchHalves(Reduction):
        def __init__(self, keep, send):
            self.keep, self.bit = keep, 1
            self.got = batch_swap(send, 1)

        def step(self, *behind):
            shape = (self.keep.shape[0] // 2,) + self.keep.shape[1:]
            self.keep, send = call(
                halve_kernel, [(shape, BF16)] * 2, [self.keep, self.got] + list(behind),
                idle=len(behind), us=1.5,
            )
            self.bit *= 2
            self.got = batch_swap(send, self.bit)
            return self.keep

        def spread(self, *behind):
            own = self.add(*behind)
            self.pieces, self.bit = {0: own}, batches // 2
            return own

        def double(self):
            got = {k | self.bit: batch_swap(self.pieces[k], self.bit) for k in self.pieces}
            self.pieces.update(got)
            self.bit //= 2
            return list(got.values())

    late_piece = late_share.shape[0] // batches
    late_halves = call(
        scatter_halves_kernel,
        [((batches // 2, late_piece, 128), BF16)] * 2,
        [mb_ref, late_share, halves[1]],
        [(late_share.shape, F32)],
        us=3,
        idle=1,
    )
    late_sum = BatchHalves(*late_halves)
    kept = early_sum.halve(late_halves[1])
    hr, pay = inner(EARLY, st_r, gw, gs, yr, kw, ks, mask, rest, behind=(kept,))
    g = exchange(pay)
    late_kept = late_sum.step(hr)
    own = early_sum.add(late_kept)
    parts = lax.all_to_all(own.reshape(batches, -1, 128), "batch", 0, 0)
    late_kept = own
    while 2 * late_sum.bit < batches:
        late_kept = late_sum.step(own)
    gy, *x_parts, sums_r = call(
        lambda *refs: early_input_kernel(pack, clips, *refs),
        [((rows, POINT), BF16)] + [((depth, rows), BF16)] * groups + [((8, 128), F32)],
        [me_ref, g, sums, st, st_r, affine, hr, ed, ep, yr, yd, yp, mask, wt, late_kept],
        [((rows, PROJECT), F32), ((groups, depth, rows), BF16)],
        idle=1,
        us=8.5,
    )
    x_parts = [x_parts[0]] + [swap(x_parts[k], k) for k in range(1, groups)]
    late_own = late_sum.spread(gy)
    point_halves = point_grads(pack, whole_units(pack.points), gy, act, (late_own,))
    point_sum = Reduction(*point_halves)
    kept = point_sum.halve()
    got = late_sum.double()
    point_own = point_sum.add(parts)
    point_parts = lax.all_to_all(point_own.reshape(batches, -1, 128), "batch", 0, 0)
    (feature_grad,) = call(
        lambda *refs: feature_kernel(pack, *refs),
        [((depth, groups * rows), F32)],
        [me_ref] + x_parts + [point_own],
        [((groups, depth, rows), BF16)],
        idle=1,
        us=2,
    )
    while late_sum.bit > 1:
        got = late_sum.double()
    kernels_size, points_size = parts.shape[1], point_parts.shape[1]
    (parts,) = call(
        total_kernel,
        [((batches, kernels_size + points_size, 128), BF16)],
        [parts, point_parts, feature_grad] + got,
        us=2,
        idle=1 + len(got),
    )
    early_total = lax.all_to_all(parts, "batch", 0, 0)
    while late_sum.bit:
        late_sum.double()
    late_pieces = [late_sum.pieces[k] for k in range(batches)]
    late_wide, late_spread = call(
        lambda *refs: late_gradients_kernel(pack, batches, *refs),
        [((pack.wide, WIDE_COLUMNS), F32), ((SPREAD_COLUMNS, pack.spread), F32)],
        [mb_ref] + late_pieces,
        [((batches, late_piece, 128), BF16), ((pack.spread, SPREAD_COLUMNS), F32)],
        us=4,
    )
    out_arrived = out_arrived.reshape(
        held_clips, LATE.frames, LATE.height, LATE.pitch, -1
    )[:, :, :, : LATE.width]
    outputs, at = [], 0
    for part in upstream:
        outputs.append(out_arrived[..., at : at + part.shape[4]])
        at += part.shape[4]

    wide_grad, early_spread, *point_outs = call(
        lambda *refs: early_gradients_kernel(pack, late_pack, kernels_size, *refs),
        [(wide_kernels.shape, F32), ((SPREAD_COLUMNS, pack.spread), F32)]
        + [(part.shape[::-1], F32) for part in early_parts + late_parts],
        [early_total, late_wide],
        [((pack.wide, WIDE_COLUMNS), F32), ((pack.spread, SPREAD_COLUMNS), F32)],
        us=8,
    )
    point_outs = [part.T for part in point_outs]
    spread_grad = jnp.stack(
        [part.reshape(spread_kernels.shape[1:]) for part in (early_spread, late_spread)]
    )

    def sum_pair(tiles, unit, low=0, high=None):
        first, second, width = SUMS[unit]
        flat = [tile.reshape(-1) for tile in tiles]
        high = width if high is None else high
        return jnp.stack([flat[t][at + low : at + high] for t, at in (first, second)])

    def own_part(early_pair, late_pair):
        both = jnp.stack([early_pair, late_pair])
        size = both.shape[2] // groups
        return lax.dynamic_slice_in_dim(both, me * size, size, 2)

    early_tiles, late_tiles = (sums, sums_r), (late_sums, late_sums_r)
    norm_grads = [
        own_part(*(sum_pair(tiles, *part) for tiles in (early_tiles, late_tiles)))
        for part in (
            ("d",), ("r", 0, NARROW), ("w",), ("r", NARROW, REDUCED), ("s",), ("p",),
        )
    ]
    return tuple(outputs) + (feature_grad,) + tuple(point_outs) + (
        wide_grad, spread_grad,
    ) + tuple(norm_grads)


def solution(mesh):
    columns = P(None, "ch")
    norm = P(None, None, "ch")
    clips = P("batch", None, None, None, "ch")
    kernels = P(None, None, None, "ch")
    return jax.shard_map(
        shards,
        mesh=mesh,
        in_specs=(P("ch", "batch"), P("batch", None, None, None)) + (columns,) * 9 + (kernels,)
        + (norm,) * 6 + (clips,) * 4,
        out_specs=(clips,) * 4 + (P("ch", "batch"),) + (columns,) * 9 + (kernels,) + (norm,) * 6,
        check_vma=False,
    )
```
